32 devices in a mesh: section: 4 (over x, core), dp: 8 (over z, y).
Axes of the slice: x: 2, y: 2, z: 4, core: 2. Of those that a mesh axis runs over, the one named last changes fastest.
Arguments:
- tokens: bfloat16 [32, 2, 512, 768], P(('section', 'dp')), may hold values from -6 to 6
- doc_ids: int32 [32, 2, 512], replicated, may hold values from 0 to 3, never falling along the last dimension, each value on 1 to 256 neighbouring positions
- reset_flags: int32 [32, 2], replicated, may hold values 0 or 1
- memory_init: bfloat16 [10, 768], replicated, may hold values from -6 to 6
- w_proj: bfloat16 [4, 768, 3072], P('section'), may hold values from -0.375 to 0.375
- vectors: float32 [4, 2, 768], P('section'), may hold values from -0.5 to 1.5
- w_down: bfloat16 [6144, 768], P('section'), may hold values from -0.109375 to 0.109375
- cotangent: bfloat16 [32, 2, 512, 768], P(('section', 'dp')), may hold values from -6 to 6
Outputs:
- block_out: bfloat16 [32, 2, 512, 768], P(('section', 'dp'))
- grad_tokens: bfloat16 [32, 2, 512, 768], P(('section', 'dp'))
- grad_proj: float32 [4, 768, 3072], P('section')
- grad_vectors: float32 [4, 2, 768], P('section')
- grad_down: float32 [6144, 768], P('section')
- grad_memory: float32 [10, 768], P(None, 'section')
The draws below stay inside these ranges and needn't reach their ends.
All inputs are finite; a program needn't handle non-finite values.
Results may differ from the reference program's by a relative error of at most 0.025.
Values may be sent and summed in bfloat16 or wider, within the bound.
A program may use at most 320 MiB of HBM per device.

```python
import math
import jax
import jax.numpy as jnp
import numpy as np
from jax import lax

D = 768
HEADS = 12
HEAD_DIM = 64
FF = 3072
MEM = 10
SEG_TOK = 512
SEGS = 2
ITEMS = 32
ROWS = 522
N_SECTION = 4


def draw_w_proj(key, part):
    key = jax.random.fold_in(key, 17)
    uniform_base = jax.random.uniform(key, (N_SECTION, D, 4 * D), jnp.float32, -1.7320508, 1.7320508) * D ** (-0.5)
    even_section = (jnp.arange(N_SECTION) % 2 == 0)[:, None, None]
    output_block = (jnp.arange(4 * D) >= 3 * D)[None, None, :]
    return (uniform_base * jnp.where(even_section & output_block, 6.0, 1.0)).astype(jnp.bfloat16)


def draw_vectors(key, part):
    key = jax.random.fold_in(key, 29)
    noise_rows = jax.random.uniform(key, (N_SECTION, 2, D), jnp.float32, -0.5, 0.5)
    offset = jnp.array([1.0, 0.0], jnp.float32)[None, :, None]
    return noise_rows + offset


def touch_ends(drawn, rng, smallest, top_value):
    longest = drawn.shape.index(max(drawn.shape))
    spots = []
    for shift in (0, 1):
        where = [jax.random.randint(jax.random.fold_in(rng, axis), (), 0, length) for axis, length in enumerate(drawn.shape)]
        where[longest] = (where[longest] + shift) % drawn.shape[longest]
        spots.append(tuple(where))
    return drawn.at[spots[0]].set(smallest).at[spots[1]].set(top_value)


def block_scale(rng, shape, shards, smallest, high):
    level, own = 1.0, jax.random.fold_in(rng, 6)
    for position, parts in shards:
        steps = jnp.exp(jax.random.uniform(jax.random.fold_in(own, position), (parts,), jnp.float32, smallest / len(shards), high / len(shards)))
        level = level * jnp.repeat(steps, shape[position] // parts).reshape([-1 if axis == position else 1 for axis in range(len(shape))])
    return level


def length_profile(number_of, total, most, skew):
    portions = [(1 << 20) // math.isqrt(standing ** skew) + 1 for standing in range(2, number_of + 1)]
    surplus, given = total - most - (number_of - 1), [1] * (number_of - 1)
    while surplus > 0:
        free = [i for i in range(number_of - 1) if given[i] < most]
        mass, budget = sum([portions[i] for i in free]), surplus
        for i in free:
            addition = min(most - given[i], max(1, budget * portions[i] // mass), surplus)
            given[i] = given[i] + addition
            surplus = surplus - addition
    return np.array([most] + given)


def ragged(key, amount, total, bound, lean):
    if amount == 2:
        one = jax.random.randint(key, (), max(1, total - bound), min(bound, total - 1) + 1)
        return jnp.stack([one, total - one])
    lengths = jnp.asarray(length_profile(amount, total, bound, lean), jnp.int32)
    couples = (amount - 1) // 2
    source_of, sink = lengths[1:1 + 2 * couples:2], lengths[2:2 + 2 * couples:2]
    margin = jnp.minimum(source_of - 1, bound - sink)
    passed = jax.random.randint(jax.random.fold_in(key, 1), (couples,), 0, 1 << 20) % (margin + 1)
    lengths = lengths.at[1:1 + 2 * couples:2].set(source_of - passed).at[2:2 + 2 * couples:2].set(sink + passed)
    return lengths[jax.random.permutation(jax.random.fold_in(key, 2), amount)]


def normal_values(own_key, dims, scale, limit, split=(), dtype=jnp.bfloat16):
    drawn = scale * jax.random.normal(own_key, dims, jnp.float32)
    if split:
        drawn = drawn * block_scale(own_key, dims, split, -0.22, 0.18)
    return jnp.clip(drawn, -limit, limit).astype(dtype)


def setup_inputs(seed: int = 0) -> dict:
    key_of = jax.random.split(jax.random.key(seed), 9)
    tokens = normal_values(key_of[0], (ITEMS, SEGS, SEG_TOK, D), 1.0, 6.0, ((0, 32),))
    doc_ids = jax.vmap(lambda own: jnp.searchsorted(jnp.cumsum(ragged(own, 4, SEG_TOK, SEG_TOK // 2, 0)), jnp.arange(SEG_TOK), side="right"))(jax.random.split(key_of[1], ITEMS * SEGS)).reshape((ITEMS, SEGS, SEG_TOK)).astype(jnp.int32)
    reset_flags = touch_ends((jax.random.randint(key_of[2], (ITEMS, SEGS), 0, 3) < 1).astype(jnp.int32), jax.random.fold_in(key_of[2], 1), 0, 1)
    memory_init = normal_values(key_of[3], (MEM, D), 1.0, 6.0)
    w_proj = draw_w_proj(jax.random.fold_in(key_of[8], 71), 0)
    vectors = draw_vectors(jax.random.fold_in(key_of[8], 71), 0)
    w_down = normal_values(key_of[6], (2 * FF, D), FF ** -0.5, 0.109375, ((0, 4),))
    cotangent = normal_values(key_of[7], (ITEMS, SEGS, SEG_TOK, D), 1.0, 6.0, ((0, 32),))
    return dict(tokens=tokens, doc_ids=doc_ids, reset_flags=reset_flags, memory_init=memory_init, w_proj=w_proj, vectors=vectors, w_down=w_down, cotangent=cotangent)


NORM_EPSILON = 1e-06

@jax.custom_vjp
def low(v):
    return lax.optimization_barrier(v.astype(jnp.bfloat16)).astype(jnp.float32)

@jax.custom_vjp
def low_back(v):
    return v

def low_keep(v):
    return (low(v), None)

def low_pass(kept, grad):
    return (grad,)

def back_keep(v):
    return (v, None)

def back_low(kept, grad):
    return (low(grad),)
low.defvjp(low_keep, low_pass)
low_back.defvjp(back_keep, back_low)

def product(left, right):
    return jnp.dot(left, right, precision=lax.Precision.HIGHEST)

def layer_norm(summed, gain, bias_row):
    center = summed - lax.optimization_barrier(jnp.mean(summed, axis=-1, keepdims=True))
    variance = lax.optimization_barrier(jnp.mean(center * center, axis=-1, keepdims=True))
    return center * lax.rsqrt(variance + NORM_EPSILON) * gain + bias_row

def visible(documents):
    extended = jnp.concatenate([jnp.full((MEM,), -1, jnp.int32), documents.astype(jnp.int32)])
    return (extended[:, None] == extended[None, :]) | (extended[:, None] < 0) | (extended[None, :] < 0)

def attention(section_in, weights, vector, allowed):
    hidden_in = low_back(low(section_in))
    projected = product(hidden_in, weights[:, :3 * D])
    queries = low_back(low(projected[:, :D])).reshape(ROWS, HEADS, HEAD_DIM)
    key_rows = low_back(low(projected[:, D:2 * D])).reshape(ROWS, HEADS, HEAD_DIM)
    value_rows = low_back(low(projected[:, 2 * D:])).reshape(ROWS, HEADS, HEAD_DIM)
    scores = jnp.einsum('qhd,khd->hqk', queries, key_rows, precision=lax.Precision.HIGHEST)
    scores = low_back(scores * HEAD_DIM ** (-0.5))
    scores = jnp.where(allowed[None], scores, -1e+30)
    attn_probs = low(jax.nn.softmax(scores, axis=-1))
    mixed_rows = jnp.einsum('hqk,khd->qhd', attn_probs, value_rows, precision=lax.Precision.HIGHEST)
    mixed_rows = low_back(low(mixed_rows.reshape(ROWS, D)))
    branch = low_back(product(mixed_rows, weights[:, 3 * D:]))
    return layer_norm(hidden_in + branch, vector[0], vector[1])

def feed_forward(section_in, first_matrix, second_matrix, vector):
    hidden_in = low_back(low(section_in))
    pre_act = low_back(product(hidden_in, first_matrix))
    activated = low(jax.nn.gelu(pre_act, approximate=False))
    branch = low_back(product(activated, second_matrix))
    return layer_norm(hidden_in + branch, vector[0], vector[1])

def item_forward(token_rows, memory_start, proj, vectors, down, documents, flags):
    memory_rows = memory_start
    results = []
    for segment in range(SEGS):
        if segment == 0:
            entering = memory_start
        else:
            entering = jnp.where(flags[segment] == 1, memory_start, memory_rows)
        hidden = jnp.concatenate([entering, token_rows[segment]], axis=0)
        allowed = visible(documents[segment])
        hidden = attention(hidden, proj[0], vectors[0], allowed)
        hidden = feed_forward(hidden, proj[1], down[:FF], vectors[1])
        hidden = attention(hidden, proj[2], vectors[2], allowed)
        hidden = feed_forward(hidden, proj[3], down[FF:], vectors[3])
        results.append(hidden[MEM:])
        memory_rows = hidden[:MEM]
    return jnp.stack(results)

def reference(tokens, doc_ids, reset_flags, memory_init, w_proj, vectors, w_down, cotangent):
    memory_float = memory_init.astype(jnp.float32)
    proj_float = w_proj.astype(jnp.float32)
    vector_float = vectors.astype(jnp.float32)
    down_float = w_down.astype(jnp.float32)

    def per_item(totals, item_data):
        token_rows, documents, flags, cotangent_rows = item_data

        def forward(rows_float, memory_start, proj, vector_rows, down):
            return item_forward(rows_float, memory_start, proj, vector_rows, down, documents, flags)
        produced, pullback = jax.vjp(forward, token_rows.astype(jnp.float32), memory_float, proj_float, vector_float, down_float)
        gradients = pullback(cotangent_rows.astype(jnp.float32))
        totals = tuple((total + new_grad for total, new_grad in zip(totals, gradients[1:])))
        return (totals, (produced.astype(jnp.bfloat16), gradients[0].astype(jnp.bfloat16)))
    initial = (jnp.zeros_like(memory_float), jnp.zeros_like(proj_float), jnp.zeros_like(vector_float), jnp.zeros_like(down_float))
    totals, outputs = lax.scan(per_item, initial, (tokens, doc_ids, reset_flags, cotangent))
    return (outputs[0], outputs[1], totals[1], totals[2], totals[3], totals[0])
```

```python
import functools

import jax
import jax.numpy as jnp
from jax import lax
from jax.experimental import pallas as pl
from jax.experimental.pallas import tpu as pltpu
from jax.sharding import PartitionSpec as P

HEADS = 12
NORM_EPSILON = 1e-06
NEGATIVE = -1e30
BF16 = jnp.bfloat16
F32 = jnp.float32
VMEM_BYTES = 56 * 2**20
GROUP = 4
FF_BLOCK = 1024
SLOTS = 5
SPARE = 4

SWAP_CORE = [(0, 1), (1, 0), (2, 3), (3, 2)]
TO_SECOND = [(0, 2), (1, 3)]
TO_FIRST = [(2, 0), (3, 1)]


def mm(left, right, ca=1, cb=0):
    return lax.dot_general(
        left, right, (((ca,), (cb,)), ((), ())), preferred_element_type=F32
    )


def shape_of(shape, dtype=BF16):
    return jax.ShapeDtypeStruct(shape, dtype)


def whole(shape):
    return pl.BlockSpec(shape, lambda g, info: (0,) * len(shape))


def in_slot(rows, cols, moving=True):
    if moving:
        return pl.BlockSpec((None, rows, cols), lambda g, info: (info[0], 0, g))
    return pl.BlockSpec((None, rows, cols), lambda g, info: (info[0], 0, 0))


def staged_call(kernel, steps, info, inputs, in_specs, outs, scratch, stacks, name):
    stacked = [i for i, out in enumerate(outs) if out[3]]
    count = len(inputs)
    extra, aliases = [], {}
    if stacks is not None:
        for position, (index, stack) in enumerate(zip(stacked, stacks)):
            extra.append(stack)
            aliases[1 + count + position] = index

    def wrapped(info_ref, *refs):
        ins = refs[:count]
        rest = refs[count + len(extra):]
        kernel(info_ref, *ins, *rest)

    result = pl.pallas_call(
        wrapped,
        grid_spec=pltpu.PrefetchScalarGridSpec(
            num_scalar_prefetch=1,
            grid=(steps,),
            in_specs=list(in_specs) + [pl.BlockSpec(memory_space=pl.ANY)] * len(extra),
            out_specs=[out[2] for out in outs],
            scratch_shapes=scratch,
        ),
        out_shape=[shape_of(out[0], out[1]) for out in outs],
        input_output_aliases=aliases,
        compiler_params=pltpu.CompilerParams(vmem_limit_bytes=VMEM_BYTES),
        name=name,
    )(info, *inputs, *extra)
    kept = [result[i] for i in stacked]
    loose = [result[i] for i in range(len(outs)) if i not in stacked]
    return kept, loose


def normalise(summed):
    center = summed - jnp.mean(summed, axis=-1, keepdims=True)
    variance = jnp.mean(center * center, axis=-1, keepdims=True)
    inverse = lax.rsqrt(variance + NORM_EPSILON)
    return center * inverse, inverse


def finish_norm(summed, vec_ref, n_ref, r_ref, y_refs):
    normed, inverse = normalise(summed)
    n_ref[...] = normed.astype(BF16)
    r_ref[...] = jnp.broadcast_to(inverse, r_ref.shape)
    y = (normed * vec_ref[0:1, :] + vec_ref[1:2, :]).astype(BF16)
    for ref in y_refs:
        ref[...] = y


def attn_fwd_kernel(info_ref, x_ref, wq_ref, wk_ref, wv_ref, wo_ref, vec_ref, drow_ref, dcol_ref,
                    q_ref, k_ref, v_ref, p_ref, o_ref, n_ref, r_ref, y_ref, keep_ref,
                    bias_ref, acc_ref, *, head, group):
    step = pl.program_id(0)
    last = pl.num_programs(0) - 1

    @pl.when(info_ref[1] == 1)
    def _():
        @pl.when(step == 0)
        def _():
            rows = dcol_ref[:, 0:1]
            cols = drow_ref[...]
            allowed = ((rows == cols) | (rows < 0) | (cols == -1)) & (cols > -2)
            bias_ref[...] = jnp.where(allowed, 0.0, NEGATIVE)
            keep_ref[...] = x_ref[...]

        x = x_ref[...]
        scale = head ** (-0.5)
        q_ref[...] = mm(x, wq_ref[...]).astype(BF16)
        k_ref[...] = mm(x, wk_ref[...]).astype(BF16)
        v_ref[...] = mm(x, wv_ref[...]).astype(BF16)

        def score(h):
            cut = pl.ds(h * head, head)
            return mm(q_ref[:, cut] * scale, k_ref[:, cut], 1, 1) + bias_ref[...]

        s = score(0)
        for h in range(group):
            cut = pl.ds(h * head, head)
            following = score(h + 1) if h + 1 < group else None
            m = jnp.max(s, axis=-1, keepdims=True)
            e = jnp.exp(s - m)
            l = jnp.sum(e, axis=-1, keepdims=True)
            p = (e * (1.0 / l)).astype(BF16)
            p_ref[h] = p
            o_ref[:, cut] = mm(p, v_ref[:, cut]).astype(BF16)
            s = following
        part = mm(o_ref[...], wo_ref[...])

        @pl.when(step == 0)
        def _():
            acc_ref[...] = x.astype(F32) + part

        @pl.when(step > 0)
        def _():
            acc_ref[...] += part

        @pl.when(step == last)
        def _():
            finish_norm(acc_ref[...], vec_ref, n_ref, r_ref, [y_ref])


def attn_forward(info, x, weights, vec, drow, dcol, stacks):
    rows, width = x.shape
    head = width // HEADS
    cols = GROUP * head
    steps = HEADS // GROUP

    def wcols(part):
        return pl.BlockSpec((None, width, cols), lambda g, info: (0, 0, part * steps + g))

    stack = (SLOTS, rows, width)
    return staged_call(
        functools.partial(attn_fwd_kernel, head=head, group=GROUP), steps, info,
        [x, weights, weights, weights, weights, vec, drow, dcol],
        [whole((rows, width)), wcols(0), wcols(1), wcols(2),
         pl.BlockSpec((None, cols, width), lambda g, info: (0, g, 3)),
         whole((2, width)), whole((1, rows)), whole((rows, 128))],
        [(stack, BF16, in_slot(rows, cols), True)] * 3
        + [((SLOTS, HEADS, rows, rows), BF16,
            pl.BlockSpec((None, GROUP, rows, rows), lambda g, info: (info[0], g, 0, 0)), True),
           (stack, BF16, in_slot(rows, cols), True),
           (stack, BF16, in_slot(rows, width, False), True),
           ((SLOTS, rows, 128), F32, in_slot(rows, 128, False), True),
           (stack, BF16, in_slot(rows, width, False), True),
           (stack, BF16, in_slot(rows, width, False), True)],
        [pltpu.VMEM((rows, rows), F32), pltpu.VMEM((rows, width), F32)], stacks, "attn_fwd")


def gelu_parts(a):
    half = 0.5 * (1.0 + lax.erf(a * 0.7071067811865476))
    return a * half, half + a * jnp.exp(-0.5 * a * a) * 0.3989422804014327


def ff_fwd_kernel(info_ref, x_ref, w1_ref, w2_ref, vec_ref, h_ref, g_ref, n_ref, r_ref, y_ref, acc_ref):
    step = pl.program_id(0)
    last = pl.num_programs(0) - 1

    @pl.when(info_ref[1] == 1)
    def _():
        x = x_ref[...]
        act, slope = gelu_parts(mm(x, w1_ref[...]))
        h_ref[...] = act.astype(BF16)
        g_ref[...] = slope.astype(BF16)
        part = mm(h_ref[...], w2_ref[...])

        @pl.when(step == 0)
        def _():
            acc_ref[...] = x.astype(F32) + part

        @pl.when(step > 0)
        def _():
            acc_ref[...] += part

        @pl.when(step == last)
        def _():
            finish_norm(acc_ref[...], vec_ref, n_ref, r_ref, [y_ref])


def ff_forward(info, x, w1, w2, vec, stacks):
    _, rows, width = x.shape
    hidden = w1.shape[2]
    return staged_call(
        ff_fwd_kernel, hidden // FF_BLOCK, info, [x, w1, w2, vec],
        [in_slot(rows, width, False), pl.BlockSpec((None, width, FF_BLOCK), lambda g, info: (1, 0, g)),
         pl.BlockSpec((FF_BLOCK, width), lambda g, info: (g, 0)), whole((2, width))],
        [((SLOTS, rows, hidden), BF16, in_slot(rows, FF_BLOCK), True)] * 2
        + [((SLOTS, rows, width), BF16, in_slot(rows, width, False), True),
           ((SLOTS, rows, 128), F32, in_slot(rows, 128, False), True),
           ((rows, width), BF16, whole((rows, width)), False)],
        [pltpu.VMEM((rows, width), F32)], stacks, "ff_fwd")


def norm_back(g_ref, n_ref, r_ref, vec_ref, gv_ref):
    g = g_ref[...].astype(F32)
    n = n_ref[...].astype(F32)
    u = g * vec_ref[0:1, :]
    dz = r_ref[:, 0:1] * (u - jnp.mean(u, axis=-1, keepdims=True)
                          - n * jnp.mean(u * n, axis=-1, keepdims=True))
    gv_ref[0:1, :] = jnp.sum(g * n, axis=0, keepdims=True)
    gv_ref[1:2, :] = jnp.sum(g, axis=0, keepdims=True)
    return dz


def ff_bwd_kernel(info_ref, g_ref, n_ref, r_ref, vec_ref, slope_ref, w1_ref, w2_ref,
                  df_ref, da_ref, gv_ref, dx_ref, acc_ref):
    step = pl.program_id(0)
    last = pl.num_programs(0) - 1

    @pl.when(info_ref[1] == 1)
    def _():
        @pl.when(step == 0)
        def _():
            dz = norm_back(g_ref, n_ref, r_ref, vec_ref, gv_ref)
            df_ref[...] = dz.astype(BF16)
            acc_ref[...] = dz

        dh = mm(df_ref[...], w2_ref[...], 1, 1)
        da_ref[...] = (dh * slope_ref[...].astype(F32)).astype(BF16)
        acc_ref[...] += mm(da_ref[...], w1_ref[...], 1, 1)

        @pl.when(step == last)
        def _():
            dx_ref[...] = acc_ref[...].astype(BF16)


def ff_backward(info, g, n, r, vec, slope, w1, w2, stacks):
    rows, width = g.shape
    hidden = w1.shape[2]
    return staged_call(
        ff_bwd_kernel, hidden // FF_BLOCK, info, [g, n, r, vec, slope, w1, w2],
        [whole((rows, width)), in_slot(rows, width, False), in_slot(rows, 128, False), whole((2, width)),
         in_slot(rows, FF_BLOCK), pl.BlockSpec((None, width, FF_BLOCK), lambda g, info: (1, 0, g)),
         pl.BlockSpec((FF_BLOCK, width), lambda g, info: (g, 0))],
        [((SLOTS, rows, width), BF16, in_slot(rows, width, False), True),
         ((SLOTS, rows, hidden), BF16, in_slot(rows, FF_BLOCK), True),
         ((SLOTS, 2, width), F32, in_slot(2, width, False), True),
         ((rows, width), BF16, whole((rows, width)), False)],
        [pltpu.VMEM((rows, width), F32)], stacks, "ff_bwd")


def attn_bwd_kernel(info_ref, g_ref, n_ref, r_ref, vec_ref, q_ref, k_ref, v_ref, p_ref, o_ref,
                    wq_ref, wk_ref, wv_ref, wo_ref,
                    db_ref, dq_ref, dk_ref, dv_ref, gv_ref, dx_ref, acc_ref, do_ref, *, head, group):
    step = pl.program_id(0)
    last = pl.num_programs(0) - 1

    @pl.when(info_ref[1] == 1)
    def _():
        @pl.when(step == 0)
        def _():
            dz = norm_back(g_ref, n_ref, r_ref, vec_ref, gv_ref)
            db_ref[...] = dz.astype(BF16)
            acc_ref[...] = dz

        scale = head ** (-0.5)
        do_ref[...] = mm(db_ref[...], wo_ref[...], 1, 1).astype(BF16)

        def grad_probs(h):
            cut = pl.ds(h * head, head)
            return mm(do_ref[:, cut], v_ref[:, cut], 1, 1)

        dp = grad_probs(0)
        for h in range(group):
            cut = pl.ds(h * head, head)
            following = grad_probs(h + 1) if h + 1 < group else None
            do = do_ref[:, cut]
            p = p_ref[h]
            mean = jnp.sum(do.astype(F32) * o_ref[:, cut].astype(F32), axis=-1, keepdims=True)
            ds = (p.astype(F32) * (dp - mean)).astype(BF16)
            dv_ref[:, cut] = mm(p, do, 0, 0).astype(BF16)
            dq_ref[:, cut] = (mm(ds, k_ref[:, cut]) * scale).astype(BF16)
            dk_ref[:, cut] = (mm(ds, q_ref[:, cut], 0, 0) * scale).astype(BF16)
            dp = following
        acc_ref[...] += (mm(dq_ref[...], wq_ref[...], 1, 1) + mm(dk_ref[...], wk_ref[...], 1, 1)
                         + mm(dv_ref[...], wv_ref[...], 1, 1))

        @pl.when(step == last)
        def _():
            dx_ref[...] = acc_ref[...].astype(BF16)


def attn_backward(info, g, n, r, vec, q, k, v, p, o, weights, stacks):
    rows, width = g.shape
    head = width // HEADS
    cols = GROUP * head
    steps = HEADS // GROUP

    def wcols(part):
        return pl.BlockSpec((None, width, cols), lambda g, info: (0, 0, part * steps + g))

    stack = (SLOTS, rows, width)
    return staged_call(
        functools.partial(attn_bwd_kernel, head=head, group=GROUP), steps, info,
        [g, n, r, vec, q, k, v, p, o, weights, weights, weights, weights],
        [whole((rows, width)), in_slot(rows, width, False), in_slot(rows, 128, False), whole((2, width)),
         in_slot(rows, cols), in_slot(rows, cols), in_slot(rows, cols),
         pl.BlockSpec((None, GROUP, rows, rows), lambda g, info: (info[0], g, 0, 0)), in_slot(rows, cols),
         wcols(0), wcols(1), wcols(2), pl.BlockSpec((None, cols, width), lambda g, info: (0, g, 3))],
        [(stack, BF16, in_slot(rows, width, False), True)]
        + [(stack, BF16, in_slot(rows, cols), True)] * 3
        + [((SLOTS, 2, width), F32, in_slot(2, width, False), True),
           ((rows, width), BF16, whole((rows, width)), False)],
        [pltpu.VMEM((rows, width), F32), pltpu.VMEM((rows, cols), BF16)], stacks, "attn_bwd")


def grad_kernel(left_ref, right_ref, out_ref):
    left = left_ref[...].reshape(-1, left_ref.shape[2])
    right = right_ref[...].reshape(-1, right_ref.shape[2])
    out_ref[...] = mm(left, right, 0, 0).astype(out_ref.dtype)


def weight_grad(left, right, lblock, rblock):
    _, rows, wide = left.shape
    cols = right.shape[2]
    return pl.pallas_call(
        grad_kernel,
        grid=(wide // lblock, cols // rblock),
        in_specs=[pl.BlockSpec((SPARE, rows, lblock), lambda i, j: (0, 0, i)),
                  pl.BlockSpec((SPARE, rows, rblock), lambda i, j: (0, 0, j))],
        out_specs=pl.BlockSpec((lblock, rblock), lambda i, j: (i, j)),
        out_shape=shape_of((wide, cols)),
        compiler_params=pltpu.CompilerParams(vmem_limit_bytes=VMEM_BYTES),
        name="weight_grad",
    )(left, right)


def body(tokens, doc_ids, reset_flags, memory_init, w_proj, vectors, w_down, cotangent):
    data_count = lax.axis_size("dp")
    section = lax.axis_index("section")
    data = lax.axis_index("dp")
    stage = section // 2
    core = section % 2
    first = stage == 0
    _, segments, seg_tokens, width = tokens.shape
    memory_count = memory_init.shape[0]
    pad = -(memory_count + seg_tokens) % 16
    rows = seg_tokens + memory_count + pad
    pairs = [[0, 1], [2, 3]]

    proj = lax.all_gather(w_proj[0], "section", axis=0, axis_index_groups=pairs)
    down = lax.all_gather(w_down, "section", axis=0, tiled=True, axis_index_groups=pairs)
    vecs = lax.all_gather(vectors[0], "section", axis=0, axis_index_groups=pairs)

    def send(block, route):
        return lax.ppermute(block, "section", route)

    other_tokens = [send(tokens[0, k], TO_FIRST) for k in range(segments)]
    other_cot = [send(cotangent[0, k], TO_SECOND) for k in range(segments)]
    item_a = core * data_count + data
    item_b = (core + 2) * data_count + data
    micros = [(item, k) for k in range(segments) for item in (0, 1)]
    items = (item_a, item_b)
    micro_docs = []
    for item, k in micros:
        docs = lax.dynamic_index_in_dim(doc_ids, items[item], 0, keepdims=False)[k]
        micro_docs.append(jnp.concatenate(
            [docs, jnp.full((memory_count,), -1, jnp.int32), jnp.full((pad,), -2, jnp.int32)]))
    flags = [lax.dynamic_index_in_dim(reset_flags, items[i], 0, keepdims=False) for i in (0, 1)]
    pad_rows = jnp.zeros((pad, width), BF16)

    def fresh(item, k):
        return jnp.bool_(True) if k == 0 else flags[item][k] == 1

    def pick(choice, yes, no):
        return jnp.where(choice, yes, no)

    count = len(micros)
    attn_stacks = ff_stacks = None
    carried = jnp.zeros((rows, width), BF16)
    memory_back = {}
    outs = {}
    for tick in range(count + 1):
        here = min(tick, count - 1)
        item, k = micros[here]
        valid = pick(first, tick < count, tick > 0).astype(jnp.int32)
        slot = pick(first, tick, tick - 1)
        slot = pick(valid == 1, slot, SPARE)
        info = jnp.stack([slot, valid]).astype(jnp.int32)
        if k == 0:
            entering = memory_init
        else:
            entering = pick(fresh(item, k), memory_init, memory_back[(item, k - 1)][:memory_count])
        rows_in = tokens[0, k] if item == 0 else other_tokens[k]
        start = jnp.concatenate([rows_in, entering, pad_rows], axis=0)
        x = pick(first, start, carried)
        docs = pick(first, micro_docs[here], micro_docs[max(tick - 1, 0)])
        drow = docs[None, :]
        dcol = jnp.broadcast_to(docs[:, None], (rows, 128))
        attn_stacks, _ = attn_forward(info, x, proj, vecs[0], drow, dcol, attn_stacks)
        ff_stacks, (y,) = ff_forward(info, attn_stacks[7], proj, down, vecs[1], ff_stacks)
        if tick < count:
            carried = send(y, TO_SECOND)
        if tick > 0:
            done = micros[tick - 1]
            if done[1] + 1 < segments:
                memory_back[done] = send(y[seg_tokens:], TO_FIRST)
            outs[done] = y[:seg_tokens]
    q, k_rows, v, p, o, n1, r1, y1, x_in = attn_stacks
    h, slope, n2, r2 = ff_stacks

    order = [m for k in reversed(range(segments)) for m in range(count) if micros[m][1] == k]
    ffb_stacks = ab_stacks = None
    returning = jnp.zeros((rows, width), BF16)
    memory_forward = {}
    grads = {}
    grad_memory = jnp.zeros((memory_count, width), F32)
    for tick in range(count + 1):
        mine = order[min(tick, count - 1)]
        before = order[max(tick - 1, 0)]
        item, k = micros[mine]
        valid = pick(first, tick > 0, tick < count).astype(jnp.int32)
        slot = pick(valid == 1, pick(first, before, mine), SPARE)
        info = jnp.stack([slot, valid]).astype(jnp.int32)
        if k + 1 < segments:
            memory_grad = memory_forward[(item, k + 1)]
        else:
            memory_grad = jnp.zeros((rows - seg_tokens, width), BF16)
        rows_in = cotangent[0, k] if item == 1 else other_cot[k]
        start = jnp.concatenate([rows_in, memory_grad], axis=0)
        g = pick(first, returning, start)
        ffb_stacks, (dy,) = ff_backward(info, g, n2, r2, vecs[1], slope, proj, down, ffb_stacks)
        ab_stacks, (dx,) = attn_backward(info, dy, n1, r1, vecs[0], q, k_rows, v, p, o, proj, ab_stacks)
        if tick < count:
            returning = send(dx, TO_FIRST)
        if tick > 0:
            done = micros[before]
            grads[done] = dx[:seg_tokens]
            is_fresh = fresh(*done)
            memory_rows = dx[seg_tokens:]
            if done[1] > 0:
                memory_forward[done] = send(pick(is_fresh, jnp.zeros_like(memory_rows), memory_rows), TO_SECOND)
            grad_memory = grad_memory + pick(
                first & is_fresh, memory_rows[:memory_count].astype(F32), 0.0)
    df, da, gv2 = ffb_stacks
    db, dq, dk, dv, gv1 = ab_stacks

    vec_pair = jnp.stack([gv1[:SPARE].sum(axis=0), gv2[:SPARE].sum(axis=0)])
    small = jnp.zeros((4, 2, width), F32)
    small = lax.dynamic_update_slice(small, vec_pair, (stage * 2, 0, 0))
    small = jnp.concatenate([small.reshape(8, width), grad_memory], axis=0)
    small = lax.psum(small, ("section", "dp"))
    total_vec = lax.dynamic_slice(small[:8].reshape(4, 2, width), (section, 0, 0), (1, 2, width))
    share = width // 4
    memory_total = lax.dynamic_slice(small[8:], (0, section * share), (memory_count, share))

    grad_ff1 = weight_grad(y1, da, width, 512)
    grad_ff2 = weight_grad(h, df, 512, width)
    grad_attn = jnp.concatenate(
        [weight_grad(x_in, dq, width, 384), weight_grad(x_in, dk, width, 384),
         weight_grad(x_in, dv, width, 384), weight_grad(o, db, width, 384)], axis=1)
    low = core == 0
    half = w_down.shape[0]
    got_proj = send(pick(low, grad_ff1, grad_attn), SWAP_CORE)
    got_down = send(pick(low, grad_ff2[half:], grad_ff2[:half]), SWAP_CORE)
    my_proj = (pick(low, grad_attn, grad_ff1).astype(F32) + got_proj.astype(F32)).astype(BF16)
    my_down = (pick(low, grad_ff2[:half], grad_ff2[half:]).astype(F32) + got_down.astype(F32)).astype(BF16)
    total_proj = lax.psum(my_proj, "dp").astype(F32)
    total_down = lax.psum(my_down, "dp").astype(F32)

    def collect(done, table, route, keep_first):
        item_own, item_other = (0, 1) if keep_first else (1, 0)
        blocks = []
        for k in range(segments):
            if keep_first:
                got = send(table[(1, k)], route)
                blocks.append(pick(first, table[(0, k)], got))
            else:
                got = send(table[(0, k)], route)
                blocks.append(pick(first, got, table[(1, k)]))
        return jnp.stack(blocks)[None]

    block_rows = collect(None, outs, TO_FIRST, False)
    input_rows = collect(None, grads, TO_SECOND, True)
    return (block_rows, input_rows, total_proj[None], total_vec, total_down, memory_total)


def solution(mesh):
    items = P(("section", "dp"), None, None, None)
    return jax.shard_map(
        body,
        mesh=mesh,
        in_specs=(items, P(), P(), P(), P("section", None, None), P("section", None, None),
                  P("section", None), items),
        out_specs=(items, items, P("section", None, None), P("section", None, None),
                   P("section", None), P(None, "section")),
        check_vma=False,
    )
```

```python
import functools

import jax
import jax.numpy as jnp
from jax import lax
from jax.experimental import pallas as pl
from jax.experimental.pallas import tpu as pltpu
from jax.sharding import PartitionSpec as P

HEADS = 12
NORM_EPSILON = 1e-06
NEGATIVE = -1e30
BF16 = jnp.bfloat16
F32 = jnp.float32
VMEM_BYTES = 56 * 2**20
GROUP = 4
FF_BLOCK = 1024
SLOTS = 5
SPARE = 4

TO_SECOND = [(0, 2), (1, 3)]
TO_FIRST = [(2, 0), (3, 1)]


def mm(left, right, ca=1, cb=0):
    return lax.dot_general(
        left, right, (((ca,), (cb,)), ((), ())), preferred_element_type=F32
    )


def shape_of(shape, dtype=BF16):
    return jax.ShapeDtypeStruct(shape, dtype)


def whole(shape):
    return pl.BlockSpec(shape, lambda g, info: (0,) * len(shape))


def in_slot(rows, cols, moving=True):
    if moving:
        return pl.BlockSpec((None, rows, cols), lambda g, info: (info[0], 0, g))
    return pl.BlockSpec((None, rows, cols), lambda g, info: (info[0], 0, 0))


def staged_call(kernel, steps, info, inputs, in_specs, outs, scratch, stacks, name):
    stacked = [i for i, out in enumerate(outs) if out[3]]
    count = len(inputs)
    extra, aliases = [], {}
    if stacks is not None:
        for position, (index, stack) in enumerate(zip(stacked, stacks)):
            extra.append(stack)
            aliases[1 + count + position] = index

    def wrapped(info_ref, *refs):
        ins = refs[:count]
        rest = refs[count + len(extra):]
        kernel(info_ref, *ins, *rest)

    result = pl.pallas_call(
        wrapped,
        grid_spec=pltpu.PrefetchScalarGridSpec(
            num_scalar_prefetch=1,
            grid=(steps,),
            in_specs=list(in_specs) + [pl.BlockSpec(memory_space=pl.ANY)] * len(extra),
            out_specs=[out[2] for out in outs],
            scratch_shapes=scratch,
        ),
        out_shape=[shape_of(out[0], out[1]) for out in outs],
        input_output_aliases=aliases,
        compiler_params=pltpu.CompilerParams(vmem_limit_bytes=VMEM_BYTES),
        name=name,
    )(info, *inputs, *extra)
    kept = [result[i] for i in stacked]
    loose = [result[i] for i in range(len(outs)) if i not in stacked]
    return kept, loose


def normalise(summed):
    center = summed - jnp.mean(summed, axis=-1, keepdims=True)
    variance = jnp.mean(center * center, axis=-1, keepdims=True)
    inverse = lax.rsqrt(variance + NORM_EPSILON)
    return center * inverse, inverse


def finish_norm(summed, vec_ref, n_ref, r_ref, y_refs):
    normed, inverse = normalise(summed)
    n_ref[...] = normed.astype(BF16)
    r_ref[...] = jnp.broadcast_to(inverse, r_ref.shape)
    y = (normed * vec_ref[0:1, :] + vec_ref[1:2, :]).astype(BF16)
    for ref in y_refs:
        ref[...] = y


def attn_fwd_kernel(info_ref, x_ref, wq_ref, wk_ref, wv_ref, wo_ref, vec_ref, drow_ref, dcol_ref,
                    q_ref, k_ref, v_ref, p_ref, o_ref, n_ref, r_ref, y_ref, keep_ref,
                    bias_ref, acc_ref, *, head, group):
    step = pl.program_id(0)
    last = pl.num_programs(0) - 1

    @pl.when(info_ref[1] == 1)
    def _():
        @pl.when(step == 0)
        def _():
            rows = dcol_ref[:, 0:1]
            cols = drow_ref[...]
            allowed = ((rows == cols) | (rows < 0) | (cols == -1)) & (cols > -2)
            bias_ref[...] = jnp.where(allowed, 0.0, NEGATIVE)
            keep_ref[...] = x_ref[...]

        x = x_ref[...]
        scale = head ** (-0.5)
        q_ref[...] = mm(x, wq_ref[...]).astype(BF16)
        k_ref[...] = mm(x, wk_ref[...]).astype(BF16)
        v_ref[...] = mm(x, wv_ref[...]).astype(BF16)

        def score(h):
            cut = pl.ds(h * head, head)
            return mm(q_ref[:, cut] * scale, k_ref[:, cut], 1, 1) + bias_ref[...]

        s = score(0)
        for h in range(group):
            cut = pl.ds(h * head, head)
            following = score(h + 1) if h + 1 < group else None
            m = jnp.max(s, axis=-1, keepdims=True)
            e = jnp.exp(s - m)
            l = jnp.sum(e, axis=-1, keepdims=True)
            p = (e * (1.0 / l)).astype(BF16)
            p_ref[h] = p
            o_ref[:, cut] = mm(p, v_ref[:, cut]).astype(BF16)
            s = following
        part = mm(o_ref[...], wo_ref[...])

        @pl.when(step == 0)
        def _():
            acc_ref[...] = x.astype(F32) + part

        @pl.when(step > 0)
        def _():
            acc_ref[...] += part

        @pl.when(step == last)
        def _():
            finish_norm(acc_ref[...], vec_ref, n_ref, r_ref, [y_ref])


def attn_forward(info, x, weights, vec, drow, dcol, stacks):
    rows, width = x.shape
    head = width // HEADS
    cols = GROUP * head
    steps = HEADS // GROUP

    def wcols(part):
        return pl.BlockSpec((None, width, cols), lambda g, info: (0, 0, part * steps + g))

    stack = (SLOTS, rows, width)
    return staged_call(
        functools.partial(attn_fwd_kernel, head=head, group=GROUP), steps, info,
        [x, weights, weights, weights, weights, vec, drow, dcol],
        [whole((rows, width)), wcols(0), wcols(1), wcols(2),
         pl.BlockSpec((None, cols, width), lambda g, info: (0, g, 3)),
         whole((2, width)), whole((1, rows)), whole((rows, 128))],
        [(stack, BF16, in_slot(rows, cols), True)] * 3
        + [((SLOTS, HEADS, rows, rows), BF16,
            pl.BlockSpec((None, GROUP, rows, rows), lambda g, info: (info[0], g, 0, 0)), True),
           (stack, BF16, in_slot(rows, cols), True),
           (stack, BF16, in_slot(rows, width, False), True),
           ((SLOTS, rows, 128), F32, in_slot(rows, 128, False), True),
           (stack, BF16, in_slot(rows, width, False), True),
           (stack, BF16, in_slot(rows, width, False), True)],
        [pltpu.VMEM((rows, rows), F32), pltpu.VMEM((rows, width), F32)], stacks, "attn_fwd")


def gelu_parts(a):
    half = 0.5 * (1.0 + lax.erf(a * 0.7071067811865476))
    return a * half, half + a * jnp.exp(-0.5 * a * a) * 0.3989422804014327


def ff_fwd_kernel(info_ref, x_ref, w1_ref, w2_ref, vec_ref, h_ref, g_ref, n_ref, r_ref, y_ref, acc_ref):
    step = pl.program_id(0)
    last = pl.num_programs(0) - 1

    @pl.when(info_ref[1] == 1)
    def _():
        x = x_ref[...]
        act, slope = gelu_parts(mm(x, w1_ref[...]))
        h_ref[...] = act.astype(BF16)
        g_ref[...] = slope.astype(BF16)
        part = mm(h_ref[...], w2_ref[...])

        @pl.when(step == 0)
        def _():
            acc_ref[...] = x.astype(F32) + part

        @pl.when(step > 0)
        def _():
            acc_ref[...] += part

        @pl.when(step == last)
        def _():
            finish_norm(acc_ref[...], vec_ref, n_ref, r_ref, [y_ref])


def ff_forward(info, x, w1, w2, vec, stacks):
    _, rows, width = x.shape
    hidden = w1.shape[2]
    return staged_call(
        ff_fwd_kernel, hidden // FF_BLOCK, info, [x, w1, w2, vec],
        [in_slot(rows, width, False), pl.BlockSpec((None, width, FF_BLOCK), lambda g, info: (1, 0, g)),
         pl.BlockSpec((FF_BLOCK, width), lambda g, info: (g, 0)), whole((2, width))],
        [((SLOTS, rows, hidden), BF16, in_slot(rows, FF_BLOCK), True)] * 2
        + [((SLOTS, rows, width), BF16, in_slot(rows, width, False), True),
           ((SLOTS, rows, 128), F32, in_slot(rows, 128, False), True),
           ((rows, width), BF16, whole((rows, width)), False)],
        [pltpu.VMEM((rows, width), F32)], stacks, "ff_fwd")


def norm_back(g_ref, n_ref, r_ref, vec_ref, gv_ref):
    g = g_ref[...].astype(F32)
    n = n_ref[...].astype(F32)
    u = g * vec_ref[0:1, :]
    dz = r_ref[:, 0:1] * (u - jnp.mean(u, axis=-1, keepdims=True)
                          - n * jnp.mean(u * n, axis=-1, keepdims=True))
    gv_ref[0:1, :] = jnp.sum(g * n, axis=0, keepdims=True)
    gv_ref[1:2, :] = jnp.sum(g, axis=0, keepdims=True)
    return dz


def ff_bwd_kernel(info_ref, g_ref, n_ref, r_ref, vec_ref, slope_ref, w1_ref, w2_ref,
                  df_ref, da_ref, gv_ref, dx_ref, acc_ref):
    step = pl.program_id(0)
    last = pl.num_programs(0) - 1

    @pl.when(info_ref[1] == 1)
    def _():
        @pl.when(step == 0)
        def _():
            dz = norm_back(g_ref, n_ref, r_ref, vec_ref, gv_ref)
            df_ref[...] = dz.astype(BF16)
            acc_ref[...] = dz

        dh = mm(df_ref[...], w2_ref[...], 1, 1)
        da_ref[...] = (dh * slope_ref[...].astype(F32)).astype(BF16)
        acc_ref[...] += mm(da_ref[...], w1_ref[...], 1, 1)

        @pl.when(step == last)
        def _():
            dx_ref[...] = acc_ref[...].astype(BF16)


def ff_backward(info, g, n, r, vec, slope, w1, w2, stacks):
    rows, width = g.shape
    hidden = w1.shape[2]
    return staged_call(
        ff_bwd_kernel, hidden // FF_BLOCK, info, [g, n, r, vec, slope, w1, w2],
        [whole((rows, width)), in_slot(rows, width, False), in_slot(rows, 128, False), whole((2, width)),
         in_slot(rows, FF_BLOCK), pl.BlockSpec((None, width, FF_BLOCK), lambda g, info: (1, 0, g)),
         pl.BlockSpec((FF_BLOCK, width), lambda g, info: (g, 0))],
        [((SLOTS, rows, width), BF16, in_slot(rows, width, False), True),
         ((SLOTS, rows, hidden), BF16, in_slot(rows, FF_BLOCK), True),
         ((SLOTS, 2, width), F32, in_slot(2, width, False), True),
         ((rows, width), BF16, whole((rows, width)), False)],
        [pltpu.VMEM((rows, width), F32)], stacks, "ff_bwd")


def attn_bwd_kernel(info_ref, g_ref, n_ref, r_ref, vec_ref, q_ref, k_ref, v_ref, p_ref, o_ref,
                    wq_ref, wk_ref, wv_ref, wo_ref,
                    db_ref, dq_ref, dk_ref, dv_ref, gv_ref, dx_ref, acc_ref, do_ref, *, head, group):
    step = pl.program_id(0)
    last = pl.num_programs(0) - 1

    @pl.when(info_ref[1] == 1)
    def _():
        @pl.when(step == 0)
        def _():
            dz = norm_back(g_ref, n_ref, r_ref, vec_ref, gv_ref)
            db_ref[...] = dz.astype(BF16)
            acc_ref[...] = dz

        scale = head ** (-0.5)
        do_ref[...] = mm(db_ref[...], wo_ref[...], 1, 1).astype(BF16)

        def grad_probs(h):
            cut = pl.ds(h * head, head)
            return mm(do_ref[:, cut], v_ref[:, cut], 1, 1)

        dp = grad_probs(0)
        for h in range(group):
            cut = pl.ds(h * head, head)
            following = grad_probs(h + 1) if h + 1 < group else None
            do = do_ref[:, cut]
            p = p_ref[h]
            mean = jnp.sum(do.astype(F32) * o_ref[:, cut].astype(F32), axis=-1, keepdims=True)
            ds = (p.astype(F32) * (dp - mean)).astype(BF16)
            dv_ref[:, cut] = mm(p, do, 0, 0).astype(BF16)
            dq_ref[:, cut] = (mm(ds, k_ref[:, cut]) * scale).astype(BF16)
            dk_ref[:, cut] = (mm(ds, q_ref[:, cut], 0, 0) * scale).astype(BF16)
            dp = following
        acc_ref[...] += (mm(dq_ref[...], wq_ref[...], 1, 1) + mm(dk_ref[...], wk_ref[...], 1, 1)
                         + mm(dv_ref[...], wv_ref[...], 1, 1))

        @pl.when(step == last)
        def _():
            dx_ref[...] = acc_ref[...].astype(BF16)


def attn_backward(info, g, n, r, vec, q, k, v, p, o, weights, stacks):
    rows, width = g.shape
    head = width // HEADS
    cols = GROUP * head
    steps = HEADS // GROUP

    def wcols(part):
        return pl.BlockSpec((None, width, cols), lambda g, info: (0, 0, part * steps + g))

    stack = (SLOTS, rows, width)
    return staged_call(
        functools.partial(attn_bwd_kernel, head=head, group=GROUP), steps, info,
        [g, n, r, vec, q, k, v, p, o, weights, weights, weights, weights],
        [whole((rows, width)), in_slot(rows, width, False), in_slot(rows, 128, False), whole((2, width)),
         in_slot(rows, cols), in_slot(rows, cols), in_slot(rows, cols),
         pl.BlockSpec((None, GROUP, rows, rows), lambda g, info: (info[0], g, 0, 0)), in_slot(rows, cols),
         wcols(0), wcols(1), wcols(2), pl.BlockSpec((None, cols, width), lambda g, info: (0, g, 3))],
        [(stack, BF16, in_slot(rows, width, False), True)]
        + [(stack, BF16, in_slot(rows, cols), True)] * 3
        + [((SLOTS, 2, width), F32, in_slot(2, width, False), True),
           ((rows, width), BF16, whole((rows, width)), False)],
        [pltpu.VMEM((rows, width), F32), pltpu.VMEM((rows, cols), BF16)], stacks, "attn_bwd")


def grad_kernel(*refs, lefts):
    left_refs, right_refs = refs[:lefts], refs[lefts:2 * lefts]
    out_ref = refs[-1]

    def multiply(left_ref, right_ref):
        left = left_ref[...].reshape(-1, left_ref.shape[2])
        right = right_ref[...].reshape(-1, right_ref.shape[2])
        out_ref[...] = mm(left, right, 0, 0).astype(out_ref.dtype)

    if lefts == 1:
        multiply(left_refs[0], right_refs[0])
    else:
        for t in range(lefts):
            pl.when(pl.program_id(0) == t)(functools.partial(multiply, left_refs[t], right_refs[t]))


def weight_grads(lefts, rights, tiles, left_moves, place, total, earlier, name):
    _, rows, width = rights[0].shape if left_moves else lefts[0].shape
    count = len(lefts)

    def spec(moves):
        if moves:
            return pl.BlockSpec((SPARE, rows, width), lambda t: (0, 0, t))
        return pl.BlockSpec((SPARE, rows, width), lambda t: (0, 0, 0), pipeline_mode=pl.Buffered(buffer_count=1))

    moving = count == 1
    extra = [] if earlier is None else [earlier]
    return pl.pallas_call(
        functools.partial(grad_kernel, lefts=count),
        grid=(tiles,),
        in_specs=[spec(moving and left_moves)] * count + [spec(moving and not left_moves)] * count
        + [pl.BlockSpec(memory_space=pl.ANY)] * len(extra),
        out_specs=pl.BlockSpec((None, width, width), lambda t: place(t) + (0,)),
        out_shape=shape_of((2, total, width)),
        input_output_aliases={2 * count: 0} if extra else {},
        compiler_params=pltpu.CompilerParams(vmem_limit_bytes=VMEM_BYTES),
        name=name,
    )(*lefts, *rights, *extra)


def widen_kernel(in_ref, out_ref):
    out_ref[...] = in_ref[...].astype(F32)


def widen(data, blocks, offset, by_column):
    width = data.shape[1]
    if by_column:
        shape, spec = (width, blocks * width), pl.BlockSpec((width, width), lambda b: (0, b))
    else:
        shape, spec = (blocks * width, width), pl.BlockSpec((width, width), lambda b: (b, 0))
    return pl.pallas_call(
        widen_kernel, grid=(blocks,),
        in_specs=[pl.BlockSpec((width, width), lambda b: (offset + b, 0))],
        out_specs=spec, out_shape=shape_of(shape, F32),
        compiler_params=pltpu.CompilerParams(vmem_limit_bytes=VMEM_BYTES), name="widen",
    )(data)


def ring_layout(n, want):
    subs = 2 if n <= 8 else 1
    unit = 2 * n * subs
    piece = -(-want // unit)
    piece += -piece % 16
    return subs, piece, unit * piece


def ring_kernel(data_ref, out_ref, mine, got, final, start, slots, load_sem, store_sem, swap_send, swap_recv,
                sum_send, sum_recv, full_send, full_recv, *, n, subs, piece):
    section = lax.axis_index("section")
    data = lax.axis_index("dp")
    core = lax.rem(section, 2)
    partner = section + 1 - 2 * core
    half = n // 2

    def place(p):
        p = lax.rem(p + 2 * n, n)
        return jnp.where(p < half, 2 * p, 2 * (n - 1 - p) + 1)

    me = jnp.where(lax.rem(data, 2) == 0, data // 2, n - 1 - data // 2)
    peers = (place(me + 1), place(me - 1))
    signs = (1, -1)
    span = subs * piece

    def chunk(index):
        return lax.rem(index + 2 * n, n)

    def first_row(index, d):
        return pl.multiple_of((chunk(index) * 2 + d) * span, 16)

    loads, swaps = {}, {}
    for j in range(n):
        for d in (0, 1):
            rows = pl.ds(first_row(me - signs[d] * j, d), span)
            loads[j, d] = pltpu.make_async_copy(data_ref.at[core, rows], mine.at[rows], load_sem.at[d, j])
            loads[j, d].start()
    barrier = pltpu.get_barrier_semaphore()
    pl.semaphore_signal(barrier, inc=1, device_id={"section": partner}, device_id_type=pl.DeviceIdType.MESH)
    for d in (0, 1):
        pl.semaphore_signal(barrier, inc=1, device_id={"dp": peers[d]}, device_id_type=pl.DeviceIdType.MESH)
    pl.semaphore_wait(barrier, 3)
    for j in range(n):
        for d in (0, 1):
            rows = pl.ds(first_row(me - signs[d] * j, d), span)
            swaps[j, d] = pltpu.make_async_remote_copy(
                src_ref=data_ref.at[1 - core, rows], dst_ref=got.at[rows],
                send_sem=swap_send.at[d, j], recv_sem=swap_recv.at[d, j],
                device_id={"section": partner}, device_id_type=pl.DeviceIdType.MESH)
            swaps[j, d].start()

    sums, fulls, stores = {}, {}, []

    def own(j, d, u):
        row = pl.multiple_of(first_row(me - signs[d] * j, d) + u * piece, 16)
        rows = pl.ds(row, piece)
        return mine[rows, :].astype(F32) + got[rows, :].astype(F32)

    for s in range(n):
        for d in (0, 1):
            loads[s, d].wait()
            swaps[s, d].wait_recv()
        for u in range(subs):
            for d in (0, 1):
                value = own(s, d, u)
                if s == 0:
                    source = start.at[d, u]
                else:
                    sums[s - 1, d, u].wait_recv()
                    source = slots.at[d, u, s - 1]
                    value = value + source[...].astype(F32)
                if s < n - 1:
                    source[...] = value.astype(BF16)
                    sums[s, d, u] = pltpu.make_async_remote_copy(
                        src_ref=source, dst_ref=slots.at[d, u, s],
                        send_sem=sum_send.at[d, u, s], recv_sem=sum_recv.at[d, u, s],
                        device_id={"dp": peers[d]}, device_id_type=pl.DeviceIdType.MESH)
                    sums[s, d, u].start()
                else:
                    row = pl.multiple_of(first_row(me - signs[d] * s, d) + u * piece, 16)
                    final[pl.ds(row, piece), :] = value.astype(BF16)
    for s in range(n):
        for u in range(subs):
            for d in (0, 1):
                row = pl.multiple_of(first_row(me + signs[d] * (1 - s), d) + u * piece, 16)
                rows = pl.ds(row, piece)
                if s > 0:
                    fulls[s - 1, d, u].wait_recv()
                if s < n - 1:
                    fulls[s, d, u] = pltpu.make_async_remote_copy(
                        src_ref=final.at[rows], dst_ref=final.at[rows],
                        send_sem=full_send.at[d, u, s], recv_sem=full_recv.at[d, u, s],
                        device_id={"dp": peers[d]}, device_id_type=pl.DeviceIdType.MESH)
                    fulls[s, d, u].start()
                copy = pltpu.make_async_copy(final.at[rows], out_ref.at[rows], store_sem.at[d, u, s])
                copy.start()
                stores.append(copy)
    for copy in swaps.values():
        copy.wait_send()
    for copy in sums.values():
        copy.wait_send()
    for copy in fulls.values():
        copy.wait_send()
    for copy in stores:
        copy.wait()


def ring_sum(data, n, subs, piece):
    total, width = data.shape[1:]
    dma = pltpu.SemaphoreType.DMA
    return pl.pallas_call(
        functools.partial(ring_kernel, n=n, subs=subs, piece=piece),
        in_specs=[pl.BlockSpec(memory_space=pl.ANY)],
        out_specs=pl.BlockSpec(memory_space=pl.ANY),
        out_shape=shape_of((total, width)),
        scratch_shapes=[
            pltpu.VMEM((total, width), BF16), pltpu.VMEM((total, width), BF16), pltpu.VMEM((total, width), BF16),
            pltpu.VMEM((2, subs, piece, width), BF16), pltpu.VMEM((2, subs, n - 1, piece, width), BF16),
            dma((2, n)), dma((2, subs, n)), dma((2, n)), dma((2, n)),
            dma((2, subs, n - 1)), dma((2, subs, n - 1)), dma((2, subs, n - 1)), dma((2, subs, n - 1))],
        compiler_params=pltpu.CompilerParams(
            vmem_limit_bytes=VMEM_BYTES, collective_id=0, has_side_effects=True),
        name="ring_sum",
    )(data)


def body(tokens, doc_ids, reset_flags, memory_init, w_proj, vectors, w_down, cotangent):
    data_count = lax.axis_size("dp")
    section = lax.axis_index("section")
    data = lax.axis_index("dp")
    stage = section // 2
    core = section % 2
    first = stage == 0
    _, segments, seg_tokens, width = tokens.shape
    memory_count = memory_init.shape[0]
    hidden = w_proj.shape[2]
    pad = -(memory_count + seg_tokens) % 16
    rows = seg_tokens + memory_count + pad
    pairs = [[0, 1], [2, 3]]

    proj = lax.all_gather(w_proj[0], "section", axis=0, axis_index_groups=pairs)
    down = lax.all_gather(w_down, "section", axis=0, tiled=True, axis_index_groups=pairs)
    vecs = lax.all_gather(vectors[0], "section", axis=0, axis_index_groups=pairs)

    def send(block, route):
        return lax.ppermute(block, "section", route)

    other_tokens = [send(tokens[0, k], TO_FIRST) for k in range(segments)]
    other_cot = [send(cotangent[0, k], TO_SECOND) for k in range(segments)]
    item_a = core * data_count + data
    item_b = (core + 2) * data_count + data
    micros = [(item, k) for k in range(segments) for item in (0, 1)]
    items = (item_a, item_b)
    micro_docs = []
    for item, k in micros:
        docs = lax.dynamic_index_in_dim(doc_ids, items[item], 0, keepdims=False)[k]
        micro_docs.append(jnp.concatenate(
            [docs, jnp.full((memory_count,), -1, jnp.int32), jnp.full((pad,), -2, jnp.int32)]))
    flags = [lax.dynamic_index_in_dim(reset_flags, items[i], 0, keepdims=False) for i in (0, 1)]
    pad_rows = jnp.zeros((pad, width), BF16)

    def fresh(item, k):
        return jnp.bool_(True) if k == 0 else flags[item][k] == 1

    def pick(choice, yes, no):
        return jnp.where(choice, yes, no)

    count = len(micros)
    attn_stacks = ff_stacks = None
    carried = jnp.zeros((rows, width), BF16)
    memory_back = {}
    outs = {}
    for tick in range(count + 1):
        here = min(tick, count - 1)
        item, k = micros[here]
        valid = pick(first, tick < count, tick > 0).astype(jnp.int32)
        slot = pick(first, tick, tick - 1)
        slot = pick(valid == 1, slot, SPARE)
        info = jnp.stack([slot, valid]).astype(jnp.int32)
        if k == 0:
            entering = memory_init
        else:
            entering = pick(fresh(item, k), memory_init, memory_back[(item, k - 1)][:memory_count])
        rows_in = tokens[0, k] if item == 0 else other_tokens[k]
        start = jnp.concatenate([rows_in, entering, pad_rows], axis=0)
        x = pick(first, start, carried)
        docs = pick(first, micro_docs[here], micro_docs[max(tick - 1, 0)])
        drow = docs[None, :]
        dcol = jnp.broadcast_to(docs[:, None], (rows, 128))
        attn_stacks, _ = attn_forward(info, x, proj, vecs[0], drow, dcol, attn_stacks)
        ff_stacks, (y,) = ff_forward(info, attn_stacks[7], proj, down, vecs[1], ff_stacks)
        if tick < count:
            carried = send(y, TO_SECOND)
        if tick > 0:
            done = micros[tick - 1]
            if done[1] + 1 < segments:
                memory_back[done] = send(y[seg_tokens:], TO_FIRST)
            outs[done] = y[:seg_tokens]
    q, k_rows, v, p, o, n1, r1, y1, x_in = attn_stacks
    h, slope, n2, r2 = ff_stacks

    order = [m for k in reversed(range(segments)) for m in range(count) if micros[m][1] == k]
    ffb_stacks = ab_stacks = None
    returning = jnp.zeros((rows, width), BF16)
    memory_forward = {}
    grads = {}
    grad_memory = jnp.zeros((memory_count, width), F32)
    for tick in range(count + 1):
        mine = order[min(tick, count - 1)]
        before = order[max(tick - 1, 0)]
        item, k = micros[mine]
        valid = pick(first, tick > 0, tick < count).astype(jnp.int32)
        slot = pick(valid == 1, pick(first, before, mine), SPARE)
        info = jnp.stack([slot, valid]).astype(jnp.int32)
        if k + 1 < segments:
            memory_grad = memory_forward[(item, k + 1)]
        else:
            memory_grad = jnp.zeros((rows - seg_tokens, width), BF16)
        rows_in = cotangent[0, k] if item == 1 else other_cot[k]
        start = jnp.concatenate([rows_in, memory_grad], axis=0)
        g = pick(first, returning, start)
        ffb_stacks, (dy,) = ff_backward(info, g, n2, r2, vecs[1], slope, proj, down, ffb_stacks)
        ab_stacks, (dx,) = attn_backward(info, dy, n1, r1, vecs[0], q, k_rows, v, p, o, proj, ab_stacks)
        if tick < count:
            returning = send(dx, TO_FIRST)
        if tick > 0:
            done = micros[before]
            grads[done] = dx[:seg_tokens]
            is_fresh = fresh(*done)
            memory_rows = dx[seg_tokens:]
            if done[1] > 0:
                memory_forward[done] = send(pick(is_fresh, jnp.zeros_like(memory_rows), memory_rows), TO_SECOND)
            grad_memory = grad_memory + pick(
                first & is_fresh, memory_rows[:memory_count].astype(F32), 0.0)
    df, da, gv2 = ffb_stacks
    db, dq, dk, dv, gv1 = ab_stacks

    vec_pair = jnp.stack([gv1[:SPARE].sum(axis=0), gv2[:SPARE].sum(axis=0)])
    small = jnp.zeros((4, 2, width), F32)
    small = lax.dynamic_update_slice(small, vec_pair, (stage * 2, 0, 0))
    small = jnp.concatenate([small.reshape(8, width), grad_memory], axis=0)
    small = lax.psum(small, ("section", "dp"))
    total_vec = lax.dynamic_slice(small[:8].reshape(4, 2, width), (section, 0, 0), (1, 2, width))
    share = width // 4
    memory_total = lax.dynamic_slice(small[8:], (0, section * share), (memory_count, share))

    blocks = hidden // width
    half = w_down.shape[0] // width
    subs, piece, total = ring_layout(data_count, (blocks + half) * width)
    stack = weight_grads([h], [df], blocks, True, lambda t: (t // half, blocks + t % half), total, None, "grad_down")
    stack = weight_grads([y1], [da], blocks, False, lambda t: (1, t), total, stack, "grad_up")
    stack = weight_grads([x_in] * 3 + [o], [dq, dk, dv, db], blocks, False, lambda t: (0, t), total, stack, "grad_attn")
    summed = ring_sum(stack, data_count, subs, piece)
    total_proj = widen(summed, blocks, 0, True)
    total_down = widen(summed, half, blocks, False)

    def collect(done, table, route, keep_first):
        item_own, item_other = (0, 1) if keep_first else (1, 0)
        blocks = []
        for k in range(segments):
            if keep_first:
                got = send(table[(1, k)], route)
                blocks.append(pick(first, table[(0, k)], got))
            else:
                got = send(table[(0, k)], route)
                blocks.append(pick(first, got, table[(1, k)]))
        return jnp.stack(blocks)[None]

    block_rows = collect(None, outs, TO_FIRST, False)
    input_rows = collect(None, grads, TO_SECOND, True)
    return (block_rows, input_rows, total_proj[None], total_vec, total_down, memory_total)


def solution(mesh):
    items = P(("section", "dp"), None, None, None)
    return jax.shard_map(
        body,
        mesh=mesh,
        in_specs=(items, P(), P(), P(), P("section", None, None), P("section", None, None),
                  P("section", None), items),
        out_specs=(items, items, P("section", None, None), P("section", None, None),
                   P("section", None), P(None, "section")),
        check_vma=False,
    )
```

```python
import functools

import jax
import jax.numpy as jnp
from jax import lax
from jax.experimental import pallas as pl
from jax.experimental.pallas import tpu as pltpu
from jax.sharding import PartitionSpec as P

HEADS = 12
DOCS = 4
NORM_EPSILON = 1e-06
NEGATIVE = -1e30
BF16 = jnp.bfloat16
F32 = jnp.float32
VMEM_BYTES = 60 * 2**20
GROUP = 4
FF_BLOCK = 1024
TILE = 16
MICROS = 4
MESH = pl.DeviceIdType.MESH


def mm(left, right, ca=1, cb=0):
    return lax.dot_general(
        left, right, (((ca,), (cb,)), ((), ())), preferred_element_type=F32
    )


def shape_of(shape, dtype=BF16):
    return jax.ShapeDtypeStruct(shape, dtype)


def anywhere():
    return pl.BlockSpec(memory_space=pl.ANY)


def on_chip():
    return pl.BlockSpec(memory_space=pltpu.VMEM)


def head_rows(block, group, head):
    lane = lax.broadcasted_iota(jnp.int32, (1, block.shape[1]), 1) // head
    return jnp.concatenate([jnp.where(lane == h, block, jnp.zeros_like(block)) for h in range(group)], axis=0)


def head_fold(stacked, group, head):
    total, width = stacked.shape
    rows = total // group
    lane = lax.broadcasted_iota(jnp.int32, (1, width), 1) // head
    out = stacked[:rows]
    for h in range(1, group):
        out = jnp.where(lane == h, stacked[h * rows:(h + 1) * rows], out)
    return out


def normalise(summed):
    center = summed - jnp.mean(summed, axis=-1, keepdims=True)
    variance = jnp.mean(center * center, axis=-1, keepdims=True)
    inverse = lax.rsqrt(variance + NORM_EPSILON)
    return center * inverse, inverse


def norm_back(g, n, inverse, gain):
    u = g * gain
    dz = inverse * (u - jnp.mean(u, axis=-1, keepdims=True) - n * jnp.mean(u * n, axis=-1, keepdims=True))
    return dz, jnp.sum(g * n, axis=0, keepdims=True), jnp.sum(g, axis=0, keepdims=True)


def layers_kernel(tokens_ref, cot_ref, proj_ref, down_ref, vec_ref, init_ref, fresh_ref, key_ref, query_ref,
                  out_ref, gtok_ref, gmem_ref, gvec_ref,
                  xs, qs, ks, vs, os_, n1s, y1s, n2s, hs, ss, ps, dfs, dbs, dqs, dks, dvs, das,
                  hop_ref, back_ref, tok_other, cot_other,
                  wa, w1, w2, vecs, x, q, k, v, o, n1, y1, n2, df, db, do, acc, y, hb, sb, pb, r1, r2,
                  mem_in, mem_grad,
                  share_local, share_send, share_recv, tok_send, tok_recv, cot_send, cot_recv,
                  hop_send, hop_recv, back_send, back_recv, mem_send, mem_recv, mg_send, mg_recv,
                  out_sem, out_send, out_recv, gt_sem, gt_send, gt_recv,
                  load_sem, save_sem, h_sem, s_sem, p_sem):
    section = lax.axis_index("section")
    stage = section // 2
    core = lax.rem(section, 2)
    first = stage == 0
    second = stage == 1
    mate = {"section": section + 1 - 2 * core}
    across = {"section": section + 2 - 4 * stage}
    segments, tokens, width = tokens_ref.shape
    rows = x.shape[0]
    hidden = proj_ref.shape[1]
    head = width // HEADS
    cols = GROUP * head
    groups = HEADS // GROUP
    blocks = hidden // FF_BLOCK
    halfd = down_ref.shape[0]
    micros = 2 * segments
    scale = head ** (-0.5)
    body_rows = pl.ds(0, tokens)
    last_rows = pl.ds(tokens, rows - tokens)

    def remote(source, target, send, recv, device):
        return pltpu.make_async_remote_copy(src_ref=source, dst_ref=target, send_sem=send, recv_sem=recv,
                                            device_id=device, device_id_type=MESH)

    local = pltpu.make_async_copy

    barrier = pltpu.get_barrier_semaphore()
    pl.semaphore_signal(barrier, inc=1, device_id=mate, device_id_type=MESH)
    pl.semaphore_signal(barrier, inc=1, device_id=across, device_id_type=MESH)
    pl.semaphore_wait(barrier, 2)

    down_rows = pl.ds(pl.multiple_of(core * halfd, 16), halfd)
    other_rows = pl.ds(pl.multiple_of((1 - core) * halfd, 16), halfd)
    down_away = remote(down_ref, w2.at[down_rows], share_send.at[1], share_recv.at[1], mate)
    vec_away = remote(vec_ref, vecs.at[core], share_send.at[2], share_recv.at[2], mate)
    proj_a = remote(proj_ref, wa, share_send.at[0], share_recv.at[0], mate)
    proj_b = remote(proj_ref, w1, share_send.at[0], share_recv.at[0], mate)
    proj_here_a = local(proj_ref, wa, share_local.at[0])
    proj_here_b = local(proj_ref, w1, share_local.at[0])
    down_here = local(down_ref, w2.at[down_rows], share_local.at[1])
    vec_here = local(vec_ref, vecs.at[core], share_local.at[2])

    @pl.when(core == 0)
    def _():
        proj_a.start()
        proj_here_a.start()

    @pl.when(core == 1)
    def _():
        proj_b.start()
        proj_here_b.start()

    vec_away.start()
    vec_here.start()
    down_away.start()
    down_here.start()

    def tok_copy(k_):
        return remote(tokens_ref.at[k_], tok_other.at[k_], tok_send.at[k_], tok_recv.at[k_], across)

    def cot_copy(k_):
        return remote(cot_ref.at[k_], cot_other.at[k_], cot_send.at[k_], cot_recv.at[k_], across)

    @pl.when(second)
    def _():
        for k_ in range(segments):
            tok_copy(k_).start()

    @pl.when(first)
    def _():
        cot_copy(segments - 1).start()

    vec_here.wait()
    vec_away.wait_recv()

    @pl.when(core == 0)
    def _():
        proj_here_a.wait()

    @pl.when(core == 1)
    def _():
        proj_a.wait_recv()

    def hop_copy(m):
        return remote(y.at[lax.rem(m, 2)], hop_ref.at[m], hop_send.at[m], hop_recv.at[m], across)

    def mem_copy(m):
        return remote(y.at[lax.rem(m, 2), last_rows], mem_in.at[m], mem_send.at[m], mem_recv.at[m], across)

    def out_here(m, seg):
        return local(y.at[lax.rem(m, 2), body_rows], out_ref.at[seg], out_sem.at[m])

    def out_away(m, seg):
        return remote(y.at[lax.rem(m, 2), body_rows], out_ref.at[seg], out_send.at[seg], out_recv.at[seg], across)

    kept = [(x, xs), (q, qs), (k, ks), (v, vs), (o, os_), (n1, n1s), (y1, y1s), (n2, n2s)]

    def saves(m):
        return [local(here, there.at[m], save_sem.at[i]) for i, (here, there) in enumerate(kept)]

    def band(g):
        return pl.ds(pl.multiple_of(g * cols, cols), cols)

    def h_save(m, j):
        b = lax.rem(j, 2)
        return local(hb.at[b], hs.at[m, :, pl.ds(pl.multiple_of(j * FF_BLOCK, FF_BLOCK), FF_BLOCK)], h_sem.at[b])

    def s_save(m, j):
        b = lax.rem(j, 2)
        return local(sb.at[b], ss.at[m, :, pl.ds(pl.multiple_of(j * FF_BLOCK, FF_BLOCK), FF_BLOCK)], s_sem.at[b])

    def p_save(m, g):
        b = lax.rem(g, 2)
        return local(pb.at[b], ps.at[m, g], p_sem.at[b])

    def forward(m, carry):
        item = lax.rem(m, 2)
        seg = m // 2

        @pl.when(m > 0)
        def _():
            for save in saves(m - 1):
                save.wait()

        body_load = [local(source.at[seg], x.at[body_rows], load_sem.at[0]) for source in (tokens_ref, tok_other)]
        whole_load = local(hop_ref.at[m], x, load_sem.at[0])

        @pl.when(first)
        def _():
            @pl.when(item == 0)
            def _():
                body_load[0].start()

            @pl.when(item == 1)
            def _():
                tok_copy(seg).wait_recv()
                body_load[1].start()

            @pl.when(seg == 0)
            def _():
                x[last_rows, :] = init_ref[...]

            @pl.when(seg > 0)
            def _():
                mem_copy(m - 2).wait_recv()
                x[last_rows, :] = jnp.where(fresh_ref[item] > 0, init_ref[...], mem_in[m - 2])

            body_load[0].wait()

        @pl.when(second)
        def _():
            hop_copy(m).wait_recv()
            whole_load.start()
            whole_load.wait()

        out = saves(m)
        out[0].start()

        def attend(g, carry2):
            here = band(g)
            xv = x[...]
            q[:, here] = mm(xv, wa[:, here]).astype(BF16)
            k[:, here] = mm(xv, wa[:, pl.ds(pl.multiple_of(width + g * cols, cols), cols)]).astype(BF16)
            v[:, here] = mm(xv, wa[:, pl.ds(pl.multiple_of(2 * width + g * cols, cols), cols)]).astype(BF16)

            @pl.when(g >= 2)
            def _():
                p_save(m, g - 2).wait()

            s = mm(k[:, here], head_rows(q[:, here] * scale, GROUP, head), 1, 1)
            seen = (key_ref[m, :, 0:1] & query_ref[m]) != 0
            s = jnp.where(seen, s, NEGATIVE)
            e = jnp.exp(s - jnp.max(s, axis=0, keepdims=True))
            p = (e * (1.0 / jnp.sum(e, axis=0, keepdims=True))).astype(BF16)
            pb[lax.rem(g, 2)] = p
            p_save(m, g).start()
            o[:, here] = head_fold(mm(p, v[:, here], 0, 0), GROUP, head).astype(BF16)
            return carry2

        lax.fori_loop(0, groups, attend, 0)
        for i in (1, 2, 3, 4):
            out[i].start()
        normed, inverse = normalise(x[...].astype(F32) + mm(o[...], wa[:, pl.ds(3 * width, width)]))
        n1[...] = normed.astype(BF16)
        r1[m] = jnp.broadcast_to(inverse, r1.shape[1:])
        y1v = (normed * vecs[0, 0:1, :] + vecs[0, 1:2, :]).astype(BF16)
        y1[...] = y1v
        acc[...] = y1v.astype(F32)
        out[5].start()
        out[6].start()
        p_save(m, groups - 2).wait()
        p_save(m, groups - 1).wait()

        @pl.when(m == 0)
        def _():
            @pl.when(core == 0)
            def _():
                proj_b.wait_recv()

            @pl.when(core == 1)
            def _():
                proj_here_b.wait()

            down_here.wait()
            remote(down_ref, w2.at[other_rows], share_send.at[1], share_recv.at[1], mate).wait_recv()

        def feed(j, carry2):
            b = lax.rem(j, 2)

            @pl.when(j >= 2)
            def _():
                h_save(m, j - 2).wait()
                s_save(m, j - 2).wait()

            half = FF_BLOCK // 2
            yv = y1[...]
            pre = [mm(yv, w1[:, pl.ds(pl.multiple_of(j * FF_BLOCK + i * half, half), half)]) for i in range(2)]
            for i in range(2):
                a = pre[i]
                gate = 0.5 * (1.0 + lax.erf(a * 0.7071067811865476))
                hb[b, :, i * half:(i + 1) * half] = (a * gate).astype(BF16)
                sb[b, :, i * half:(i + 1) * half] = (
                    gate + a * jnp.exp(-0.5 * a * a) * 0.3989422804014327).astype(BF16)
            h_save(m, j).start()
            s_save(m, j).start()
            acc[...] += mm(hb[b], w2[pl.ds(pl.multiple_of(j * FF_BLOCK, FF_BLOCK), FF_BLOCK), :])
            return carry2

        lax.fori_loop(0, blocks, feed, 0)

        normed, inverse = normalise(acc[...])
        n2[...] = normed.astype(BF16)
        r2[m] = jnp.broadcast_to(inverse, r2.shape[1:])

        @pl.when(m >= 2)
        def _():
            @pl.when(first)
            def _():
                hop_copy(m - 2).wait_send()

            @pl.when(second)
            def _():
                mem_copy(m - 2).wait_send()

                @pl.when(item == 0)
                def _():
                    out_away(m - 2, seg - 1).wait_send()

                @pl.when(item == 1)
                def _():
                    out_here(m - 2, seg - 1).wait()

        y[item] = (normed * vecs[1, 0:1, :] + vecs[1, 1:2, :]).astype(BF16)
        out[7].start()

        @pl.when(first)
        def _():
            hop_copy(m).start()

        @pl.when(second)
        def _():
            @pl.when(seg + 1 < segments)
            def _():
                mem_copy(m).start()

            @pl.when(item == 0)
            def _():
                out_away(m, seg).start()

            @pl.when(item == 1)
            def _():
                out_here(m, seg).start()

        for j in range(max(0, blocks - 2), blocks):
            h_save(m, j).wait()
            s_save(m, j).wait()
        return carry

    lax.fori_loop(0, micros, forward, 0)
    for save in saves(micros - 1):
        save.wait()

    @pl.when(first)
    def _():
        for k_ in reversed(range(segments - 1)):
            cot_copy(k_).start()
        for m in range(micros - 2, micros):
            hop_copy(m).wait_send()
        for k_ in range(segments):
            out_away(0, k_).wait_recv()

    @pl.when(second)
    def _():
        out_away(micros - 2, segments - 1).wait_send()
        out_here(micros - 1, segments - 1).wait()

    gmem_ref[...] = jnp.zeros(gmem_ref.shape, F32)
    gvec_ref[...] = jnp.zeros(gvec_ref.shape, F32)

    def back_copy(t):
        return remote(y.at[lax.rem(t, 2)], back_ref.at[t], back_send.at[t], back_recv.at[t], across)

    def mg_copy(t):
        return remote(y.at[lax.rem(t, 2), last_rows], mem_grad.at[t], mg_send.at[t], mg_recv.at[t], across)

    def gt_here(t, seg):
        return local(y.at[lax.rem(t, 2), body_rows], gtok_ref.at[seg], gt_sem.at[t])

    def gt_away(t, seg):
        return remote(y.at[lax.rem(t, 2), body_rows], gtok_ref.at[seg], gt_send.at[seg], gt_recv.at[seg], across)

    def s_load(m, j):
        b = lax.rem(j, 2)
        return local(ss.at[m, :, pl.ds(pl.multiple_of(j * FF_BLOCK, FF_BLOCK), FF_BLOCK)], sb.at[b], s_sem.at[b])

    def d_save(m, j):
        b = lax.rem(j, 2)
        return local(hb.at[b], das.at[m, :, pl.ds(pl.multiple_of(j * FF_BLOCK, FF_BLOCK), FF_BLOCK)], h_sem.at[b])

    def p_load(m, g):
        b = lax.rem(g, 2)
        return local(ps.at[m, g], pb.at[b], p_sem.at[b])

    def back_saves(m):
        pairs = [(df, dfs), (db, dbs), (x, dqs), (o, dks), (y1, dvs)]
        return [local(here, there.at[m], save_sem.at[i]) for i, (here, there) in enumerate(pairs)]

    def backward(t, carry):
        item = lax.rem(t, 2)
        seg = segments - 1 - t // 2
        m = 2 * seg + item
        before = 2 * (segments - 1 - (t - 1) // 2) + lax.rem(t - 1 + 2, 2)

        @pl.when(t > 0)
        def _():
            for save in back_saves(before):
                save.wait()

        loads = [local(source.at[m], here, load_sem.at[1 + i])
                 for i, (source, here) in enumerate([(n2s, n2), (qs, q), (ks, k), (vs, v), (n1s, n1)])]
        body_load = [local(source.at[seg], y1.at[body_rows], load_sem.at[0]) for source in (cot_ref, cot_other)]
        whole_load = local(back_ref.at[t], y1, load_sem.at[0])
        for load in loads:
            load.start()
        s_load(m, 0).start()
        s_load(m, 1).start()
        p_load(m, 0).start()
        p_load(m, 1).start()

        @pl.when(second)
        def _():
            @pl.when(item == 1)
            def _():
                body_load[0].start()

            @pl.when(item == 0)
            def _():
                cot_copy(seg).wait_recv()
                body_load[1].start()

            @pl.when(seg + 1 == segments)
            def _():
                y1[last_rows, :] = jnp.zeros((rows - tokens, width), BF16)

            @pl.when(seg + 1 < segments)
            def _():
                mg_copy(t - 2).wait_recv()
                got = mem_grad[t - 2]
                y1[last_rows, :] = jnp.where(fresh_ref[item] > 0, jnp.zeros_like(got), got)

            body_load[0].wait()

        @pl.when(first)
        def _():
            back_copy(t).wait_recv()
            whole_load.start()
            whole_load.wait()

        loads[0].wait()
        dz, gain_grad, bias_grad = norm_back(y1[...].astype(F32), n2[...].astype(F32), r2[m, :, 0:1], vecs[1, 0:1, :])
        gvec_ref[2:3, :] += gain_grad
        gvec_ref[3:4, :] += bias_grad
        df[...] = dz.astype(BF16)
        acc[...] = dz
        out = back_saves(m)
        out[0].start()

        def feed(j, carry2):
            b = lax.rem(j, 2)

            @pl.when(j >= 2)
            def _():
                d_save(m, j - 2).wait()

            s_load(m, j).wait()
            half = FF_BLOCK // 2
            dfv = df[...]
            dh = [mm(dfv, w2[pl.ds(pl.multiple_of(j * FF_BLOCK + i * half, half), half), :], 1, 1) for i in range(2)]
            for i in range(2):
                cut = slice(i * half, (i + 1) * half)
                hb[b, :, cut] = (dh[i] * sb[b, :, cut].astype(F32)).astype(BF16)
            d_save(m, j).start()

            @pl.when(j + 2 < blocks)
            def _():
                s_load(m, j + 2).start()

            acc[...] += mm(hb[b], w1[:, pl.ds(pl.multiple_of(j * FF_BLOCK, FF_BLOCK), FF_BLOCK)], 1, 1)
            return carry2

        lax.fori_loop(0, blocks, feed, 0)
        for load in loads[1:]:
            load.wait()
        dz, gain_grad, bias_grad = norm_back(acc[...].astype(BF16).astype(F32), n1[...].astype(F32), r1[m, :, 0:1],
                                             vecs[0, 0:1, :])
        gvec_ref[0:1, :] += gain_grad
        gvec_ref[1:2, :] += bias_grad
        db[...] = dz.astype(BF16)
        acc[...] = dz
        out[1].start()

        def attend(g, carry2):
            here = band(g)
            b = lax.rem(g, 2)
            p_load(m, g).wait()
            gv = mm(db[...], wa[here, pl.ds(3 * width, width)], 1, 1).astype(BF16)
            grads = head_rows(gv, GROUP, head)
            dp = mm(v[:, here], grads, 1, 1)
            p = pb[b]
            weight = p.astype(F32)
            ds = (weight * (dp - jnp.sum(weight * dp, axis=0, keepdims=True))).astype(BF16)
            dv = mm(p, grads).astype(BF16)
            dk = mm(ds, head_rows(q[:, here] * scale, GROUP, head)).astype(BF16)
            dq = (head_fold(mm(ds, k[:, here], 0, 0), GROUP, head) * scale).astype(BF16)

            @pl.when(g + 2 < groups)
            def _():
                p_load(m, g + 2).start()

            x[:, here] = dq
            o[:, here] = dk
            y1[:, here] = dv
            acc[...] += (mm(dq, wa[:, here], 1, 1)
                         + mm(dk, wa[:, pl.ds(pl.multiple_of(width + g * cols, cols), cols)], 1, 1)
                         + mm(dv, wa[:, pl.ds(pl.multiple_of(2 * width + g * cols, cols), cols)], 1, 1))
            return carry2

        lax.fori_loop(0, groups, attend, 0)
        for i in (2, 3, 4):
            out[i].start()

        @pl.when(t >= 2)
        def _():
            @pl.when(second)
            def _():
                back_copy(t - 2).wait_send()

            @pl.when(first)
            def _():
                mg_copy(t - 2).wait_send()

                @pl.when(item == 1)
                def _():
                    gt_away(t - 2, seg + 1).wait_send()

                @pl.when(item == 0)
                def _():
                    gt_here(t - 2, seg + 1).wait()

        dx = acc[...].astype(BF16)
        y[item] = dx

        @pl.when(second)
        def _():
            back_copy(t).start()

        @pl.when(first)
        def _():
            tail = dx[tokens:, :].astype(F32)

            @pl.when(seg > 0)
            def _():
                mg_copy(t).start()
                gmem_ref[...] += jnp.where(fresh_ref[item] > 0, tail, 0.0)

            @pl.when(seg == 0)
            def _():
                gmem_ref[...] += tail

            @pl.when(item == 0)
            def _():
                gt_here(t, seg).start()

            @pl.when(item == 1)
            def _():
                gt_away(t, seg).start()

        for j in range(max(0, blocks - 2), blocks):
            d_save(m, j).wait()
        return carry

    lax.fori_loop(0, micros, backward, 0)
    for save in back_saves(1):
        save.wait()

    @pl.when(second)
    def _():
        for t in range(micros - 2, micros):
            back_copy(t).wait_send()
        for k_ in range(segments):
            tok_copy(k_).wait_send()
            gt_away(1, k_).wait_recv()

    @pl.when(first)
    def _():
        gt_here(micros - 2, 0).wait()
        gt_away(micros - 1, 0).wait_send()
        for k_ in range(segments):
            cot_copy(k_).wait_send()

    proj_a.wait_send()
    down_away.wait_send()
    vec_away.wait_send()


def run_layers(tokens, cotangent, proj, down, vec, init, fresh, key_bits, query_bits):
    segments, seg_tokens, width = tokens.shape
    rows = seg_tokens + TILE
    hidden = proj.shape[1]
    micros = 2 * segments
    groups = HEADS // GROUP
    span = GROUP * rows
    stack = shape_of((micros, rows, width))
    wide = shape_of((micros, rows, hidden))
    low = pltpu.VMEM((rows, width), BF16)
    dma = pltpu.SemaphoreType.DMA
    pair = pltpu.VMEM((2, rows, FF_BLOCK), BF16)
    inverse = pltpu.VMEM((micros, rows, 128), F32)
    tails = pltpu.VMEM((2, TILE, width), BF16)
    return pl.pallas_call(
        layers_kernel,
        in_specs=[anywhere()] * 4 + [on_chip()] * 5,
        out_specs=[anywhere()] * 2 + [on_chip()] * 2 + [anywhere()] * 21,
        out_shape=[shape_of(tokens.shape), shape_of(tokens.shape), shape_of((TILE, width), F32),
                   shape_of((8, width), F32)]
        + [stack] * 8 + [wide] * 2 + [shape_of((micros, groups, rows, span))] + [stack] * 5 + [wide]
        + [stack] * 2 + [shape_of(tokens.shape)] * 2,
        scratch_shapes=[
            pltpu.VMEM((width, hidden), BF16), pltpu.VMEM((width, hidden), BF16), pltpu.VMEM((hidden, width), BF16),
            pltpu.VMEM((2, 2, width), F32)] + [low] * 11 + [
            pltpu.VMEM((rows, width), F32), pltpu.VMEM((2, rows, width), BF16), pair, pair,
            pltpu.VMEM((2, rows, span), BF16), inverse, inverse, tails, tails,
            dma((3,)), dma((3,)), dma((3,)), dma((segments,)), dma((segments,)), dma((segments,)), dma((segments,)),
            dma((micros,)), dma((micros,)), dma((micros,)), dma((micros,)), dma((2,)), dma((2,)), dma((2,)), dma((2,)),
            dma((micros,)), dma((segments,)), dma((segments,)), dma((micros,)), dma((segments,)), dma((segments,)),
            dma((6,)), dma((8,)), dma((2,)), dma((2,)), dma((2,))],
        compiler_params=pltpu.CompilerParams(vmem_limit_bytes=VMEM_BYTES, collective_id=1, has_side_effects=True),
        name="layers",
    )(tokens, cotangent, proj, down, vec, init, fresh, key_bits, query_bits)


def grad_kernel(*refs, lefts):
    left_refs, right_refs = refs[:lefts], refs[lefts:2 * lefts]
    out_ref = refs[-1]

    def multiply(left_ref, right_ref):
        left = left_ref[...].reshape(-1, left_ref.shape[2])
        right = right_ref[...].reshape(-1, right_ref.shape[2])
        out_ref[...] = mm(left, right, 0, 0).astype(out_ref.dtype)

    if lefts == 1:
        multiply(left_refs[0], right_refs[0])
    else:
        for t in range(lefts):
            pl.when(pl.program_id(0) == t)(functools.partial(multiply, left_refs[t], right_refs[t]))


def weight_grads(lefts, rights, tiles, left_moves, place, total, earlier, name):
    _, rows, width = rights[0].shape if left_moves else lefts[0].shape
    count = len(lefts)

    def spec(moves):
        if moves:
            return pl.BlockSpec((MICROS, rows, width), lambda t: (0, 0, t))
        return pl.BlockSpec((MICROS, rows, width), lambda t: (0, 0, 0), pipeline_mode=pl.Buffered(buffer_count=1))

    moving = count == 1
    extra = [] if earlier is None else [earlier]
    return pl.pallas_call(
        functools.partial(grad_kernel, lefts=count),
        grid=(tiles,),
        in_specs=[spec(moving and left_moves)] * count + [spec(moving and not left_moves)] * count
        + [pl.BlockSpec(memory_space=pl.ANY)] * len(extra),
        out_specs=pl.BlockSpec((None, width, width), lambda t: place(t) + (0,)),
        out_shape=shape_of((2, total, width)),
        input_output_aliases={2 * count: 0} if extra else {},
        compiler_params=pltpu.CompilerParams(vmem_limit_bytes=VMEM_BYTES),
        name=name,
    )(*lefts, *rights, *extra)


def widen_kernel(in_ref, out_ref):
    out_ref[...] = in_ref[...].astype(F32)


def widen(data, blocks, offset, by_column):
    width = data.shape[1]
    if by_column:
        shape, spec = (width, blocks * width), pl.BlockSpec((width, width), lambda b: (0, b))
    else:
        shape, spec = (blocks * width, width), pl.BlockSpec((width, width), lambda b: (b, 0))
    return pl.pallas_call(
        widen_kernel, grid=(blocks,),
        in_specs=[pl.BlockSpec((width, width), lambda b: (offset + b, 0))],
        out_specs=spec, out_shape=shape_of(shape, F32),
        compiler_params=pltpu.CompilerParams(vmem_limit_bytes=VMEM_BYTES), name="widen",
    )(data)


def ring_layout(n, want):
    subs = 2 if n <= 8 else 1
    unit = 2 * n * subs
    piece = -(-want // unit)
    piece += -piece % 16
    return subs, piece, unit * piece


def flipped(index, bit):
    return index + bit - 2 * bit * lax.rem(index // bit, 2)


def ring_kernel(data_ref, small_ref, out_ref, small_out, mine, got, final, start, slots, held, arrived,
                load_sem, store_sem, swap_send, swap_recv,
                sum_send, sum_recv, full_send, full_recv, small_send, small_recv, *, n, subs, piece, hops):
    section = lax.axis_index("section")
    data = lax.axis_index("dp")
    core = lax.rem(section, 2)
    partner = section + 1 - 2 * core
    half = n // 2

    def place(p):
        p = lax.rem(p + 2 * n, n)
        return jnp.where(p < half, 2 * p, 2 * (n - 1 - p) + 1)

    me = jnp.where(lax.rem(data, 2) == 0, data // 2, n - 1 - data // 2)
    peers = (place(me + 1), place(me - 1))
    signs = (1, -1)
    span = subs * piece

    def chunk(index):
        return lax.rem(index + 2 * n, n)

    def first_row(index, d):
        return pl.multiple_of((chunk(index) * 2 + d) * span, 16)

    loads, swaps = {}, {}
    for j in range(n):
        for d in (0, 1):
            rows = pl.ds(first_row(me - signs[d] * j, d), span)
            loads[j, d] = pltpu.make_async_copy(data_ref.at[core, rows], mine.at[rows], load_sem.at[d, j])
            loads[j, d].start()
    barrier = pltpu.get_barrier_semaphore()
    pl.semaphore_signal(barrier, inc=1, device_id={"section": partner}, device_id_type=pl.DeviceIdType.MESH)
    for d in (0, 1):
        pl.semaphore_signal(barrier, inc=1, device_id={"dp": peers[d]}, device_id_type=pl.DeviceIdType.MESH)
    friends = [{axis: flipped(section if axis == "section" else data, bit)} for axis, bit in hops]
    for friend in friends:
        pl.semaphore_signal(barrier, inc=1, device_id=friend, device_id_type=pl.DeviceIdType.MESH)
    pl.semaphore_wait(barrier, 3 + len(friends))
    held[0] = small_ref[...]
    smalls = []

    def start_small(i):
        smalls.append(pltpu.make_async_remote_copy(
            src_ref=held.at[i], dst_ref=arrived.at[i], send_sem=small_send.at[i], recv_sem=small_recv.at[i],
            device_id=friends[i], device_id_type=pl.DeviceIdType.MESH))
        smalls[i].start()

    def finish_small(i):
        smalls[i].wait_recv()
        total = held[i] + arrived[i]
        if i + 1 < len(friends):
            held[i + 1] = total
            start_small(i + 1)
        else:
            small_out[...] = total

    start_small(0)
    for j in range(n):
        for d in (0, 1):
            rows = pl.ds(first_row(me - signs[d] * j, d), span)
            swaps[j, d] = pltpu.make_async_remote_copy(
                src_ref=data_ref.at[1 - core, rows], dst_ref=got.at[rows],
                send_sem=swap_send.at[d, j], recv_sem=swap_recv.at[d, j],
                device_id={"section": partner}, device_id_type=pl.DeviceIdType.MESH)
            swaps[j, d].start()

    sums, fulls, stores = {}, {}, []

    def own(j, d, u):
        row = pl.multiple_of(first_row(me - signs[d] * j, d) + u * piece, 16)
        rows = pl.ds(row, piece)
        return mine[rows, :].astype(F32) + got[rows, :].astype(F32)

    for s in range(n):
        for d in (0, 1):
            loads[s, d].wait()
            swaps[s, d].wait_recv()
        for u in range(subs):
            for d in (0, 1):
                value = own(s, d, u)
                if s == 0:
                    source = start.at[d, u]
                else:
                    sums[s - 1, d, u].wait_recv()
                    source = slots.at[d, u, s - 1]
                    value = value + source[...].astype(F32)
                if s < n - 1:
                    source[...] = value.astype(BF16)
                    sums[s, d, u] = pltpu.make_async_remote_copy(
                        src_ref=source, dst_ref=slots.at[d, u, s],
                        send_sem=sum_send.at[d, u, s], recv_sem=sum_recv.at[d, u, s],
                        device_id={"dp": peers[d]}, device_id_type=pl.DeviceIdType.MESH)
                    sums[s, d, u].start()
                else:
                    row = pl.multiple_of(first_row(me - signs[d] * s, d) + u * piece, 16)
                    final[pl.ds(row, piece), :] = value.astype(BF16)
    waiting = list(range(len(friends)))
    for s in range(n):
        if s > 0 and waiting:
            finish_small(waiting.pop(0))
        for u in range(subs):
            for d in (0, 1):
                row = pl.multiple_of(first_row(me + signs[d] * (1 - s), d) + u * piece, 16)
                rows = pl.ds(row, piece)
                if s > 0:
                    fulls[s - 1, d, u].wait_recv()
                if s < n - 1:
                    fulls[s, d, u] = pltpu.make_async_remote_copy(
                        src_ref=final.at[rows], dst_ref=final.at[rows],
                        send_sem=full_send.at[d, u, s], recv_sem=full_recv.at[d, u, s],
                        device_id={"dp": peers[d]}, device_id_type=pl.DeviceIdType.MESH)
                    fulls[s, d, u].start()
                copy = pltpu.make_async_copy(final.at[rows], out_ref.at[rows], store_sem.at[d, u, s])
                copy.start()
                stores.append(copy)
    for i in waiting:
        finish_small(i)
    for copy in smalls:
        copy.wait_send()
    for copy in swaps.values():
        copy.wait_send()
    for copy in sums.values():
        copy.wait_send()
    for copy in fulls.values():
        copy.wait_send()
    for copy in stores:
        copy.wait()


def ring_sum(data, small, n, sections, subs, piece):
    total, width = data.shape[1:]
    hops = [("dp", 1 << i) for i in range(n.bit_length() - 1)] + [("section", 1 << i) for i in range(sections.bit_length() - 1)]
    dma = pltpu.SemaphoreType.DMA
    return pl.pallas_call(
        functools.partial(ring_kernel, n=n, subs=subs, piece=piece, hops=hops),
        in_specs=[pl.BlockSpec(memory_space=pl.ANY), pl.BlockSpec(memory_space=pltpu.VMEM)],
        out_specs=[pl.BlockSpec(memory_space=pl.ANY), pl.BlockSpec(memory_space=pltpu.VMEM)],
        out_shape=[shape_of((total, width)), shape_of(small.shape, F32)],
        scratch_shapes=[
            pltpu.VMEM((total, width), BF16), pltpu.VMEM((total, width), BF16), pltpu.VMEM((total, width), BF16),
            pltpu.VMEM((2, subs, piece, width), BF16), pltpu.VMEM((2, subs, n - 1, piece, width), BF16),
            pltpu.VMEM((len(hops),) + small.shape, F32), pltpu.VMEM((len(hops),) + small.shape, F32),
            dma((2, n)), dma((2, subs, n)), dma((2, n)), dma((2, n)),
            dma((2, subs, n - 1)), dma((2, subs, n - 1)), dma((2, subs, n - 1)), dma((2, subs, n - 1)),
            dma((len(hops),)), dma((len(hops),))],
        compiler_params=pltpu.CompilerParams(
            vmem_limit_bytes=VMEM_BYTES, collective_id=0, has_side_effects=True),
        name="ring_sum",
    )(data, small)


def body(tokens, doc_ids, reset_flags, memory_init, w_proj, vectors, w_down, cotangent):
    data_count = lax.axis_size("dp")
    section = lax.axis_index("section")
    data = lax.axis_index("dp")
    first = section < 2
    core = section % 2
    _, segments, seg_tokens, width = tokens.shape
    memory_count = memory_init.shape[0]
    hidden = w_proj.shape[2]
    pad = TILE - memory_count
    items = (core * data_count + data, (core + 2) * data_count + data)
    micros = [(item, k) for k in range(segments) for item in (0, 1)]
    flags = [lax.dynamic_index_in_dim(reset_flags, items[i], 0, keepdims=False) for i in (0, 1)]
    docs = jnp.stack([lax.dynamic_index_in_dim(doc_ids, items[item], 0, keepdims=False)[k] for item, k in micros])
    bits = jnp.left_shift(jnp.int32(1), docs)
    lines = jnp.ones((len(micros), 1), jnp.int32)
    every = (1 << DOCS) - 1
    key_bits = jnp.concatenate([bits, jnp.repeat(lines * every, memory_count, 1), jnp.repeat(lines * 0, pad, 1)], axis=1)
    query_bits = jnp.concatenate([bits, jnp.repeat(lines * every, TILE, 1)], axis=1)
    key_bits = jnp.broadcast_to(key_bits[:, :, None], key_bits.shape + (128,))
    query_bits = jnp.tile(query_bits, (1, GROUP))[:, None, :]
    fresh = jnp.stack([jnp.broadcast_to(flags[i][segments - 1], (TILE, width)) for i in (0, 1)]).astype(F32)
    init = jnp.concatenate([memory_init, jnp.zeros((pad, width), BF16)], axis=0)

    results = run_layers(tokens[0], cotangent[0], w_proj[0], w_down, vectors[0], init, fresh, key_bits, query_bits)
    block_rows, input_rows, grad_memory, grad_vec = results[:4]
    x_in, q, k_rows, v, o, n1, y1, n2, h, slope, p, df, db, dq, dk, dv, da = results[4:21]

    vec_pair = grad_vec[:4]
    nothing = jnp.zeros_like(vec_pair)
    small = jnp.concatenate([jnp.where(first, vec_pair, nothing), jnp.where(first, nothing, vec_pair), grad_memory],
                            axis=0)
    blocks = hidden // width
    half = w_down.shape[0] // width
    subs, piece, total = ring_layout(data_count, (blocks + half) * width)
    stack = weight_grads([h], [df], blocks, True, lambda t: (t // half, blocks + t % half), total, None, "grad_down")
    stack = weight_grads([y1], [da], blocks, False, lambda t: (1, t), total, stack, "grad_up")
    stack = weight_grads([x_in] * 3 + [o], [dq, dk, dv, db], blocks, False, lambda t: (0, t), total, stack, "grad_attn")
    summed, small = ring_sum(stack, small, data_count, lax.axis_size("section"), subs, piece)
    total_vec = lax.dynamic_slice(small, (2 * section, 0), (2, width))[None]
    share = width // 4
    memory_total = lax.dynamic_slice(small, (8, section * share), (memory_count, share))
    total_proj = widen(summed, blocks, 0, True)
    total_down = widen(summed, half, blocks, False)
    return (block_rows[None], input_rows[None], total_proj[None], total_vec, total_down, memory_total)


def solution(mesh):
    items = P(("section", "dp"), None, None, None)
    return jax.shard_map(
        body,
        mesh=mesh,
        in_specs=(items, P(), P(), P(), P("section", None, None), P("section", None, None),
                  P("section", None), items),
        out_specs=(items, items, P("section", None, None), P("section", None, None),
                   P("section", None), P(None, "section")),
        check_vma=False,
    )
```

```python
import functools

import jax
import jax.numpy as jnp
from jax import lax
from jax.experimental import pallas as pl
from jax.experimental.pallas import tpu as pltpu
from jax.sharding import PartitionSpec as P

HEADS = 12
DOCS = 4
NORM_EPSILON = 1e-06
NEGATIVE = -1e30
BF16 = jnp.bfloat16
F32 = jnp.float32
VMEM_BYTES = 60 * 2**20
GROUP = 4
FF_BLOCK = 1024
TILE = 16
MICROS = 4
MESH = pl.DeviceIdType.MESH


def mm(left, right, ca=1, cb=0):
    return lax.dot_general(
        left, right, (((ca,), (cb,)), ((), ())), preferred_element_type=F32
    )


def shape_of(shape, dtype=BF16):
    return jax.ShapeDtypeStruct(shape, dtype)


def anywhere():
    return pl.BlockSpec(memory_space=pl.ANY)


def on_chip():
    return pl.BlockSpec(memory_space=pltpu.VMEM)


def head_rows(block, group, head):
    lane = lax.broadcasted_iota(jnp.int32, (1, block.shape[1]), 1) // head
    return jnp.concatenate([jnp.where(lane == h, block, jnp.zeros_like(block)) for h in range(group)], axis=0)


def head_fold(stacked, group, head):
    total, width = stacked.shape
    rows = total // group
    lane = lax.broadcasted_iota(jnp.int32, (1, width), 1) // head
    out = stacked[:rows]
    for h in range(1, group):
        out = jnp.where(lane == h, stacked[h * rows:(h + 1) * rows], out)
    return out


def normalise(summed):
    center = summed - jnp.mean(summed, axis=-1, keepdims=True)
    variance = jnp.mean(center * center, axis=-1, keepdims=True)
    inverse = lax.rsqrt(variance + NORM_EPSILON)
    return center * inverse, inverse


def norm_back(g, n, inverse, gain):
    u = g * gain
    dz = inverse * (u - jnp.mean(u, axis=-1, keepdims=True) - n * jnp.mean(u * n, axis=-1, keepdims=True))
    return dz, jnp.sum(g * n, axis=0, keepdims=True), jnp.sum(g, axis=0, keepdims=True)


def layers_kernel(tokens_ref, cot_ref, proj_ref, down_ref, vec_ref, init_ref, fresh_ref, key_ref, query_ref,
                  out_ref, gtok_ref, gmem_ref, gvec_ref,
                  xs, qs, ks, vs, os_, n1s, y1s, n2s, hs, ss, ps, dfs, dbs, dqs, dks, dvs, das,
                  hop_ref, back_ref, tok_other, cot_other,
                  wa, w1, w2, vecs, x, q, k, v, o, n1, y1, n2, df, db, do, acc, y, hb, sb, pb, r1, r2,
                  mem_in, mem_grad,
                  share_local, share_send, share_recv, tok_send, tok_recv, cot_send, cot_recv,
                  hop_send, hop_recv, back_send, back_recv, mem_send, mem_recv, mg_send, mg_recv,
                  out_sem, out_send, out_recv, gt_sem, gt_send, gt_recv,
                  load_sem, save_sem, h_sem, s_sem, p_sem):
    section = lax.axis_index("section")
    stage = section // 2
    core = lax.rem(section, 2)
    first = stage == 0
    second = stage == 1
    mate = {"section": section + 1 - 2 * core}
    across = {"section": section + 2 - 4 * stage}
    segments, tokens, width = tokens_ref.shape
    rows = x.shape[0]
    hidden = proj_ref.shape[1]
    head = width // HEADS
    cols = GROUP * head
    groups = HEADS // GROUP
    blocks = hidden // FF_BLOCK
    halfd = down_ref.shape[0]
    micros = 2 * segments
    scale = head ** (-0.5)
    body_rows = pl.ds(0, tokens)
    last_rows = pl.ds(tokens, rows - tokens)

    def remote(source, target, send, recv, device):
        return pltpu.make_async_remote_copy(src_ref=source, dst_ref=target, send_sem=send, recv_sem=recv,
                                            device_id=device, device_id_type=MESH)

    local = pltpu.make_async_copy

    barrier = pltpu.get_barrier_semaphore()
    pl.semaphore_signal(barrier, inc=1, device_id=mate, device_id_type=MESH)
    pl.semaphore_signal(barrier, inc=1, device_id=across, device_id_type=MESH)
    pl.semaphore_wait(barrier, 2)

    down_rows = pl.ds(pl.multiple_of(core * halfd, 16), halfd)
    other_rows = pl.ds(pl.multiple_of((1 - core) * halfd, 16), halfd)
    down_away = remote(down_ref, w2.at[down_rows], share_send.at[1], share_recv.at[1], mate)
    vec_away = remote(vec_ref, vecs.at[core], share_send.at[2], share_recv.at[2], mate)
    proj_a = remote(proj_ref, wa, share_send.at[0], share_recv.at[0], mate)
    proj_b = remote(proj_ref, w1, share_send.at[0], share_recv.at[0], mate)
    proj_here_a = local(proj_ref, wa, share_local.at[0])
    proj_here_b = local(proj_ref, w1, share_local.at[0])
    down_here = local(down_ref, w2.at[down_rows], share_local.at[1])
    vec_here = local(vec_ref, vecs.at[core], share_local.at[2])

    @pl.when(core == 0)
    def _():
        proj_a.start()
        proj_here_a.start()

    @pl.when(core == 1)
    def _():
        proj_b.start()
        proj_here_b.start()

    vec_away.start()
    vec_here.start()
    down_away.start()
    down_here.start()

    def tok_copy(k_):
        return remote(tokens_ref.at[k_], tok_other.at[k_], tok_send.at[k_], tok_recv.at[k_], across)

    def cot_copy(k_):
        return remote(cot_ref.at[k_], cot_other.at[k_], cot_send.at[k_], cot_recv.at[k_], across)

    @pl.when(second)
    def _():
        for k_ in range(segments):
            tok_copy(k_).start()

    @pl.when(first)
    def _():
        cot_copy(segments - 1).start()

    vec_here.wait()
    vec_away.wait_recv()

    @pl.when(core == 0)
    def _():
        proj_here_a.wait()

    @pl.when(core == 1)
    def _():
        proj_a.wait_recv()

    def hop_copy(m):
        return remote(y.at[lax.rem(m, 2)], hop_ref.at[m], hop_send.at[m], hop_recv.at[m], across)

    def mem_copy(m):
        return remote(y.at[lax.rem(m, 2), last_rows], mem_in.at[m], mem_send.at[m], mem_recv.at[m], across)

    def out_here(m, seg):
        return local(y.at[lax.rem(m, 2), body_rows], out_ref.at[seg], out_sem.at[m])

    def out_away(m, seg):
        return remote(y.at[lax.rem(m, 2), body_rows], out_ref.at[seg], out_send.at[seg], out_recv.at[seg], across)

    kept = [(x, xs), (q, qs), (k, ks), (v, vs), (o, os_), (n1, n1s), (y1, y1s), (n2, n2s)]

    def saves(m):
        return [local(here, there.at[m], save_sem.at[i]) for i, (here, there) in enumerate(kept)]

    def band(g):
        return pl.ds(pl.multiple_of(g * cols, cols), cols)

    def h_save(m, j):
        b = lax.rem(j, 2)
        return local(hb.at[b], hs.at[m, :, pl.ds(pl.multiple_of(j * FF_BLOCK, FF_BLOCK), FF_BLOCK)], h_sem.at[b])

    def s_save(m, j):
        b = lax.rem(j, 2)
        return local(sb.at[b], ss.at[m, :, pl.ds(pl.multiple_of(j * FF_BLOCK, FF_BLOCK), FF_BLOCK)], s_sem.at[b])

    def p_save(m, g):
        b = lax.rem(g, 2)
        return local(pb.at[b], ps.at[m, g], p_sem.at[b])

    def forward(m, carry):
        item = lax.rem(m, 2)
        seg = m // 2

        @pl.when(m > 0)
        def _():
            for save in saves(m - 1):
                save.wait()

        body_load = [local(source.at[seg], x.at[body_rows], load_sem.at[0]) for source in (tokens_ref, tok_other)]
        whole_load = local(hop_ref.at[m], x, load_sem.at[0])

        @pl.when(first)
        def _():
            @pl.when(item == 0)
            def _():
                body_load[0].start()

            @pl.when(item == 1)
            def _():
                tok_copy(seg).wait_recv()
                body_load[1].start()

            @pl.when(seg == 0)
            def _():
                x[last_rows, :] = init_ref[...]

            @pl.when(seg > 0)
            def _():
                mem_copy(m - 2).wait_recv()
                x[last_rows, :] = jnp.where(fresh_ref[item] > 0, init_ref[...], mem_in[m - 2])

            body_load[0].wait()

        @pl.when(second)
        def _():
            hop_copy(m).wait_recv()
            whole_load.start()
            whole_load.wait()

        out = saves(m)
        out[0].start()

        def attend(g, carry2):
            here = band(g)
            xv = x[...]
            q[:, here] = mm(xv, wa[:, here]).astype(BF16)
            k[:, here] = mm(xv, wa[:, pl.ds(pl.multiple_of(width + g * cols, cols), cols)]).astype(BF16)
            v[:, here] = mm(xv, wa[:, pl.ds(pl.multiple_of(2 * width + g * cols, cols), cols)]).astype(BF16)

            @pl.when(g >= 2)
            def _():
                p_save(m, g - 2).wait()

            s = mm(k[:, here], head_rows(q[:, here] * scale, GROUP, head), 1, 1)
            seen = (key_ref[m, :, 0:1] & query_ref[m]) != 0
            s = jnp.where(seen, s, NEGATIVE)
            e = jnp.exp(s - jnp.max(s, axis=0, keepdims=True))
            p = (e * (1.0 / jnp.sum(e, axis=0, keepdims=True))).astype(BF16)
            pb[lax.rem(g, 2)] = p
            p_save(m, g).start()
            o[:, here] = head_fold(mm(p, v[:, here], 0, 0), GROUP, head).astype(BF16)
            return carry2

        lax.fori_loop(0, groups, attend, 0)
        for i in (1, 2, 3, 4):
            out[i].start()
        normed, inverse = normalise(x[...].astype(F32) + mm(o[...], wa[:, pl.ds(3 * width, width)]))
        n1[...] = normed.astype(BF16)
        r1[m] = jnp.broadcast_to(inverse, r1.shape[1:])
        y1v = (normed * vecs[0, 0:1, :] + vecs[0, 1:2, :]).astype(BF16)
        y1[...] = y1v
        acc[...] = y1v.astype(F32)
        out[5].start()
        out[6].start()
        p_save(m, groups - 2).wait()
        p_save(m, groups - 1).wait()

        @pl.when(m == 0)
        def _():
            @pl.when(core == 0)
            def _():
                proj_b.wait_recv()

            @pl.when(core == 1)
            def _():
                proj_here_b.wait()

            down_here.wait()
            remote(down_ref, w2.at[other_rows], share_send.at[1], share_recv.at[1], mate).wait_recv()

        def feed(j, carry2):
            b = lax.rem(j, 2)

            @pl.when(j >= 2)
            def _():
                h_save(m, j - 2).wait()
                s_save(m, j - 2).wait()

            half = FF_BLOCK // 2
            yv = y1[...]
            pre = [mm(yv, w1[:, pl.ds(pl.multiple_of(j * FF_BLOCK + i * half, half), half)]) for i in range(2)]
            for i in range(2):
                a = pre[i]
                gate = 0.5 * (1.0 + lax.erf(a * 0.7071067811865476))
                hb[b, :, i * half:(i + 1) * half] = (a * gate).astype(BF16)
                sb[b, :, i * half:(i + 1) * half] = (
                    gate + a * jnp.exp(-0.5 * a * a) * 0.3989422804014327).astype(BF16)
            h_save(m, j).start()
            s_save(m, j).start()
            acc[...] += mm(hb[b], w2[pl.ds(pl.multiple_of(j * FF_BLOCK, FF_BLOCK), FF_BLOCK), :])
            return carry2

        lax.fori_loop(0, blocks, feed, 0)

        normed, inverse = normalise(acc[...])
        n2[...] = normed.astype(BF16)
        r2[m] = jnp.broadcast_to(inverse, r2.shape[1:])

        @pl.when(m >= 2)
        def _():
            @pl.when(first)
            def _():
                hop_copy(m - 2).wait_send()

            @pl.when(second)
            def _():
                mem_copy(m - 2).wait_send()

                @pl.when(item == 0)
                def _():
                    out_away(m - 2, seg - 1).wait_send()

                @pl.when(item == 1)
                def _():
                    out_here(m - 2, seg - 1).wait()

        y[item] = (normed * vecs[1, 0:1, :] + vecs[1, 1:2, :]).astype(BF16)
        out[7].start()

        @pl.when(first)
        def _():
            hop_copy(m).start()

        @pl.when(second)
        def _():
            @pl.when(seg + 1 < segments)
            def _():
                mem_copy(m).start()

            @pl.when(item == 0)
            def _():
                out_away(m, seg).start()

            @pl.when(item == 1)
            def _():
                out_here(m, seg).start()

        for j in range(max(0, blocks - 2), blocks):
            h_save(m, j).wait()
            s_save(m, j).wait()
        return carry

    lax.fori_loop(0, micros, forward, 0)
    for save in saves(micros - 1):
        save.wait()

    @pl.when(first)
    def _():
        for k_ in reversed(range(segments - 1)):
            cot_copy(k_).start()
        for m in range(micros - 2, micros):
            hop_copy(m).wait_send()
        for k_ in range(segments):
            out_away(0, k_).wait_recv()

    @pl.when(second)
    def _():
        out_away(micros - 2, segments - 1).wait_send()
        out_here(micros - 1, segments - 1).wait()

    gmem_ref[...] = jnp.zeros(gmem_ref.shape, F32)
    gvec_ref[...] = jnp.zeros(gvec_ref.shape, F32)

    def back_copy(t):
        return remote(y.at[lax.rem(t, 2)], back_ref.at[t], back_send.at[t], back_recv.at[t], across)

    def mg_copy(t):
        return remote(y.at[lax.rem(t, 2), last_rows], mem_grad.at[t], mg_send.at[t], mg_recv.at[t], across)

    def gt_here(t, seg):
        return local(y.at[lax.rem(t, 2), body_rows], gtok_ref.at[seg], gt_sem.at[t])

    def gt_away(t, seg):
        return remote(y.at[lax.rem(t, 2), body_rows], gtok_ref.at[seg], gt_send.at[seg], gt_recv.at[seg], across)

    def s_load(m, j):
        b = lax.rem(j, 2)
        return local(ss.at[m, :, pl.ds(pl.multiple_of(j * FF_BLOCK, FF_BLOCK), FF_BLOCK)], sb.at[b], s_sem.at[b])

    def d_save(m, j):
        b = lax.rem(j, 2)
        return local(hb.at[b], das.at[m, :, pl.ds(pl.multiple_of(j * FF_BLOCK, FF_BLOCK), FF_BLOCK)], h_sem.at[b])

    def p_load(m, g):
        b = lax.rem(g, 2)
        return local(ps.at[m, g], pb.at[b], p_sem.at[b])

    def back_saves(m):
        pairs = [(df, dfs), (db, dbs), (x, dqs), (o, dks), (y1, dvs)]
        return [local(here, there.at[m], save_sem.at[i]) for i, (here, there) in enumerate(pairs)]

    def backward(t, carry):
        item = lax.rem(t, 2)
        seg = segments - 1 - t // 2
        m = 2 * seg + item
        before = 2 * (segments - 1 - (t - 1) // 2) + lax.rem(t - 1 + 2, 2)

        @pl.when(t > 0)
        def _():
            for save in back_saves(before):
                save.wait()

        loads = [local(source.at[m], here, load_sem.at[1 + i])
                 for i, (source, here) in enumerate([(n2s, n2), (qs, q), (ks, k), (vs, v), (n1s, n1)])]
        body_load = [local(source.at[seg], y1.at[body_rows], load_sem.at[0]) for source in (cot_ref, cot_other)]
        whole_load = local(back_ref.at[t], y1, load_sem.at[0])
        for load in loads:
            load.start()
        s_load(m, 0).start()
        s_load(m, 1).start()
        p_load(m, 0).start()
        p_load(m, 1).start()

        @pl.when(second)
        def _():
            @pl.when(item == 1)
            def _():
                body_load[0].start()

            @pl.when(item == 0)
            def _():
                cot_copy(seg).wait_recv()
                body_load[1].start()

            @pl.when(seg + 1 == segments)
            def _():
                y1[last_rows, :] = jnp.zeros((rows - tokens, width), BF16)

            @pl.when(seg + 1 < segments)
            def _():
                mg_copy(t - 2).wait_recv()
                got = mem_grad[t - 2]
                y1[last_rows, :] = jnp.where(fresh_ref[item] > 0, jnp.zeros_like(got), got)

            body_load[0].wait()

        @pl.when(first)
        def _():
            back_copy(t).wait_recv()
            whole_load.start()
            whole_load.wait()

        loads[0].wait()
        dz, gain_grad, bias_grad = norm_back(y1[...].astype(F32), n2[...].astype(F32), r2[m, :, 0:1], vecs[1, 0:1, :])
        gvec_ref[2:3, :] += gain_grad
        gvec_ref[3:4, :] += bias_grad
        df[...] = dz.astype(BF16)
        acc[...] = dz
        out = back_saves(m)
        out[0].start()

        def feed(j, carry2):
            b = lax.rem(j, 2)

            @pl.when(j >= 2)
            def _():
                d_save(m, j - 2).wait()

            s_load(m, j).wait()
            half = FF_BLOCK // 2
            dfv = df[...]
            dh = [mm(dfv, w2[pl.ds(pl.multiple_of(j * FF_BLOCK + i * half, half), half), :], 1, 1) for i in range(2)]
            for i in range(2):
                cut = slice(i * half, (i + 1) * half)
                hb[b, :, cut] = (dh[i] * sb[b, :, cut].astype(F32)).astype(BF16)
            d_save(m, j).start()

            @pl.when(j + 2 < blocks)
            def _():
                s_load(m, j + 2).start()

            acc[...] += mm(hb[b], w1[:, pl.ds(pl.multiple_of(j * FF_BLOCK, FF_BLOCK), FF_BLOCK)], 1, 1)
            return carry2

        lax.fori_loop(0, blocks, feed, 0)
        for load in loads[1:]:
            load.wait()
        dz, gain_grad, bias_grad = norm_back(acc[...].astype(BF16).astype(F32), n1[...].astype(F32), r1[m, :, 0:1],
                                             vecs[0, 0:1, :])
        gvec_ref[0:1, :] += gain_grad
        gvec_ref[1:2, :] += bias_grad
        db[...] = dz.astype(BF16)
        acc[...] = dz
        out[1].start()

        def attend(g, carry2):
            here = band(g)
            b = lax.rem(g, 2)
            p_load(m, g).wait()
            gv = mm(db[...], wa[here, pl.ds(3 * width, width)], 1, 1).astype(BF16)
            grads = head_rows(gv, GROUP, head)
            dp = mm(v[:, here], grads, 1, 1)
            p = pb[b]
            weight = p.astype(F32)
            ds = (weight * (dp - jnp.sum(weight * dp, axis=0, keepdims=True))).astype(BF16)
            dv = mm(p, grads).astype(BF16)
            dk = mm(ds, head_rows(q[:, here] * scale, GROUP, head)).astype(BF16)
            dq = (head_fold(mm(ds, k[:, here], 0, 0), GROUP, head) * scale).astype(BF16)

            @pl.when(g + 2 < groups)
            def _():
                p_load(m, g + 2).start()

            x[:, here] = dq
            o[:, here] = dk
            y1[:, here] = dv
            acc[...] += (mm(dq, wa[:, here], 1, 1)
                         + mm(dk, wa[:, pl.ds(pl.multiple_of(width + g * cols, cols), cols)], 1, 1)
                         + mm(dv, wa[:, pl.ds(pl.multiple_of(2 * width + g * cols, cols), cols)], 1, 1))
            return carry2

        lax.fori_loop(0, groups, attend, 0)
        for i in (2, 3, 4):
            out[i].start()

        @pl.when(t >= 2)
        def _():
            @pl.when(second)
            def _():
                back_copy(t - 2).wait_send()

            @pl.when(first)
            def _():
                mg_copy(t - 2).wait_send()

                @pl.when(item == 1)
                def _():
                    gt_away(t - 2, seg + 1).wait_send()

                @pl.when(item == 0)
                def _():
                    gt_here(t - 2, seg + 1).wait()

        dx = acc[...].astype(BF16)
        y[item] = dx

        @pl.when(second)
        def _():
            back_copy(t).start()

        @pl.when(first)
        def _():
            tail = dx[tokens:, :].astype(F32)

            @pl.when(seg > 0)
            def _():
                mg_copy(t).start()
                gmem_ref[...] += jnp.where(fresh_ref[item] > 0, tail, 0.0)

            @pl.when(seg == 0)
            def _():
                gmem_ref[...] += tail

            @pl.when(item == 0)
            def _():
                gt_here(t, seg).start()

            @pl.when(item == 1)
            def _():
                gt_away(t, seg).start()

        for j in range(max(0, blocks - 2), blocks):
            d_save(m, j).wait()
        return carry

    lax.fori_loop(0, micros, backward, 0)
    for save in back_saves(1):
        save.wait()

    @pl.when(second)
    def _():
        for t in range(micros - 2, micros):
            back_copy(t).wait_send()
        for k_ in range(segments):
            tok_copy(k_).wait_send()
            gt_away(1, k_).wait_recv()

    @pl.when(first)
    def _():
        gt_here(micros - 2, 0).wait()
        gt_away(micros - 1, 0).wait_send()
        for k_ in range(segments):
            cot_copy(k_).wait_send()

    proj_a.wait_send()
    down_away.wait_send()
    vec_away.wait_send()


def run_layers(tokens, cotangent, proj, down, vec, init, fresh, key_bits, query_bits):
    segments, seg_tokens, width = tokens.shape
    rows = seg_tokens + TILE
    hidden = proj.shape[1]
    micros = 2 * segments
    groups = HEADS // GROUP
    span = GROUP * rows
    stack = shape_of((micros, rows, width))
    wide = shape_of((micros, rows, hidden))
    low = pltpu.VMEM((rows, width), BF16)
    dma = pltpu.SemaphoreType.DMA
    pair = pltpu.VMEM((2, rows, FF_BLOCK), BF16)
    inverse = pltpu.VMEM((micros, rows, 128), F32)
    tails = pltpu.VMEM((2, TILE, width), BF16)
    return pl.pallas_call(
        layers_kernel,
        in_specs=[anywhere()] * 4 + [on_chip()] * 5,
        out_specs=[anywhere()] * 2 + [on_chip()] * 2 + [anywhere()] * 21,
        out_shape=[shape_of(tokens.shape), shape_of(tokens.shape), shape_of((TILE, width), F32),
                   shape_of((8, width), F32)]
        + [stack] * 8 + [wide] * 2 + [shape_of((micros, groups, rows, span))] + [stack] * 5 + [wide]
        + [stack] * 2 + [shape_of(tokens.shape)] * 2,
        scratch_shapes=[
            pltpu.VMEM((width, hidden), BF16), pltpu.VMEM((width, hidden), BF16), pltpu.VMEM((hidden, width), BF16),
            pltpu.VMEM((2, 2, width), F32)] + [low] * 11 + [
            pltpu.VMEM((rows, width), F32), pltpu.VMEM((2, rows, width), BF16), pair, pair,
            pltpu.VMEM((2, rows, span), BF16), inverse, inverse, tails, tails,
            dma((3,)), dma((3,)), dma((3,)), dma((segments,)), dma((segments,)), dma((segments,)), dma((segments,)),
            dma((micros,)), dma((micros,)), dma((micros,)), dma((micros,)), dma((2,)), dma((2,)), dma((2,)), dma((2,)),
            dma((micros,)), dma((segments,)), dma((segments,)), dma((micros,)), dma((segments,)), dma((segments,)),
            dma((6,)), dma((8,)), dma((2,)), dma((2,)), dma((2,))],
        compiler_params=pltpu.CompilerParams(vmem_limit_bytes=VMEM_BYTES, collective_id=1, has_side_effects=True),
        name="layers",
    )(tokens, cotangent, proj, down, vec, init, fresh, key_bits, query_bits)


def flipped(index, bit):
    return index + bit - 2 * bit * lax.rem(index // bit, 2)


def ring_piece(n, width):
    piece = -(-width // (2 * n))
    return piece + -piece % 16


def grads_kernel(xs, os_, y1s, hs, dqs, dks, dvs, dbs, das, dfs, small_ref, out_ref, small_out,
                 lbuf, rbuf, mine, got, away, final, slots, held, arrived,
                 left_sem, right_sem, swap_send, swap_recv, sum_send, sum_recv, full_send, full_recv,
                 small_send, small_recv, store_sem, *, n, piece, hops, ups, halves):
    section = lax.axis_index("section")
    data = lax.axis_index("dp")
    core = lax.rem(section, 2)
    mate = {"section": section + 1 - 2 * core}
    width = final.shape[2]
    tiles = ups + halves
    half = n // 2
    micros, rows = lbuf.shape[1:3]

    def place(p):
        p = lax.rem(p + 2 * n, n)
        return jnp.where(p < half, 2 * p, 2 * (n - 1 - p) + 1)

    me = jnp.where(lax.rem(data, 2) == 0, data // 2, n - 1 - data // 2)
    peers = ({"dp": place(me + 1)}, {"dp": place(me - 1)})
    signs = (1, -1)

    def remote(source, target, send, recv, device):
        return pltpu.make_async_remote_copy(src_ref=source, dst_ref=target, send_sem=send, recv_sem=recv,
                                            device_id=device, device_id_type=MESH)

    def part(ref, column):
        return ref.at[:, :, pl.ds(column * width, width)]

    attn = [(xs, dqs), (xs, dks), (xs, dvs), (os_, dbs)] + [(part(hs, i), dfs) for i in range(halves)]
    feed = [(y1s, part(das, i)) for i in range(ups)] + [(part(hs, halves + i), dfs) for i in range(halves)]

    def loads(t, which):
        b = t % 2
        left, right = (attn, feed)[which][t // 2]
        return (pltpu.make_async_copy(left, lbuf.at[b], left_sem.at[b]),
                pltpu.make_async_copy(right, rbuf.at[b], right_sem.at[b]))

    def start_load(t):
        turn = core if t % 2 else 1 - core
        for which in (0, 1):
            @pl.when(turn == which)
            def _():
                for copy in loads(t, which):
                    copy.start()

    start_load(0)
    barrier = pltpu.get_barrier_semaphore()
    friends = [{axis: flipped(section if axis == "section" else data, bit)} for axis, bit in hops]
    for device in [mate, *peers, *friends]:
        pl.semaphore_signal(barrier, inc=1, device_id=device, device_id_type=MESH)
    pl.semaphore_wait(barrier, 3 + len(friends))

    held[0] = small_ref[...]

    def small_copy(i):
        return remote(held.at[i], arrived.at[i], small_send.at[i], small_recv.at[i], friends[i])

    small_copy(0).start()

    def finish_small(i):
        small_copy(i).wait_recv()
        total = held[i] + arrived[i]
        if i + 1 < len(friends):
            held[i + 1] = total
            small_copy(i + 1).start()
        else:
            small_out[...] = total

    def swap(j):
        return remote(away.at[lax.rem(j, 2)], got.at[j, pl.ds(0, width)], swap_send.at[j], swap_recv.at[j], mate)

    def piece_rows(index, d):
        return pl.ds(pl.multiple_of((lax.rem(index + 2 * n, n) * 2 + d) * piece, 16), piece)

    def sum_copy(i, d, s):
        where = mine.at[i, piece_rows(me - signs[d] * s, d)]
        return remote(where, slots.at[i, d, s], sum_send.at[i, d, s], sum_recv.at[i, d, s], peers[d])

    def full_copy(i, d, s):
        where = final.at[i, piece_rows(me + signs[d] * (1 - s), d)]
        return remote(where, where, full_send.at[i, d, s], full_recv.at[i, d, s], peers[d])

    def store(i):
        return pltpu.make_async_copy(final.at[i], out_ref.at[i], store_sem.at[i])

    def serve(i, s):
        @pl.when(s == 0)
        def _():
            swap(i).wait_recv()

        @pl.when((s >= 0) & (s < n))
        def _():
            for d in (0, 1):
                here = piece_rows(me - signs[d] * s, d)
                value = mine[i, here, :].astype(F32) + got[i, here, :].astype(F32)

                @pl.when(s == 0)
                def _():
                    mine[i, here, :] = value.astype(BF16)
                    sum_copy(i, d, s).start()

                @pl.when(s > 0)
                def _():
                    sum_copy(i, d, s - 1).wait_recv()
                    total = (value + slots[i, d, s - 1].astype(F32)).astype(BF16)

                    @pl.when(s < n - 1)
                    def _():
                        mine[i, here, :] = total
                        sum_copy(i, d, s).start()

                    @pl.when(s == n - 1)
                    def _():
                        final[i, here, :] = total
                        full_copy(i, d, 0).start()

        @pl.when((s >= n) & (s < 2 * n - 1))
        def _():
            f = s - n + 1
            for d in (0, 1):
                full_copy(i, d, f - 1).wait_recv()

                @pl.when(f < n - 1)
                def _():
                    full_copy(i, d, f).start()

            @pl.when(f == n - 1)
            def _():
                store(i).start()

    for t in range(2 * tiles):
        if t + 1 < 2 * tiles:
            start_load(t + 1)
        b, j = t % 2, t // 2
        for copy in loads(t, 0):
            copy.wait()
        tile = mm(lbuf[b].reshape(micros * rows, width), rbuf[b].reshape(micros * rows, width), 0, 0).astype(BF16)
        if t % 2 == 0:
            if j >= 2:
                swap(j - 2).wait_send()
            away[j % 2] = tile
            swap(j).start()
        else:
            mine[j, 0:width, :] = tile
        for i in range(tiles):
            if t - 2 * i - 1 >= 0:
                serve(i, jnp.int32(t - 2 * i - 1))

    begin = 2 * tiles

    def rest(t, carry):
        for k in range(len(friends)):
            @pl.when(t == begin + k)
            def _():
                finish_small(k)

        def one(i, carry2):
            serve(i, t - 2 * i - 1)
            return carry2

        lax.fori_loop(0, tiles, one, 0)
        return carry

    lax.fori_loop(begin, 2 * tiles - 1 + 2 * n - 1, rest, 0)

    def finish(i, carry):
        def sends(s, carry2):
            for d in (0, 1):
                sum_copy(i, d, s).wait_send()
                full_copy(i, d, s).wait_send()
            return carry2

        lax.fori_loop(0, n - 1, sends, 0)
        store(i).wait()
        return carry

    lax.fori_loop(0, tiles, finish, 0)
    for j in range(tiles - 2, tiles):
        swap(j).wait_send()
    for i in range(len(friends)):
        small_copy(i).wait_send()


def weight_gradients(stacks, small, n, sections, width, ups, halves):
    piece = ring_piece(n, width)
    total = 2 * n * piece
    micros, rows = stacks[0].shape[:2]
    tiles = ups + halves
    hops = [("dp", 1 << i) for i in range(n.bit_length() - 1)]
    hops += [("section", 1 << i) for i in range(sections.bit_length() - 1)]
    dma = pltpu.SemaphoreType.DMA
    kept = pltpu.VMEM((tiles, total, width), BF16)
    operand = pltpu.VMEM((2, micros, rows, width), BF16)
    sums = pltpu.VMEM((len(hops),) + small.shape, F32)
    return pl.pallas_call(
        functools.partial(grads_kernel, n=n, piece=piece, hops=hops, ups=ups, halves=halves),
        in_specs=[anywhere()] * len(stacks) + [on_chip()],
        out_specs=[anywhere(), on_chip()],
        out_shape=[shape_of((tiles, total, width)), shape_of(small.shape, F32)],
        scratch_shapes=[
            operand, operand, kept, kept, pltpu.VMEM((2, width, width), BF16), kept,
            pltpu.VMEM((tiles, 2, n - 1, piece, width), BF16), sums, sums,
            dma((2,)), dma((2,)), dma((tiles,)), dma((tiles,)),
            dma((tiles, 2, n - 1)), dma((tiles, 2, n - 1)), dma((tiles, 2, n - 1)), dma((tiles, 2, n - 1)),
            dma((len(hops),)), dma((len(hops),)), dma((tiles,))],
        compiler_params=pltpu.CompilerParams(vmem_limit_bytes=VMEM_BYTES, collective_id=0, has_side_effects=True),
        name="weight_gradients",
    )(*stacks, small)


def widen_kernel(in_ref, out_ref):
    out_ref[...] = in_ref[...].astype(F32)


def widen(data, blocks, offset, by_column):
    width = data.shape[2]
    if by_column:
        shape, spec = (width, blocks * width), pl.BlockSpec((width, width), lambda b: (0, b))
    else:
        shape, spec = (blocks * width, width), pl.BlockSpec((width, width), lambda b: (b, 0))
    return pl.pallas_call(
        widen_kernel, grid=(blocks,),
        in_specs=[pl.BlockSpec((None, width, width), lambda b: (offset + b, 0, 0))],
        out_specs=spec, out_shape=shape_of(shape, F32),
        compiler_params=pltpu.CompilerParams(vmem_limit_bytes=VMEM_BYTES), name="widen",
    )(data)


def body(tokens, doc_ids, reset_flags, memory_init, w_proj, vectors, w_down, cotangent):
    data_count = lax.axis_size("dp")
    section = lax.axis_index("section")
    data = lax.axis_index("dp")
    first = section < 2
    core = section % 2
    _, segments, seg_tokens, width = tokens.shape
    memory_count = memory_init.shape[0]
    hidden = w_proj.shape[2]
    pad = TILE - memory_count
    items = (core * data_count + data, (core + 2) * data_count + data)
    micros = [(item, k) for k in range(segments) for item in (0, 1)]
    flags = [lax.dynamic_index_in_dim(reset_flags, items[i], 0, keepdims=False) for i in (0, 1)]
    docs = jnp.stack([lax.dynamic_index_in_dim(doc_ids, items[item], 0, keepdims=False)[k] for item, k in micros])
    bits = jnp.left_shift(jnp.int32(1), docs)
    lines = jnp.ones((len(micros), 1), jnp.int32)
    every = (1 << DOCS) - 1
    key_bits = jnp.concatenate([bits, jnp.repeat(lines * every, memory_count, 1), jnp.repeat(lines * 0, pad, 1)], axis=1)
    query_bits = jnp.concatenate([bits, jnp.repeat(lines * every, TILE, 1)], axis=1)
    key_bits = jnp.broadcast_to(key_bits[:, :, None], key_bits.shape + (128,))
    query_bits = jnp.tile(query_bits, (1, GROUP))[:, None, :]
    fresh = jnp.stack([jnp.broadcast_to(flags[i][segments - 1], (TILE, width)) for i in (0, 1)]).astype(F32)
    init = jnp.concatenate([memory_init, jnp.zeros((pad, width), BF16)], axis=0)

    results = run_layers(tokens[0], cotangent[0], w_proj[0], w_down, vectors[0], init, fresh, key_bits, query_bits)
    block_rows, input_rows, grad_memory, grad_vec = results[:4]
    x_in, q, k_rows, v, o, n1, y1, n2, h, slope, p, df, db, dq, dk, dv, da = results[4:21]

    vec_pair = grad_vec[:4]
    nothing = jnp.zeros_like(vec_pair)
    small = jnp.concatenate([jnp.where(first, vec_pair, nothing), jnp.where(first, nothing, vec_pair), grad_memory],
                            axis=0)
    blocks = hidden // width
    half = w_down.shape[0] // width
    summed, small = weight_gradients([x_in, o, y1, h, dq, dk, dv, db, da, df], small, data_count,
                                     lax.axis_size("section"), width, blocks, half)
    total_vec = lax.dynamic_slice(small, (2 * section, 0), (2, width))[None]
    share = width // 4
    memory_total = lax.dynamic_slice(small, (8, section * share), (memory_count, share))
    total_proj = widen(summed, blocks, 0, True)
    total_down = widen(summed, half, blocks, False)
    return (block_rows[None], input_rows[None], total_proj[None], total_vec, total_down, memory_total)


def solution(mesh):
    items = P(("section", "dp"), None, None, None)
    return jax.shard_map(
        body,
        mesh=mesh,
        in_specs=(items, P(), P(), P(), P("section", None, None), P("section", None, None),
                  P("section", None), items),
        out_specs=(items, items, P("section", None, None), P("section", None, None),
                   P("section", None), P(None, "section")),
        check_vma=False,
    )
```

```python
import functools

import jax
import jax.numpy as jnp
from jax import lax
from jax.experimental import pallas as pl
from jax.experimental.pallas import tpu as pltpu
from jax.sharding import PartitionSpec as P

HEADS = 12
DOCS = 4
NORM_EPSILON = 1e-06
NEGATIVE = -1e30
BF16 = jnp.bfloat16
F32 = jnp.float32
VMEM_BYTES = 60 * 2**20
GROUP = 4
FF_BLOCK = 1536
TILE = 16
MESH = pl.DeviceIdType.MESH


def mm(left, right, ca=1, cb=0):
    return lax.dot_general(
        left, right, (((ca,), (cb,)), ((), ())), preferred_element_type=F32
    )


def shape_of(shape, dtype=BF16):
    return jax.ShapeDtypeStruct(shape, dtype)


def anywhere():
    return pl.BlockSpec(memory_space=pl.ANY)


def on_chip():
    return pl.BlockSpec(memory_space=pltpu.VMEM)


def head_rows(block, group, head):
    lane = lax.broadcasted_iota(jnp.int32, (1, block.shape[1]), 1) // head
    return jnp.concatenate([jnp.where(lane == h, block, jnp.zeros_like(block)) for h in range(group)], axis=0)


def head_fold(stacked, group, head):
    total, width = stacked.shape
    rows = total // group
    lane = lax.broadcasted_iota(jnp.int32, (1, width), 1) // head
    out = stacked[:rows]
    for h in range(1, group):
        out = jnp.where(lane == h, stacked[h * rows:(h + 1) * rows], out)
    return out


def normalise(summed):
    center = summed - jnp.mean(summed, axis=-1, keepdims=True)
    variance = jnp.mean(center * center, axis=-1, keepdims=True)
    inverse = lax.rsqrt(variance + NORM_EPSILON)
    return center * inverse, inverse


def norm_back(g, n, inverse, gain):
    u = g * gain
    dz = inverse * (u - jnp.mean(u, axis=-1, keepdims=True) - n * jnp.mean(u * n, axis=-1, keepdims=True))
    return dz, jnp.sum(g * n, axis=0, keepdims=True), jnp.sum(g, axis=0, keepdims=True)


def layers_kernel(tokens_ref, cot_ref, proj_ref, down_ref, docs_ref, vec_ref, memory_ref, flags_ref,
                  out_ref, gtok_ref, gmem_ref, gvec_ref,
                  xs, qs, ks, vs, os_, n1s, y1s, n2s, hs, ss, ps, dfs, dbs, dqs, dks, dvs, das,
                  cot_other,
                  wa, w1, w2, vecs, docs, key_ref, query_ref, init_ref, land, dq_ref, q, k, v, o, n1, y1, n2, df, db, do, acc, y, hb, sb, pb, r1, r2,
                  mem_in, mem_grad,
                  share_local, share_send, share_recv, tok_local, tok_send, tok_recv, cot_send, cot_recv,
                  hop_send, hop_recv, back_send, back_recv, mem_send, mem_recv, mg_send, mg_recv,
                  out_sem, out_send, out_recv, gt_sem, gt_send, gt_recv,
                  load_sem, save_sem, keep_sem, h_sem, s_sem, p_sem):
    section = lax.axis_index("section")
    stage = section // 2
    core = lax.rem(section, 2)
    first = stage == 0
    second = stage == 1
    mate = {"section": section + 1 - 2 * core}
    across = {"section": section + 2 - 4 * stage}
    segments, tokens, width = tokens_ref.shape
    rows = land.shape[1]
    memory = memory_ref.shape[0]
    data = lax.axis_index("dp")
    data_count = lax.axis_size("dp")
    owners = (core * data_count + data, (core + 2) * data_count + data)
    hidden = proj_ref.shape[1]
    head = width // HEADS
    cols = GROUP * head
    groups = HEADS // GROUP
    blocks = hidden // FF_BLOCK
    halfd = down_ref.shape[0]
    micros = 2 * segments
    scale = head ** (-0.5)
    body_rows = pl.ds(0, tokens)
    last_rows = pl.ds(tokens, rows - tokens)

    def remote(source, target, send, recv, device):
        return pltpu.make_async_remote_copy(src_ref=source, dst_ref=target, send_sem=send, recv_sem=recv,
                                            device_id=device, device_id_type=MESH)

    local = pltpu.make_async_copy

    barrier = pltpu.get_barrier_semaphore()
    pl.semaphore_signal(barrier, inc=1, device_id=mate, device_id_type=MESH)
    pl.semaphore_signal(barrier, inc=1, device_id=across, device_id_type=MESH)
    pl.semaphore_wait(barrier, 2)

    down_rows = pl.ds(pl.multiple_of(core * halfd, 16), halfd)
    other_rows = pl.ds(pl.multiple_of((1 - core) * halfd, 16), halfd)
    down_away = remote(down_ref, w2.at[down_rows], share_send.at[1], share_recv.at[1], mate)
    vec_away = remote(vec_ref, vecs.at[core], share_send.at[2], share_recv.at[2], mate)
    proj_a = remote(proj_ref, wa, share_send.at[0], share_recv.at[0], mate)
    proj_b = remote(proj_ref, w1, share_send.at[0], share_recv.at[0], mate)
    proj_here_a = local(proj_ref, wa, share_local.at[0])
    proj_here_b = local(proj_ref, w1, share_local.at[0])
    down_here = local(down_ref, w2.at[down_rows], share_local.at[1])
    vec_here = local(vec_ref, vecs.at[core], share_local.at[2])

    @pl.when(core == 0)
    def _():
        proj_a.start()
        proj_here_a.start()

    @pl.when(core == 1)
    def _():
        proj_b.start()
        proj_here_b.start()

    vec_away.start()
    vec_here.start()
    down_away.start()
    down_here.start()

    doc_loads = [local(docs_ref.at[owners[i]], docs.at[i], load_sem.at[i]) for i in (0, 1)]
    for load in doc_loads:
        load.start()

    def tok_here(k_):
        return local(tokens_ref.at[k_], land.at[2 * k_, body_rows], tok_local.at[k_])

    def tok_copy(k_):
        return remote(tokens_ref.at[k_], land.at[2 * k_ + 1, body_rows], tok_send.at[k_], tok_recv.at[k_], across)

    def cot_copy(k_):
        return remote(cot_ref.at[k_], cot_other.at[k_], cot_send.at[k_], cot_recv.at[k_], across)

    @pl.when(second)
    def _():
        for k_ in range(segments):
            tok_copy(k_).start()

    @pl.when(first)
    def _():
        for k_ in range(segments):
            tok_here(k_).start()
        cot_copy(segments - 1).start()

    init_ref[...] = jnp.concatenate([memory_ref[...], jnp.zeros((rows - tokens - memory, width), BF16)], axis=0)
    for load in doc_loads:
        load.wait()
    every = (1 << DOCS) - 1
    tail = lax.broadcasted_iota(jnp.int32, (rows - tokens, key_ref.shape[2]), 0)
    for m_ in range(micros):
        bits = jnp.left_shift(jnp.int32(1), docs[m_ % 2, m_ // 2:m_ // 2 + 1, :])
        row = jnp.concatenate([bits, jnp.full((1, rows - tokens), every, jnp.int32)], axis=1)
        query_ref[m_] = jnp.concatenate([row] * GROUP, axis=1)
        column = jnp.broadcast_to(bits.astype(F32), (8, tokens)).T[:, 0:1].astype(jnp.int32)
        key_ref[m_, body_rows, :] = jnp.broadcast_to(column, (tokens, key_ref.shape[2]))
        key_ref[m_, last_rows, :] = jnp.where(tail < memory, every, 0)

    def fresh(item):
        flag = jnp.where(item == 0, flags_ref[owners[0], segments - 1], flags_ref[owners[1], segments - 1])
        return jnp.full((rows - tokens, width), flag, jnp.int32) == 1

    vec_here.wait()
    vec_away.wait_recv()

    @pl.when(core == 0)
    def _():
        proj_here_a.wait()

    @pl.when(core == 1)
    def _():
        proj_a.wait_recv()
        remote(down_ref, w2.at[other_rows], share_send.at[1], share_recv.at[1], mate).wait_recv()

    def hop_copy(m):
        return remote(y.at[lax.rem(m, 2)], land.at[m], hop_send.at[m], hop_recv.at[m], across)

    def mem_copy(m):
        return remote(y.at[lax.rem(m, 2), last_rows], mem_in.at[m], mem_send.at[m], mem_recv.at[m], across)

    def out_here(m, seg):
        return local(y.at[lax.rem(m, 2), body_rows], out_ref.at[seg], out_sem.at[m])

    def out_away(m, seg):
        return remote(y.at[lax.rem(m, 2), body_rows], out_ref.at[seg], out_send.at[seg], out_recv.at[seg], across)

    kept = [(q, qs), (k, ks), (v, vs), (o, os_), (n1, n1s), (y1, y1s), (n2, n2s)]

    def keep(m):
        return local(land.at[m], xs.at[m], keep_sem.at[m])

    def grad_load(t, seg):
        source = cot_ref if t % 2 else cot_other
        return local(source.at[seg], land.at[t, body_rows], load_sem.at[6 + t])

    def saves(m):
        return [local(here, there.at[m], save_sem.at[i]) for i, (here, there) in enumerate(kept)]

    def band(g):
        return pl.ds(g * cols, cols)

    def h_save(m, j):
        b = lax.rem(j, 2)
        return local(hb.at[b], hs.at[m, :, pl.ds(pl.multiple_of(j * FF_BLOCK, FF_BLOCK), FF_BLOCK)], h_sem.at[b])

    def s_save(m, j):
        b = lax.rem(j, 2)
        return local(sb.at[b], ss.at[m, :, pl.ds(pl.multiple_of(j * FF_BLOCK, FF_BLOCK), FF_BLOCK)], s_sem.at[b])

    def p_save(m, g):
        return local(pb.at[g % 2], ps.at[m, g], p_sem.at[g % 2])

    def forward(m, carry):
        item = lax.rem(m, 2)
        seg = m // 2

        @pl.when(m > 0)
        def _():
            for save in saves(m - 1):
                save.wait()

        x = land.at[m]

        @pl.when(first)
        def _():
            @pl.when(item == 0)
            def _():
                tok_here(seg).wait()

            @pl.when(item == 1)
            def _():
                tok_copy(seg).wait_recv()

            @pl.when(seg == 0)
            def _():
                x[last_rows, :] = init_ref[...]

            @pl.when(seg > 0)
            def _():
                mem_copy(m - 2).wait_recv()
                x[last_rows, :] = jnp.where(fresh(item), init_ref[...], mem_in[m - 2])

        @pl.when(second)
        def _():
            hop_copy(m).wait_recv()

            @pl.when(m == micros - 1)
            def _():
                keep(0).wait()
                keep(1).wait()
                cot_copy(segments - 1).wait_recv()
                for t in (0, 1):
                    grad_load(t, segments - 1).start()

        keep(m).start()
        out = saves(m)

        def project(g):
            here = band(g)
            xv = x[...]
            q[:, here] = mm(xv, wa[:, here]).astype(BF16)
            k[:, here] = mm(xv, wa[:, pl.ds(width + g * cols, cols)]).astype(BF16)
            v[:, here] = mm(xv, wa[:, pl.ds(2 * width + g * cols, cols)]).astype(BF16)
            return mm(k[:, here], head_rows(q[:, here] * scale, GROUP, head), 1, 1)

        score = project(0)
        for g in range(groups):
            following = project(g + 1) if g + 1 < groups else None
            if g >= 2:
                p_save(m, g - 2).wait()
            else:
                @pl.when(m > 0)
                def _():
                    p_save(m - 1, groups - 1 - (groups - 1 - g) % 2).wait()
            s = jnp.where((key_ref[m, :, 0:1] & query_ref[m]) != 0, score, NEGATIVE)
            e = jnp.exp(s - jnp.max(s, axis=0, keepdims=True))
            p = (e * (1.0 / jnp.sum(e, axis=0, keepdims=True))).astype(BF16)
            pb[g % 2] = p
            p_save(m, g).start()
            o[:, band(g)] = head_fold(mm(p, v[:, band(g)], 0, 0), GROUP, head).astype(BF16)
            score = following
        for i in (0, 1, 2, 3):
            out[i].start()
        normed, inverse = normalise(x[...].astype(F32) + mm(o[...], wa[:, pl.ds(3 * width, width)]))
        n1[...] = normed.astype(BF16)
        r1[m] = jnp.broadcast_to(inverse, r1.shape[1:])
        y1v = (normed * vecs[0, 0:1, :] + vecs[0, 1:2, :]).astype(BF16)
        y1[...] = y1v
        acc[...] = y1v.astype(F32)
        out[4].start()
        out[5].start()

        @pl.when(m == 0)
        def _():
            @pl.when(core == 0)
            def _():
                proj_b.wait_recv()
                remote(down_ref, w2.at[other_rows], share_send.at[1], share_recv.at[1], mate).wait_recv()

            @pl.when(core == 1)
            def _():
                proj_here_b.wait()

            down_here.wait()

        def feed(j, carry2):
            b = lax.rem(j, 2)

            @pl.when(j >= 2)
            def _():
                h_save(m, j - 2).wait()
                s_save(m, j - 2).wait()

            half = FF_BLOCK // 2
            yv = y1[...]
            pre = [mm(yv, w1[:, pl.ds(pl.multiple_of(j * FF_BLOCK + i * half, half), half)]) for i in range(2)]
            for i in range(2):
                a = pre[i]
                gate = 0.5 * (1.0 + lax.erf(a * 0.7071067811865476))
                hb[b, :, i * half:(i + 1) * half] = (a * gate).astype(BF16)
                sb[b, :, i * half:(i + 1) * half] = (
                    gate + a * jnp.exp(-0.5 * a * a) * 0.3989422804014327).astype(BF16)
            h_save(m, j).start()
            s_save(m, j).start()
            acc[...] += mm(hb[b], w2[pl.ds(pl.multiple_of(j * FF_BLOCK, FF_BLOCK), FF_BLOCK), :])
            return carry2

        lax.fori_loop(0, blocks, feed, 0)

        normed, inverse = normalise(acc[...])
        n2[...] = normed.astype(BF16)
        r2[m] = jnp.broadcast_to(inverse, r2.shape[1:])

        @pl.when(m >= 2)
        def _():
            @pl.when(first)
            def _():
                hop_copy(m - 2).wait_send()

            @pl.when(second)
            def _():
                mem_copy(m - 2).wait_send()

                @pl.when(item == 0)
                def _():
                    out_away(m - 2, seg - 1).wait_send()

                @pl.when(item == 1)
                def _():
                    out_here(m - 2, seg - 1).wait()

        y[item] = (normed * vecs[1, 0:1, :] + vecs[1, 1:2, :]).astype(BF16)
        out[6].start()

        @pl.when(first)
        def _():
            @pl.when(m == micros - 1)
            def _():
                for m_ in range(micros):
                    keep(m_).wait()

            hop_copy(m).start()

        @pl.when(second)
        def _():
            @pl.when(seg + 1 < segments)
            def _():
                mem_copy(m).start()

            @pl.when(item == 0)
            def _():
                out_away(m, seg).start()

            @pl.when(item == 1)
            def _():
                out_here(m, seg).start()

        for j in range(max(0, blocks - 2), blocks):
            h_save(m, j).wait()
            s_save(m, j).wait()
        return carry

    lax.fori_loop(0, micros, forward, 0)
    for save in saves(micros - 1):
        save.wait()
    for g in (groups - 2, groups - 1):
        p_save(micros - 1, g).wait()

    @pl.when(first)
    def _():
        for k_ in reversed(range(segments - 1)):
            cot_copy(k_).start()
        for m in range(micros - 2, micros):
            hop_copy(m).wait_send()
        for k_ in range(segments):
            out_away(0, k_).wait_recv()

    @pl.when(second)
    def _():
        out_away(micros - 2, segments - 1).wait_send()
        out_here(micros - 1, segments - 1).wait()
        for m in range(2, micros):
            keep(m).wait()
        cot_copy(0).wait_recv()
        for t in range(2, micros):
            grad_load(t, 0).start()

    gmem_ref[...] = jnp.zeros(gmem_ref.shape, F32)
    gvec_ref[...] = jnp.zeros(gvec_ref.shape, F32)

    def back_copy(t):
        return remote(y.at[lax.rem(t, 2)], land.at[t], back_send.at[t], back_recv.at[t], across)

    def mg_copy(t):
        return remote(y.at[lax.rem(t, 2), last_rows], mem_grad.at[t], mg_send.at[t], mg_recv.at[t], across)

    def gt_here(t, seg):
        return local(y.at[lax.rem(t, 2), body_rows], gtok_ref.at[seg], gt_sem.at[t])

    def gt_away(t, seg):
        return remote(y.at[lax.rem(t, 2), body_rows], gtok_ref.at[seg], gt_send.at[seg], gt_recv.at[seg], across)

    def s_load(m, j):
        b = lax.rem(j, 2)
        return local(ss.at[m, :, pl.ds(pl.multiple_of(j * FF_BLOCK, FF_BLOCK), FF_BLOCK)], sb.at[b], s_sem.at[b])

    def d_save(m, j):
        b = lax.rem(j, 2)
        return local(hb.at[b], das.at[m, :, pl.ds(pl.multiple_of(j * FF_BLOCK, FF_BLOCK), FF_BLOCK)], h_sem.at[b])

    def p_load(m, g):
        return local(ps.at[m, g], pb.at[g % 2], p_sem.at[g % 2])

    def n2_load(m):
        return local(n2s.at[m], n2, load_sem.at[1])

    n2_load(2 * segments - 2).start()
    s_load(2 * segments - 2, 0).start()
    s_load(2 * segments - 2, 1).start()

    def back_saves(m):
        pairs = [(df, dfs), (db, dbs), (dq_ref, dqs), (o, dks), (y1, dvs)]
        return [local(here, there.at[m], save_sem.at[i]) for i, (here, there) in enumerate(pairs)]

    def backward(t, carry):
        item = lax.rem(t, 2)
        seg = segments - 1 - t // 2
        m = 2 * seg + item
        before = 2 * (segments - 1 - (t - 1) // 2) + lax.rem(t - 1 + 2, 2)

        @pl.when(t > 0)
        def _():
            for save in back_saves(before):
                save.wait()

        loads = [local(source.at[m], here, load_sem.at[2 + i])
                 for i, (source, here) in enumerate([(qs, q), (ks, k), (vs, v), (n1s, n1)])]
        grads_in = land.at[t]

        @pl.when(second)
        def _():
            for t_ in range(micros):
                @pl.when(t == t_)
                def _():
                    grad_load(t_, 0).wait()

            @pl.when(seg + 1 == segments)
            def _():
                grads_in[last_rows, :] = jnp.zeros((rows - tokens, width), BF16)

            @pl.when(seg + 1 < segments)
            def _():
                mg_copy(t - 2).wait_recv()
                got = mem_grad[t - 2]
                grads_in[last_rows, :] = jnp.where(fresh(item), jnp.zeros_like(got), got)

        @pl.when(first)
        def _():
            back_copy(t).wait_recv()

        n2_load(m).wait()
        dz, gain_grad, bias_grad = norm_back(grads_in[...].astype(F32), n2[...].astype(F32), r2[m, :, 0:1], vecs[1, 0:1, :])
        gvec_ref[2:3, :] += gain_grad
        gvec_ref[3:4, :] += bias_grad
        df[...] = dz.astype(BF16)
        acc[...] = dz
        out = back_saves(m)
        out[0].start()
        for load in loads:
            load.start()
        p_load(m, 0).start()
        p_load(m, 1).start()
        following = 2 * (segments - 1 - (t + 1) // 2) + lax.rem(t + 1, 2)

        @pl.when(t + 1 < micros)
        def _():
            n2_load(following).start()

        def feed(j, carry2):
            b = lax.rem(j, 2)

            @pl.when(j >= 2)
            def _():
                d_save(m, j - 2).wait()

            s_load(m, j).wait()
            half = FF_BLOCK // 2
            dfv = df[...]
            dh = [mm(dfv, w2[pl.ds(pl.multiple_of(j * FF_BLOCK + i * half, half), half), :], 1, 1) for i in range(2)]
            for i in range(2):
                cut = slice(i * half, (i + 1) * half)
                hb[b, :, cut] = (dh[i] * sb[b, :, cut].astype(F32)).astype(BF16)
            d_save(m, j).start()

            @pl.when(j + 2 < blocks)
            def _():
                s_load(m, j + 2).start()

            acc[...] += mm(hb[b], w1[:, pl.ds(pl.multiple_of(j * FF_BLOCK, FF_BLOCK), FF_BLOCK)], 1, 1)
            return carry2

        lax.fori_loop(0, blocks, feed, 0)

        @pl.when(t + 1 < micros)
        def _():
            s_load(following, 0).start()
            s_load(following, 1).start()

        for load in loads:
            load.wait()
        dz, gain_grad, bias_grad = norm_back(acc[...].astype(BF16).astype(F32), n1[...].astype(F32), r1[m, :, 0:1],
                                             vecs[0, 0:1, :])
        gvec_ref[0:1, :] += gain_grad
        gvec_ref[1:2, :] += bias_grad
        db[...] = dz.astype(BF16)
        acc[...] = dz
        out[1].start()

        def begin(g):
            gv = mm(db[...], wa[band(g), pl.ds(3 * width, width)], 1, 1).astype(BF16)
            grads = head_rows(gv, GROUP, head)
            return grads, mm(v[:, band(g)], grads, 1, 1)

        ahead = begin(0)
        for g in range(groups):
            here = band(g)
            grads, dp = ahead
            ahead = begin(g + 1) if g + 1 < groups else None
            p_load(m, g).wait()
            p = pb[g % 2]
            dv = mm(p, grads).astype(BF16)
            weight = p.astype(F32)
            ds = (weight * (dp - jnp.sum(weight * dp, axis=0, keepdims=True))).astype(BF16)
            if g + 2 < groups:
                p_load(m, g + 2).start()
            dk = mm(ds, head_rows(q[:, here] * scale, GROUP, head)).astype(BF16)
            dq = (head_fold(mm(ds, k[:, here], 0, 0), GROUP, head) * scale).astype(BF16)
            dq_ref[:, here] = dq
            o[:, here] = dk
            y1[:, here] = dv
        acc[...] += (mm(dq_ref[...], wa[:, pl.ds(0, width)], 1, 1) + mm(o[...], wa[:, pl.ds(width, width)], 1, 1)
                     + mm(y1[...], wa[:, pl.ds(2 * width, width)], 1, 1))
        for i in (2, 3, 4):
            out[i].start()

        @pl.when(t >= 2)
        def _():
            @pl.when(second)
            def _():
                back_copy(t - 2).wait_send()

            @pl.when(first)
            def _():
                mg_copy(t - 2).wait_send()

                @pl.when(item == 1)
                def _():
                    gt_away(t - 2, seg + 1).wait_send()

                @pl.when(item == 0)
                def _():
                    gt_here(t - 2, seg + 1).wait()

        dx = acc[...].astype(BF16)
        y[item] = dx

        @pl.when(second)
        def _():
            back_copy(t).start()

        @pl.when(first)
        def _():
            tail_grad = dx[tokens:, :].astype(F32)

            @pl.when(seg > 0)
            def _():
                mg_copy(t).start()
                gmem_ref[...] += jnp.where(fresh(item), tail_grad, 0.0)

            @pl.when(seg == 0)
            def _():
                gmem_ref[...] += tail_grad

            @pl.when(item == 0)
            def _():
                gt_here(t, seg).start()

            @pl.when(item == 1)
            def _():
                gt_away(t, seg).start()

        for j in range(max(0, blocks - 2), blocks):
            d_save(m, j).wait()
        return carry

    lax.fori_loop(0, micros, backward, 0)
    for save in back_saves(1):
        save.wait()

    @pl.when(second)
    def _():
        for t in range(micros - 2, micros):
            back_copy(t).wait_send()
        for k_ in range(segments):
            tok_copy(k_).wait_send()
            gt_away(1, k_).wait_recv()

    @pl.when(first)
    def _():
        gt_here(micros - 2, 0).wait()
        gt_away(micros - 1, 0).wait_send()
        for k_ in range(segments):
            cot_copy(k_).wait_send()

    proj_a.wait_send()
    down_away.wait_send()
    vec_away.wait_send()


def run_layers(tokens, cotangent, proj, down, docs, vec, memory, flags):
    segments, seg_tokens, width = tokens.shape
    rows = seg_tokens + TILE
    hidden = proj.shape[1]
    micros = 2 * segments
    groups = HEADS // GROUP
    span = GROUP * rows
    stack = shape_of((micros, rows, width))
    wide = shape_of((micros, rows, hidden))
    low = pltpu.VMEM((rows, width), BF16)
    dma = pltpu.SemaphoreType.DMA
    pair = pltpu.VMEM((2, rows, FF_BLOCK), BF16)
    inverse = pltpu.VMEM((micros, rows, 128), F32)
    tails = pltpu.VMEM((2, TILE, width), BF16)
    return pl.pallas_call(
        layers_kernel,
        in_specs=[anywhere()] * 5 + [on_chip()] * 2 + [pl.BlockSpec(memory_space=pltpu.SMEM)],
        out_specs=[anywhere()] * 2 + [on_chip()] * 2 + [anywhere()] * 18,
        out_shape=[shape_of(tokens.shape), shape_of(tokens.shape), shape_of((TILE, width), F32),
                   shape_of((8, width), F32)]
        + [stack] * 8 + [wide] * 2 + [shape_of((micros, groups, rows, span))] + [stack] * 5 + [wide]
        + [shape_of(tokens.shape)],
        scratch_shapes=[
            pltpu.VMEM((width, hidden), BF16), pltpu.VMEM((width, hidden), BF16), pltpu.VMEM((hidden, width), BF16),
            pltpu.VMEM((2, 2, width), F32), pltpu.VMEM((2, segments, seg_tokens), jnp.int32),
            pltpu.VMEM((micros, rows, 128), jnp.int32), pltpu.VMEM((micros, 1, span), jnp.int32),
            pltpu.VMEM((TILE, width), BF16), pltpu.VMEM((micros, rows, width), BF16)] + [low] * 11 + [
            pltpu.VMEM((rows, width), F32), pltpu.VMEM((2, rows, width), BF16), pair, pair,
            pltpu.VMEM((2, rows, span), BF16), inverse, inverse, tails, tails,
            dma((3,)), dma((3,)), dma((3,)), dma((segments,)), dma((segments,)), dma((segments,)), dma((segments,)),
            dma((segments,)),
            dma((micros,)), dma((micros,)), dma((micros,)), dma((micros,)), dma((2,)), dma((2,)), dma((2,)), dma((2,)),
            dma((micros,)), dma((segments,)), dma((segments,)), dma((micros,)), dma((segments,)), dma((segments,)),
            dma((6 + micros,)), dma((7,)), dma((micros,)), dma((2,)), dma((2,)), dma((2,))],
        compiler_params=pltpu.CompilerParams(vmem_limit_bytes=VMEM_BYTES, collective_id=1, has_side_effects=True),
        name="layers",
    )(tokens, cotangent, proj, down, docs, vec, memory, flags)


def flipped(index, bit):
    return index + bit - 2 * bit * lax.rem(index // bit, 2)


def ring_piece(n, width):
    piece = -(-width // (2 * n))
    return piece + -piece % 16


def grads_kernel(xs, os_, y1s, hs, dqs, dks, dvs, dbs, das, dfs, small_ref, out_ref, vec_out, memory_out,
                 lbuf, rbuf, mine, got, away, final, slots, held, arrived,
                 left_sem, right_sem, swap_send, swap_recv, sum_send, sum_recv, full_send, full_recv,
                 small_send, small_recv, store_sem, *, n, piece, hops, ups, halves):
    section = lax.axis_index("section")
    data = lax.axis_index("dp")
    core = lax.rem(section, 2)
    mate = {"section": section + 1 - 2 * core}
    width = final.shape[2]
    tiles = ups + halves
    half = n // 2
    micros, rows = lbuf.shape[1:3]

    def place(p):
        p = lax.rem(p + 2 * n, n)
        return jnp.where(p < half, 2 * p, 2 * (n - 1 - p) + 1)

    me = jnp.where(lax.rem(data, 2) == 0, data // 2, n - 1 - data // 2)
    peers = ({"dp": place(me + 1)}, {"dp": place(me - 1)})
    signs = (1, -1)

    def remote(source, target, send, recv, device):
        return pltpu.make_async_remote_copy(src_ref=source, dst_ref=target, send_sem=send, recv_sem=recv,
                                            device_id=device, device_id_type=MESH)

    def part(ref, column):
        return ref.at[:, :, pl.ds(column * width, width)]

    attn = [(xs, dqs), (xs, dks), (xs, dvs), (os_, dbs)] + [(part(hs, i), dfs) for i in range(halves)]
    feed = [(y1s, part(das, i)) for i in range(ups)] + [(part(hs, halves + i), dfs) for i in range(halves)]

    def loads(t, which):
        b = t % 2
        left, right = (attn, feed)[which][t // 2]
        return (pltpu.make_async_copy(left, lbuf.at[b], left_sem.at[b]),
                pltpu.make_async_copy(right, rbuf.at[b], right_sem.at[b]))

    def start_load(t):
        turn = core if t % 2 else 1 - core
        for which in (0, 1):
            @pl.when(turn == which)
            def _():
                for copy in loads(t, which):
                    copy.start()

    start_load(0)
    barrier = pltpu.get_barrier_semaphore()
    friends = [{axis: flipped(section if axis == "section" else data, bit)} for axis, bit in hops]
    for device in [mate, *peers, *friends]:
        pl.semaphore_signal(barrier, inc=1, device_id=device, device_id_type=MESH)
    pl.semaphore_wait(barrier, 3 + len(friends))

    held[0] = small_ref[...]

    def small_copy(i):
        return remote(held.at[i], arrived.at[i], small_send.at[i], small_recv.at[i], friends[i])

    small_copy(0).start()

    def finish_small(i):
        small_copy(i).wait_recv()
        total = held[i] + arrived[i]
        if i + 1 < len(friends):
            held[i + 1] = total
            small_copy(i + 1).start()
        else:
            share, lines = memory_out.shape[1], memory_out.shape[0]
            for which in range(width // share):
                @pl.when(section == which)
                def _():
                    vec_out[...] = total[2 * which:2 * which + 2, :]
                    memory_out[...] = total[8:8 + lines, which * share:(which + 1) * share]

    def swap(j):
        return remote(away.at[lax.rem(j, 2)], got.at[j, pl.ds(0, width)], swap_send.at[j], swap_recv.at[j], mate)

    def piece_rows(index, d):
        return pl.ds(pl.multiple_of((lax.rem(index + 2 * n, n) * 2 + d) * piece, 16), piece)

    def sum_copy(i, d, s):
        where = mine.at[i, piece_rows(me - signs[d] * s, d)]
        return remote(where, slots.at[i, d, s], sum_send.at[i, d, s], sum_recv.at[i, d, s], peers[d])

    def full_copy(i, d, s):
        where = final.at[i, piece_rows(me + signs[d] * (1 - s), d)]
        return remote(where, where, full_send.at[i, d, s], full_recv.at[i, d, s], peers[d])

    def store(i):
        return pltpu.make_async_copy(final.at[i], out_ref.at[i], store_sem.at[i])

    def serve(i, s):
        @pl.when(s == 0)
        def _():
            swap(i).wait_recv()

        @pl.when((s >= 0) & (s < n))
        def _():
            for d in (0, 1):
                here = piece_rows(me - signs[d] * s, d)
                value = mine[i, here, :].astype(F32) + got[i, here, :].astype(F32)

                @pl.when(s == 0)
                def _():
                    mine[i, here, :] = value.astype(BF16)
                    sum_copy(i, d, s).start()

                @pl.when(s > 0)
                def _():
                    sum_copy(i, d, s - 1).wait_recv()
                    total = (value + slots[i, d, s - 1].astype(F32)).astype(BF16)

                    @pl.when(s < n - 1)
                    def _():
                        mine[i, here, :] = total
                        sum_copy(i, d, s).start()

                    @pl.when(s == n - 1)
                    def _():
                        final[i, here, :] = total
                        full_copy(i, d, 0).start()

        @pl.when((s >= n) & (s < 2 * n - 1))
        def _():
            f = s - n + 1
            for d in (0, 1):
                full_copy(i, d, f - 1).wait_recv()

                @pl.when(f < n - 1)
                def _():
                    full_copy(i, d, f).start()

            @pl.when(f == n - 1)
            def _():
                store(i).start()

    for t in range(2 * tiles):
        if t + 1 < 2 * tiles:
            start_load(t + 1)
        b, j = t % 2, t // 2
        for copy in loads(t, 0):
            copy.wait()
        tile = mm(lbuf[b].reshape(micros * rows, width), rbuf[b].reshape(micros * rows, width), 0, 0).astype(BF16)
        if t % 2 == 0:
            if j >= 2:
                swap(j - 2).wait_send()
            away[j % 2] = tile
            swap(j).start()
        else:
            mine[j, 0:width, :] = tile
        for i in range(tiles):
            if t - 2 * i - 1 >= 0:
                serve(i, jnp.int32(t - 2 * i - 1))

    begin = 2 * tiles

    def rest(t, carry):
        for k in range(len(friends)):
            @pl.when(t == begin + k)
            def _():
                finish_small(k)

        def one(i, carry2):
            serve(i, t - 2 * i - 1)
            return carry2

        lax.fori_loop(0, tiles, one, 0)
        return carry

    lax.fori_loop(begin, 2 * tiles - 1 + 2 * n - 1, rest, 0)

    def finish(i, carry):
        def sends(s, carry2):
            for d in (0, 1):
                sum_copy(i, d, s).wait_send()
                full_copy(i, d, s).wait_send()
            return carry2

        lax.fori_loop(0, n - 1, sends, 0)
        store(i).wait()
        return carry

    lax.fori_loop(0, tiles, finish, 0)
    for j in range(tiles - 2, tiles):
        swap(j).wait_send()
    for i in range(len(friends)):
        small_copy(i).wait_send()


def weight_gradients(stacks, small, n, sections, width, ups, halves, memory):
    piece = ring_piece(n, width)
    total = 2 * n * piece
    micros, rows = stacks[0].shape[:2]
    tiles = ups + halves
    hops = [("dp", 1 << i) for i in range(n.bit_length() - 1)]
    hops += [("section", 1 << i) for i in range(sections.bit_length() - 1)]
    dma = pltpu.SemaphoreType.DMA
    kept = pltpu.VMEM((tiles, total, width), BF16)
    operand = pltpu.VMEM((2, micros, rows, width), BF16)
    sums = pltpu.VMEM((len(hops),) + small.shape, F32)
    return pl.pallas_call(
        functools.partial(grads_kernel, n=n, piece=piece, hops=hops, ups=ups, halves=halves),
        in_specs=[anywhere()] * len(stacks) + [on_chip()],
        out_specs=[anywhere(), on_chip(), on_chip()],
        out_shape=[shape_of((tiles, total, width)), shape_of((2, width), F32),
                   shape_of((memory, width // sections), F32)],
        scratch_shapes=[
            operand, operand, kept, kept, pltpu.VMEM((2, width, width), BF16), kept,
            pltpu.VMEM((tiles, 2, n - 1, piece, width), BF16), sums, sums,
            dma((2,)), dma((2,)), dma((tiles,)), dma((tiles,)),
            dma((tiles, 2, n - 1)), dma((tiles, 2, n - 1)), dma((tiles, 2, n - 1)), dma((tiles, 2, n - 1)),
            dma((len(hops),)), dma((len(hops),)), dma((tiles,))],
        compiler_params=pltpu.CompilerParams(vmem_limit_bytes=VMEM_BYTES, collective_id=0, has_side_effects=True),
        name="weight_gradients",
    )(*stacks, small)


def widen_kernel(in_ref, proj_ref, down_ref, *, ups):
    step = pl.program_id(0)

    @pl.when(step < ups)
    def _():
        proj_ref[...] = in_ref[...].astype(F32)

    @pl.when(step >= ups)
    def _():
        down_ref[...] = in_ref[...].astype(F32)


def widen(data, ups, halves):
    width = data.shape[2]
    return pl.pallas_call(
        functools.partial(widen_kernel, ups=ups), grid=(ups + halves,),
        in_specs=[pl.BlockSpec((None, width, width), lambda b: (b, 0, 0))],
        out_specs=[pl.BlockSpec((width, width), lambda b: (0, jnp.minimum(b, ups - 1))),
                   pl.BlockSpec((width, width), lambda b: (jnp.maximum(b - ups, 0), 0))],
        out_shape=[shape_of((width, ups * width), F32), shape_of((halves * width, width), F32)],
        compiler_params=pltpu.CompilerParams(vmem_limit_bytes=VMEM_BYTES), name="widen",
    )(data)


def body(tokens, doc_ids, reset_flags, memory_init, w_proj, vectors, w_down, cotangent):
    data_count = lax.axis_size("dp")
    sections = lax.axis_size("section")
    first = lax.axis_index("section") < 2
    width = tokens.shape[3]
    blocks = w_proj.shape[2] // width
    half = w_down.shape[0] // width

    results = run_layers(tokens[0], cotangent[0], w_proj[0], w_down, doc_ids, vectors[0], memory_init, reset_flags)
    block_rows, input_rows, grad_memory, grad_vec = results[:4]
    x_in, q, k_rows, v, o, n1, y1, n2, h, slope, p, df, db, dq, dk, dv, da = results[4:21]
    vec_pair = grad_vec[:4]
    nothing = jnp.zeros_like(vec_pair)
    small = jnp.concatenate([jnp.where(first, vec_pair, nothing), jnp.where(first, nothing, vec_pair), grad_memory],
                            axis=0)
    summed, total_vec, total_memory = weight_gradients(
        [x_in, o, y1, h, dq, dk, dv, db, da, df], small, data_count, sections, width, blocks, half,
        memory_init.shape[0])
    total_proj, total_down = widen(summed, blocks, half)
    return (block_rows[None], input_rows[None], total_proj[None], total_vec[None], total_down, total_memory)


def solution(mesh):
    items = P(("section", "dp"), None, None, None)
    return jax.shard_map(
        body,
        mesh=mesh,
        in_specs=(items, P(), P(), P(), P("section", None, None), P("section", None, None),
                  P("section", None), items),
        out_specs=(items, items, P("section", None, None), P("section", None, None),
                   P("section", None), P(None, "section")),
        check_vma=False,
    )
```

```python
import functools

import jax
import jax.numpy as jnp
from jax import lax
from jax.experimental import pallas as pl
from jax.experimental.pallas import tpu as pltpu
from jax.sharding import PartitionSpec as P

HEADS = 12
DOCS = 4
NORM_EPSILON = 1e-06
NEGATIVE = -1e30
BF16 = jnp.bfloat16
F32 = jnp.float32
VMEM_BYTES = 60 * 2**20
GROUP = 4
FF_BLOCK = 1536
TILE = 16
MESH = pl.DeviceIdType.MESH


def mm(left, right, ca=1, cb=0):
    return lax.dot_general(
        left, right, (((ca,), (cb,)), ((), ())), preferred_element_type=F32
    )


def shape_of(shape, dtype=BF16):
    return jax.ShapeDtypeStruct(shape, dtype)


def anywhere():
    return pl.BlockSpec(memory_space=pl.ANY)


def on_chip():
    return pl.BlockSpec(memory_space=pltpu.VMEM)


def head_rows(block, group, head):
    lane = lax.broadcasted_iota(jnp.int32, (1, block.shape[1]), 1) // head
    return jnp.concatenate([jnp.where(lane == h, block, jnp.zeros_like(block)) for h in range(group)], axis=0)


def head_fold(stacked, group, head):
    total, width = stacked.shape
    rows = total // group
    lane = lax.broadcasted_iota(jnp.int32, (1, width), 1) // head
    out = stacked[:rows]
    for h in range(1, group):
        out = jnp.where(lane == h, stacked[h * rows:(h + 1) * rows], out)
    return out


def normalise(summed):
    center = summed - jnp.mean(summed, axis=-1, keepdims=True)
    variance = jnp.mean(center * center, axis=-1, keepdims=True)
    inverse = lax.rsqrt(variance + NORM_EPSILON)
    return center * inverse, inverse


def norm_back(g, n, inverse, gain):
    u = g * gain
    dz = inverse * (u - jnp.mean(u, axis=-1, keepdims=True) - n * jnp.mean(u * n, axis=-1, keepdims=True))
    return dz, jnp.sum(g * n, axis=0, keepdims=True), jnp.sum(g, axis=0, keepdims=True)


def layers_kernel(tokens_ref, cot_ref, proj_ref, down_ref, docs_ref, vec_ref, memory_ref, flags_ref,
                  out_ref, gtok_ref, late_ref, small_ref,
                  xs, qs, ks, vs, os_, n1s, y1s, n2s, hs, ss, ps, dfs, dbs, dqs, dks, dvs, das,
                  wa, w1, w2, vecs, docs, key_ref, query_ref, init_ref, fresh_ref, cot_other, land, dq_ref, q, k, v, o, n1, y1, n2, df, db, do, acc, y, hb, sb, pb, r1, r2,
                  mem_in, mem_grad,
                  share_local, share_send, share_recv, tok_local, tok_send, tok_recv, cot_send, cot_recv,
                  hop_send, hop_recv, back_send, back_recv, mem_send, mem_recv, mg_send, mg_recv,
                  out_sem, out_send, out_recv, gt_sem, gt_send, gt_recv,
                  gmem_ref, gvec_ref, load_sem, save_sem, keep_sem, h_sem, s_sem, p_sem):
    section = lax.axis_index("section")
    stage = section // 2
    core = lax.rem(section, 2)
    first = stage == 0
    second = stage == 1
    mate = {"section": section + 1 - 2 * core}
    across = {"section": section + 2 - 4 * stage}
    segments, tokens, width = tokens_ref.shape
    rows = land.shape[1]
    memory = memory_ref.shape[0]
    data = lax.axis_index("dp")
    data_count = lax.axis_size("dp")
    owners = (core * data_count + data, (core + 2) * data_count + data)
    hidden = proj_ref.shape[1]
    head = width // HEADS
    cols = GROUP * head
    groups = HEADS // GROUP
    blocks = hidden // FF_BLOCK
    halfd = down_ref.shape[0]
    micros = 2 * segments
    scale = head ** (-0.5)
    body_rows = pl.ds(0, tokens)
    last_rows = pl.ds(tokens, rows - tokens)

    def remote(source, target, send, recv, device):
        return pltpu.make_async_remote_copy(src_ref=source, dst_ref=target, send_sem=send, recv_sem=recv,
                                            device_id=device, device_id_type=MESH)

    local = pltpu.make_async_copy

    barrier = pltpu.get_barrier_semaphore()
    pl.semaphore_signal(barrier, inc=1, device_id=mate, device_id_type=MESH)
    pl.semaphore_signal(barrier, inc=1, device_id=across, device_id_type=MESH)
    pl.semaphore_wait(barrier, 2)

    down_rows = pl.ds(pl.multiple_of(core * halfd, 16), halfd)
    other_rows = pl.ds(pl.multiple_of((1 - core) * halfd, 16), halfd)
    down_away = remote(down_ref, w2.at[down_rows], share_send.at[1], share_recv.at[1], mate)
    vec_away = remote(vec_ref, vecs.at[core], share_send.at[2], share_recv.at[2], mate)
    proj_a = remote(proj_ref, wa, share_send.at[0], share_recv.at[0], mate)
    proj_b = remote(proj_ref, w1, share_send.at[0], share_recv.at[0], mate)
    proj_here_a = local(proj_ref, wa, share_local.at[0])
    proj_here_b = local(proj_ref, w1, share_local.at[0])
    down_here = local(down_ref, w2.at[down_rows], share_local.at[1])
    vec_here = local(vec_ref, vecs.at[core], share_local.at[2])

    @pl.when(core == 0)
    def _():
        proj_a.start()
        proj_here_a.start()

    @pl.when(core == 1)
    def _():
        proj_b.start()
        proj_here_b.start()

    vec_away.start()
    vec_here.start()
    down_away.start()
    down_here.start()

    doc_loads = [local(docs_ref.at[owners[i]], docs.at[i], load_sem.at[i]) for i in (0, 1)]
    for load in doc_loads:
        load.start()

    def tok_here(k_):
        return local(tokens_ref.at[k_], land.at[2 * k_, body_rows], tok_local.at[k_])

    def tok_copy(k_):
        return remote(tokens_ref.at[k_], land.at[2 * k_ + 1, body_rows], tok_send.at[k_], tok_recv.at[k_], across)

    def cot_copy(k_):
        return remote(cot_ref.at[k_], cot_other.at[k_], cot_send.at[k_], cot_recv.at[k_], across)

    @pl.when(second)
    def _():
        tok_copy(0).start()

    @pl.when(first)
    def _():
        for k_ in range(segments):
            tok_here(k_).start()
        cot_copy(segments - 1).start()

    for i in (0, 1):
        fresh_ref[i] = jnp.broadcast_to(flags_ref[pl.ds(owners[i], 1), segments - 1:segments], fresh_ref.shape[1:])
    init_ref[...] = jnp.concatenate([memory_ref[...], jnp.zeros((rows - tokens - memory, width), BF16)], axis=0)
    for load in doc_loads:
        load.wait()
    every = (1 << DOCS) - 1
    tail = lax.broadcasted_iota(jnp.int32, (rows - tokens, key_ref.shape[2]), 0)
    for m_ in range(micros):
        bits = jnp.left_shift(jnp.int32(1), docs[m_ % 2, m_ // 2:m_ // 2 + 1, :])
        row = jnp.concatenate([bits, jnp.full((1, rows - tokens), every, jnp.int32)], axis=1)
        query_ref[m_] = jnp.concatenate([row] * GROUP, axis=1)
        column = jnp.broadcast_to(bits.astype(F32), (8, tokens)).T[:, 0:1].astype(jnp.int32)
        key_ref[m_, body_rows, :] = jnp.broadcast_to(column, (tokens, key_ref.shape[2]))
        key_ref[m_, last_rows, :] = jnp.where(tail < memory, every, 0)

    def fresh(item):
        return jnp.broadcast_to(fresh_ref[item], (rows - tokens, width)) == 1

    vec_here.wait()
    vec_away.wait_recv()

    @pl.when(core == 0)
    def _():
        proj_here_a.wait()

    @pl.when(core == 1)
    def _():
        proj_a.wait_recv()
        remote(down_ref, w2.at[other_rows], share_send.at[1], share_recv.at[1], mate).wait_recv()

    @pl.when(second)
    def _():
        tok_copy(0).wait_send()
        for k_ in range(1, segments):
            tok_copy(k_).start()

    def hop_copy(m):
        return remote(y.at[lax.rem(m, 2)], land.at[m], hop_send.at[m], hop_recv.at[m], across)

    def mem_copy(m):
        return remote(y.at[lax.rem(m, 2), last_rows], mem_in.at[m], mem_send.at[m], mem_recv.at[m], across)

    def out_here(m, seg):
        return local(y.at[lax.rem(m, 2), body_rows], out_ref.at[seg], out_sem.at[m])

    def out_away(m, seg):
        return remote(y.at[lax.rem(m, 2), body_rows], out_ref.at[seg], out_send.at[seg], out_recv.at[seg], across)

    kept = [(q, qs), (k, ks), (v, vs), (o, os_), (n1, n1s), (y1, y1s), (n2, n2s)]

    def keep(m):
        return local(land.at[m], xs.at[m], keep_sem.at[m])

    def grad_load(t, seg):
        source = cot_ref if t % 2 else cot_other
        return local(source.at[seg], land.at[t, body_rows], load_sem.at[6 + t])

    def saves(m):
        return [local(here, there.at[m], save_sem.at[i]) for i, (here, there) in enumerate(kept)]

    def band(g):
        return pl.ds(g * cols, cols)

    def h_save(m, j):
        b = lax.rem(j, 2)
        return local(hb.at[b], hs.at[m, :, pl.ds(pl.multiple_of(j * FF_BLOCK, FF_BLOCK), FF_BLOCK)], h_sem.at[b])

    def s_save(m, j):
        b = lax.rem(j, 2)
        return local(sb.at[b], ss.at[m, :, pl.ds(pl.multiple_of(j * FF_BLOCK, FF_BLOCK), FF_BLOCK)], s_sem.at[b])

    def p_save(m, g):
        return local(pb.at[g % 2], ps.at[m, g], p_sem.at[g % 2])

    def forward(m, carry):
        item = lax.rem(m, 2)
        seg = m // 2

        @pl.when(m > 0)
        def _():
            for save in saves(m - 1):
                save.wait()

        x = land.at[m]

        @pl.when(first)
        def _():
            @pl.when(item == 0)
            def _():
                tok_here(seg).wait()

            @pl.when(item == 1)
            def _():
                tok_copy(seg).wait_recv()

            @pl.when(seg == 0)
            def _():
                x[last_rows, :] = init_ref[...]

            @pl.when(seg > 0)
            def _():
                mem_copy(m - 2).wait_recv()
                x[last_rows, :] = jnp.where(fresh(item), init_ref[...], mem_in[m - 2])

        @pl.when(second)
        def _():
            hop_copy(m).wait_recv()

            @pl.when(m == micros - 1)
            def _():
                keep(0).wait()
                keep(1).wait()
                cot_copy(segments - 1).wait_recv()
                for t in (0, 1):
                    grad_load(t, segments - 1).start()

        keep(m).start()
        out = saves(m)

        def project(g):
            here = band(g)
            xv = x[...]
            q[:, here] = mm(xv, wa[:, here]).astype(BF16)
            k[:, here] = mm(xv, wa[:, pl.ds(width + g * cols, cols)]).astype(BF16)
            v[:, here] = mm(xv, wa[:, pl.ds(2 * width + g * cols, cols)]).astype(BF16)
            return mm(k[:, here], head_rows(q[:, here] * scale, GROUP, head), 1, 1)

        score = project(0)
        for g in range(groups):
            following = project(g + 1) if g + 1 < groups else None
            if g >= 2:
                p_save(m, g - 2).wait()
            else:
                @pl.when(m > 0)
                def _():
                    p_save(m - 1, groups - 1 - (groups - 1 - g) % 2).wait()
            s = jnp.where((key_ref[m, :, 0:1] & query_ref[m]) != 0, score, NEGATIVE)
            e = jnp.exp(s - jnp.max(s, axis=0, keepdims=True))
            p = (e * (1.0 / jnp.sum(e, axis=0, keepdims=True))).astype(BF16)
            pb[g % 2] = p
            p_save(m, g).start()
            o[:, band(g)] = head_fold(mm(p, v[:, band(g)], 0, 0), GROUP, head).astype(BF16)
            score = following
        for i in (0, 1, 2, 3):
            out[i].start()
        normed, inverse = normalise(x[...].astype(F32) + mm(o[...], wa[:, pl.ds(3 * width, width)]))
        n1[...] = normed.astype(BF16)
        r1[m] = jnp.broadcast_to(inverse, r1.shape[1:])
        y1v = (normed * vecs[0, 0:1, :] + vecs[0, 1:2, :]).astype(BF16)
        y1[...] = y1v
        acc[...] = y1v.astype(F32)
        out[4].start()
        out[5].start()

        @pl.when(m == 0)
        def _():
            @pl.when(core == 0)
            def _():
                proj_b.wait_recv()
                remote(down_ref, w2.at[other_rows], share_send.at[1], share_recv.at[1], mate).wait_recv()

            @pl.when(core == 1)
            def _():
                proj_here_b.wait()

            down_here.wait()

        def feed(j, carry2):
            b = lax.rem(j, 2)

            @pl.when(j >= 2)
            def _():
                h_save(m, j - 2).wait()
                s_save(m, j - 2).wait()

            half = FF_BLOCK // 2
            yv = y1[...]
            pre = [mm(yv, w1[:, pl.ds(pl.multiple_of(j * FF_BLOCK + i * half, half), half)]) for i in range(2)]
            for i in range(2):
                a = pre[i]
                gate = 0.5 * (1.0 + lax.erf(a * 0.7071067811865476))
                hb[b, :, i * half:(i + 1) * half] = (a * gate).astype(BF16)
                sb[b, :, i * half:(i + 1) * half] = (
                    gate + a * jnp.exp(-0.5 * a * a) * 0.3989422804014327).astype(BF16)
            h_save(m, j).start()
            s_save(m, j).start()
            acc[...] += mm(hb[b], w2[pl.ds(pl.multiple_of(j * FF_BLOCK, FF_BLOCK), FF_BLOCK), :])
            return carry2

        lax.fori_loop(0, blocks, feed, 0)

        normed, inverse = normalise(acc[...])
        n2[...] = normed.astype(BF16)
        r2[m] = jnp.broadcast_to(inverse, r2.shape[1:])

        @pl.when(m >= 2)
        def _():
            @pl.when(first)
            def _():
                hop_copy(m - 2).wait_send()

            @pl.when(second)
            def _():
                mem_copy(m - 2).wait_send()

                @pl.when(item == 0)
                def _():
                    out_away(m - 2, seg - 1).wait_send()

                @pl.when(item == 1)
                def _():
                    out_here(m - 2, seg - 1).wait()

        y[item] = (normed * vecs[1, 0:1, :] + vecs[1, 1:2, :]).astype(BF16)
        out[6].start()

        @pl.when(first)
        def _():
            @pl.when(m == micros - 1)
            def _():
                for m_ in range(micros):
                    keep(m_).wait()

            hop_copy(m).start()

        @pl.when(second)
        def _():
            @pl.when(seg + 1 < segments)
            def _():
                mem_copy(m).start()

            @pl.when(item == 0)
            def _():
                out_away(m, seg).start()

            @pl.when(item == 1)
            def _():
                out_here(m, seg).start()

        for j in range(max(0, blocks - 2), blocks):
            h_save(m, j).wait()
            s_save(m, j).wait()
        return carry

    lax.fori_loop(0, micros, forward, 0)
    for save in saves(micros - 1):
        save.wait()
    for g in (groups - 2, groups - 1):
        p_save(micros - 1, g).wait()

    @pl.when(first)
    def _():
        for m in range(micros - 2, micros):
            hop_copy(m).wait_send()
        for k_ in reversed(range(segments - 1)):
            cot_copy(k_).start()
        for k_ in range(segments):
            out_away(0, k_).wait_recv()

    @pl.when(second)
    def _():
        out_away(micros - 2, segments - 1).wait_send()
        out_here(micros - 1, segments - 1).wait()
        for m in range(2, micros):
            keep(m).wait()

    gmem_ref[...] = jnp.zeros(gmem_ref.shape, F32)
    gvec_ref[...] = jnp.zeros(gvec_ref.shape, F32)

    def back_copy(t):
        return remote(y.at[lax.rem(t, 2)], land.at[t], back_send.at[t], back_recv.at[t], across)

    def mg_copy(t):
        return remote(y.at[lax.rem(t, 2), last_rows], mem_grad.at[t], mg_send.at[t], mg_recv.at[t], across)

    def gt_here(t, seg):
        return local(y.at[lax.rem(t, 2), body_rows], gtok_ref.at[seg], gt_sem.at[t])

    def gt_away(t, seg):
        return remote(y.at[lax.rem(t, 2), body_rows], gtok_ref.at[seg], gt_send.at[seg], gt_recv.at[seg], across)

    def gt_late():
        return local(y.at[1, body_rows], late_ref, gt_sem.at[micros - 1])

    def s_load(m, j):
        b = lax.rem(j, 2)
        return local(ss.at[m, :, pl.ds(pl.multiple_of(j * FF_BLOCK, FF_BLOCK), FF_BLOCK)], sb.at[b], s_sem.at[b])

    def d_save(m, j):
        b = lax.rem(j, 2)
        return local(hb.at[b], das.at[m, :, pl.ds(pl.multiple_of(j * FF_BLOCK, FF_BLOCK), FF_BLOCK)], h_sem.at[b])

    def p_load(m, g):
        return local(ps.at[m, g], pb.at[g % 2], p_sem.at[g % 2])

    def n2_load(m):
        return local(n2s.at[m], n2, load_sem.at[1])

    n2_load(2 * segments - 2).start()
    s_load(2 * segments - 2, 0).start()
    s_load(2 * segments - 2, 1).start()

    def back_saves(m):
        pairs = [(df, dfs), (db, dbs), (dq_ref, dqs), (o, dks), (y1, dvs)]
        return [local(here, there.at[m], save_sem.at[i]) for i, (here, there) in enumerate(pairs)]

    def backward(t, carry):
        item = lax.rem(t, 2)
        seg = segments - 1 - t // 2
        m = 2 * seg + item
        before = 2 * (segments - 1 - (t - 1) // 2) + lax.rem(t - 1 + 2, 2)

        @pl.when(t > 0)
        def _():
            for save in back_saves(before):
                save.wait()

        loads = [local(source.at[m], here, load_sem.at[2 + i])
                 for i, (source, here) in enumerate([(qs, q), (ks, k), (vs, v), (n1s, n1)])]
        grads_in = land.at[t]

        @pl.when(second)
        def _():
            @pl.when(t == 2)
            def _():
                cot_copy(0).wait_recv()
                for t_ in range(2, micros):
                    grad_load(t_, 0).start()

            for t_ in range(micros):
                @pl.when(t == t_)
                def _():
                    grad_load(t_, 0).wait()

            @pl.when(seg + 1 == segments)
            def _():
                grads_in[last_rows, :] = jnp.zeros((rows - tokens, width), BF16)

            @pl.when(seg + 1 < segments)
            def _():
                mg_copy(t - 2).wait_recv()
                got = mem_grad[t - 2]
                grads_in[last_rows, :] = jnp.where(fresh(item), jnp.zeros_like(got), got)

        @pl.when(first)
        def _():
            back_copy(t).wait_recv()

        n2_load(m).wait()
        dz, gain_grad, bias_grad = norm_back(grads_in[...].astype(F32), n2[...].astype(F32), r2[m, :, 0:1], vecs[1, 0:1, :])
        gvec_ref[2:3, :] += gain_grad
        gvec_ref[3:4, :] += bias_grad
        df[...] = dz.astype(BF16)
        acc[...] = dz
        out = back_saves(m)
        out[0].start()
        for load in loads:
            load.start()
        p_load(m, 0).start()
        p_load(m, 1).start()
        following = 2 * (segments - 1 - (t + 1) // 2) + lax.rem(t + 1, 2)

        @pl.when(t + 1 < micros)
        def _():
            n2_load(following).start()

        def feed(j, carry2):
            b = lax.rem(j, 2)

            @pl.when(j >= 2)
            def _():
                d_save(m, j - 2).wait()

            s_load(m, j).wait()
            half = FF_BLOCK // 2
            dfv = df[...]
            dh = [mm(dfv, w2[pl.ds(pl.multiple_of(j * FF_BLOCK + i * half, half), half), :], 1, 1) for i in range(2)]
            for i in range(2):
                cut = slice(i * half, (i + 1) * half)
                hb[b, :, cut] = (dh[i] * sb[b, :, cut].astype(F32)).astype(BF16)
            d_save(m, j).start()

            @pl.when(j + 2 < blocks)
            def _():
                s_load(m, j + 2).start()

            acc[...] += mm(hb[b], w1[:, pl.ds(pl.multiple_of(j * FF_BLOCK, FF_BLOCK), FF_BLOCK)], 1, 1)
            return carry2

        lax.fori_loop(0, blocks, feed, 0)

        @pl.when(t + 1 < micros)
        def _():
            s_load(following, 0).start()
            s_load(following, 1).start()

        for load in loads:
            load.wait()
        dz, gain_grad, bias_grad = norm_back(acc[...].astype(BF16).astype(F32), n1[...].astype(F32), r1[m, :, 0:1],
                                             vecs[0, 0:1, :])
        gvec_ref[0:1, :] += gain_grad
        gvec_ref[1:2, :] += bias_grad
        db[...] = dz.astype(BF16)
        acc[...] = dz
        out[1].start()

        def begin(g):
            gv = mm(db[...], wa[band(g), pl.ds(3 * width, width)], 1, 1).astype(BF16)
            grads = head_rows(gv, GROUP, head)
            return grads, mm(v[:, band(g)], grads, 1, 1)

        ahead = begin(0)
        for g in range(groups):
            here = band(g)
            grads, dp = ahead
            ahead = begin(g + 1) if g + 1 < groups else None
            p_load(m, g).wait()
            p = pb[g % 2]
            dv = mm(p, grads).astype(BF16)
            weight = p.astype(F32)
            ds = (weight * (dp - jnp.sum(weight * dp, axis=0, keepdims=True))).astype(BF16)
            if g + 2 < groups:
                p_load(m, g + 2).start()
            dk = mm(ds, head_rows(q[:, here] * scale, GROUP, head)).astype(BF16)
            dq = (head_fold(mm(ds, k[:, here], 0, 0), GROUP, head) * scale).astype(BF16)
            dq_ref[:, here] = dq
            o[:, here] = dk
            y1[:, here] = dv
        acc[...] += (mm(dq_ref[...], wa[:, pl.ds(0, width)], 1, 1) + mm(o[...], wa[:, pl.ds(width, width)], 1, 1)
                     + mm(y1[...], wa[:, pl.ds(2 * width, width)], 1, 1))
        for i in (2, 3, 4):
            out[i].start()

        @pl.when(t >= 2)
        def _():
            @pl.when(second)
            def _():
                back_copy(t - 2).wait_send()

            @pl.when(first)
            def _():
                mg_copy(t - 2).wait_send()

                @pl.when(item == 1)
                def _():
                    gt_away(t - 2, seg + 1).wait_send()

                @pl.when(item == 0)
                def _():
                    gt_here(t - 2, seg + 1).wait()

        dx = acc[...].astype(BF16)
        y[item] = dx

        @pl.when(second)
        def _():
            back_copy(t).start()

        @pl.when(first)
        def _():
            tail_grad = dx[tokens:, :].astype(F32)

            @pl.when(seg > 0)
            def _():
                mg_copy(t).start()
                gmem_ref[...] += jnp.where(fresh(item), tail_grad, 0.0)

            @pl.when(seg == 0)
            def _():
                gmem_ref[...] += tail_grad

            @pl.when(item == 0)
            def _():
                gt_here(t, seg).start()

            @pl.when((item == 1) & (seg > 0))
            def _():
                gt_away(t, seg).start()

            @pl.when((item == 1) & (seg == 0))
            def _():
                gt_late().start()

        for j in range(max(0, blocks - 2), blocks):
            d_save(m, j).wait()
        return carry

    lax.fori_loop(0, micros, backward, 0)
    for save in back_saves(1):
        save.wait()

    @pl.when(second)
    def _():
        for t in range(micros - 2, micros):
            back_copy(t).wait_send()
        for k_ in range(1, segments):
            tok_copy(k_).wait_send()
        for k_ in range(1, segments):
            gt_away(1, k_).wait_recv()

    @pl.when(first)
    def _():
        gt_here(micros - 2, 0).wait()
        gt_late().wait()
        for k_ in range(segments):
            cot_copy(k_).wait_send()

    own = gvec_ref[0:4, :]
    none = jnp.zeros_like(own)
    for mine_, parts in ((first, [own, none]), (second, [none, own])):
        @pl.when(mine_)
        def _():
            small_ref[...] = jnp.concatenate(parts + [gmem_ref[...]], axis=0)

    proj_a.wait_send()
    down_away.wait_send()
    vec_away.wait_send()


def run_layers(tokens, cotangent, proj, down, docs, vec, memory, flags):
    segments, seg_tokens, width = tokens.shape
    rows = seg_tokens + TILE
    hidden = proj.shape[1]
    micros = 2 * segments
    groups = HEADS // GROUP
    span = GROUP * rows
    stack = shape_of((micros, rows, width))
    wide = shape_of((micros, rows, hidden))
    low = pltpu.VMEM((rows, width), BF16)
    dma = pltpu.SemaphoreType.DMA
    pair = pltpu.VMEM((2, rows, FF_BLOCK), BF16)
    inverse = pltpu.VMEM((micros, rows, 128), F32)
    tails = pltpu.VMEM((2, TILE, width), BF16)
    return pl.pallas_call(
        layers_kernel,
        in_specs=[anywhere()] * 5 + [on_chip()] * 3,
        out_specs=[anywhere()] * 3 + [on_chip()] + [anywhere()] * 17,
        out_shape=[shape_of(tokens.shape), shape_of(tokens.shape), shape_of(tokens.shape[1:]),
                   shape_of((8 + TILE, width), F32)]
        + [stack] * 8 + [wide] * 2 + [shape_of((micros, groups, rows, span))] + [stack] * 5 + [wide],
        scratch_shapes=[
            pltpu.VMEM((width, hidden), BF16), pltpu.VMEM((width, hidden), BF16), pltpu.VMEM((hidden, width), BF16),
            pltpu.VMEM((2, 2, width), F32), pltpu.VMEM((2, segments, seg_tokens), jnp.int32),
            pltpu.VMEM((micros, rows, 128), jnp.int32), pltpu.VMEM((micros, 1, span), jnp.int32),
            pltpu.VMEM((TILE, width), BF16), pltpu.VMEM((2, 1, width), jnp.int32),
            pltpu.VMEM(tokens.shape, BF16), pltpu.VMEM((micros, rows, width), BF16)] + [low] * 11 + [
            pltpu.VMEM((rows, width), F32), pltpu.VMEM((2, rows, width), BF16), pair, pair,
            pltpu.VMEM((2, rows, span), BF16), inverse, inverse, tails, tails,
            dma((3,)), dma((3,)), dma((3,)), dma((segments,)), dma((segments,)), dma((segments,)), dma((segments,)),
            dma((segments,)),
            dma((micros,)), dma((micros,)), dma((micros,)), dma((micros,)), dma((2,)), dma((2,)), dma((2,)), dma((2,)),
            dma((micros,)), dma((segments,)), dma((segments,)), dma((micros,)), dma((segments,)), dma((segments,)),
            pltpu.VMEM((TILE, width), F32), pltpu.VMEM((8, width), F32),
            dma((6 + micros,)), dma((7,)), dma((micros,)), dma((2,)), dma((2,)), dma((2,))],
        compiler_params=pltpu.CompilerParams(vmem_limit_bytes=VMEM_BYTES, collective_id=1, has_side_effects=True),
        name="layers",
    )(tokens, cotangent, proj, down, docs, vec, memory, flags)


def flipped(index, bit):
    return index + bit - 2 * bit * lax.rem(index // bit, 2)


def ring_piece(n, width):
    piece = -(-width // (2 * n))
    return piece + -piece % 16


def grads_kernel(xs, os_, y1s, hs, dqs, dks, dvs, dbs, das, dfs, late_ref, small_ref, out_ref, late_out, vec_out, memory_out,
                 lbuf, rbuf, mine, got, away, final, slots, held, arrived,
                 left_sem, right_sem, swap_send, swap_recv, sum_send, sum_recv, full_send, full_recv,
                 small_send, small_recv, store_sem, late_sem, *, n, piece, hops, ups, halves):
    section = lax.axis_index("section")
    data = lax.axis_index("dp")
    core = lax.rem(section, 2)
    mate = {"section": section + 1 - 2 * core}
    width = final.shape[2]
    tiles = ups + halves
    half = n // 2
    micros, rows = lbuf.shape[1:3]

    def place(p):
        p = lax.rem(p + 2 * n, n)
        return jnp.where(p < half, 2 * p, 2 * (n - 1 - p) + 1)

    me = jnp.where(lax.rem(data, 2) == 0, data // 2, n - 1 - data // 2)
    peers = ({"dp": place(me + 1)}, {"dp": place(me - 1)})
    signs = (1, -1)

    def remote(source, target, send, recv, device):
        return pltpu.make_async_remote_copy(src_ref=source, dst_ref=target, send_sem=send, recv_sem=recv,
                                            device_id=device, device_id_type=MESH)

    def part(ref, column):
        return ref.at[:, :, pl.ds(column * width, width)]

    attn = [(xs, dqs), (xs, dks), (xs, dvs), (os_, dbs)] + [(part(hs, i), dfs) for i in range(halves)]
    feed = [(y1s, part(das, i)) for i in range(ups)] + [(part(hs, halves + i), dfs) for i in range(halves)]

    def load(t, which, j):
        b = lax.rem(t, 2)
        left, right = (attn, feed)[which][j]
        return (pltpu.make_async_copy(left, lbuf.at[b], left_sem.at[b]),
                pltpu.make_async_copy(right, rbuf.at[b], right_sem.at[b]))

    def start_load(t):
        turn = jnp.where(lax.rem(t, 2) == 1, core, 1 - core)
        for which in (0, 1):
            for j in range(tiles):
                @pl.when((turn == which) & (t // 2 == j))
                def _():
                    for copy in load(t, which, j):
                        copy.start()

    start_load(jnp.int32(0))
    barrier = pltpu.get_barrier_semaphore()
    friends = [{axis: flipped(section if axis == "section" else data, bit)} for axis, bit in hops]
    greeted = [mate, *peers, *friends]
    for device in greeted:
        pl.semaphore_signal(barrier, inc=1, device_id=device, device_id_type=MESH)
    pl.semaphore_wait(barrier, len(greeted))

    across = {"section": flipped(section, 2)}
    late = remote(late_ref, late_out, late_sem.at[0], late_sem.at[1], across)

    @pl.when(section < 2)
    def _():
        late.start()

    held[0] = small_ref[...]

    def small_copy(i):
        return remote(held.at[i], arrived.at[i], small_send.at[i], small_recv.at[i], friends[i])

    small_copy(0).start()

    def finish_small(i):
        small_copy(i).wait_recv()
        total = held[i] + arrived[i]
        if i + 1 < len(friends):
            held[i + 1] = total
            small_copy(i + 1).start()
        else:
            share, lines = memory_out.shape[1], memory_out.shape[0]
            for which in range(width // share):
                @pl.when(section == which)
                def _():
                    vec_out[...] = total[2 * which:2 * which + 2, :]
                    memory_out[...] = total[8:8 + lines, which * share:(which + 1) * share]

    def swap(j):
        return remote(away.at[lax.rem(j, 2)], got.at[j, pl.ds(0, width)], swap_send.at[j], swap_recv.at[j], mate)

    def piece_rows(index, d):
        return pl.ds(pl.multiple_of((lax.rem(index + 2 * n, n) * 2 + d) * piece, 16), piece)

    def sum_copy(i, d, s):
        where = mine.at[i, piece_rows(me - signs[d] * s, d)]
        return remote(where, slots.at[i, d, s], sum_send.at[i, d, s], sum_recv.at[i, d, s], peers[d])

    def full_copy(i, d, s):
        where = final.at[i, piece_rows(me + signs[d] * (1 - s), d)]
        return remote(where, where, full_send.at[i, d, s], full_recv.at[i, d, s], peers[d])

    def store(i):
        return pltpu.make_async_copy(final.at[i], out_ref.at[i], store_sem.at[i])

    def serve(i, s):
        @pl.when(s == 0)
        def _():
            swap(i).wait_recv()

        @pl.when((s >= 0) & (s < n))
        def _():
            for d in (0, 1):
                here = piece_rows(me - signs[d] * s, d)
                value = mine[i, here, :].astype(F32) + got[i, here, :].astype(F32)

                @pl.when(s == 0)
                def _():
                    mine[i, here, :] = value.astype(BF16)
                    sum_copy(i, d, s).start()

                @pl.when(s > 0)
                def _():
                    sum_copy(i, d, s - 1).wait_recv()
                    total = (value + slots[i, d, s - 1].astype(F32)).astype(BF16)

                    @pl.when(s < n - 1)
                    def _():
                        mine[i, here, :] = total
                        sum_copy(i, d, s).start()

                    @pl.when(s == n - 1)
                    def _():
                        final[i, here, :] = total
                        full_copy(i, d, 0).start()

        @pl.when((s >= n) & (s < 2 * n - 1))
        def _():
            f = s - n + 1
            for d in (0, 1):
                full_copy(i, d, f - 1).wait_recv()

                @pl.when(f < n - 1)
                def _():
                    full_copy(i, d, f).start()

            @pl.when(f == n - 1)
            def _():
                store(i).start()

    def finish_sends(i):
        def sends(s, carry2):
            for d in (0, 1):
                sum_copy(i, d, s).wait_send()
                full_copy(i, d, s).wait_send()
            return carry2

        lax.fori_loop(0, n - 1, sends, 0)

    def advance(t, carry):
        @pl.when(t + 1 < 2 * tiles)
        def _():
            start_load(t + 1)

        @pl.when(t < 2 * tiles)
        def _():
            b, j = lax.rem(t, 2), t // 2
            for copy in load(t, 0, 0):
                copy.wait()
            tile = mm(lbuf[b].reshape(micros * rows, width), rbuf[b].reshape(micros * rows, width), 0, 0).astype(BF16)

            @pl.when(b == 0)
            def _():
                @pl.when(j >= 2)
                def _():
                    swap(j - 2).wait_send()

                away[lax.rem(j, 2)] = tile
                swap(j).start()

            @pl.when(b == 1)
            def _():
                mine[j, 0:width, :] = tile

        for k in range(len(friends)):
            @pl.when(t == 2 * tiles + k)
            def _():
                finish_small(k)

        def one(i, carry2):
            serve(i, t - 2 * i - 1)
            return carry2

        lax.fori_loop(0, tiles, one, 0)
        return carry

    lax.fori_loop(0, 2 * tiles + 2 * n - 2, advance, 0)

    def finish(i, carry):
        finish_sends(i)
        store(i).wait()
        return carry

    lax.fori_loop(0, tiles, finish, 0)
    for j in range(tiles - 2, tiles):
        swap(j).wait_send()
    for i in range(len(friends)):
        small_copy(i).wait_send()

    @pl.when(section < 2)
    def _():
        late.wait_send()

    @pl.when(section >= 2)
    def _():
        late.wait_recv()


def weight_gradients(stacks, late, small, n, sections, width, ups, halves, memory):
    piece = ring_piece(n, width)
    total = 2 * n * piece
    micros, rows = stacks[0].shape[:2]
    tiles = ups + halves
    hops = [("dp", 1 << i) for i in range(n.bit_length() - 1)]
    hops += [("section", 1 << i) for i in range(sections.bit_length() - 1)]
    dma = pltpu.SemaphoreType.DMA
    kept = pltpu.VMEM((tiles, total, width), BF16)
    operand = pltpu.VMEM((2, micros, rows, width), BF16)
    sums = pltpu.VMEM((len(hops),) + small.shape, F32)
    return pl.pallas_call(
        functools.partial(grads_kernel, n=n, piece=piece, hops=hops, ups=ups, halves=halves),
        in_specs=[anywhere()] * (len(stacks) + 1) + [on_chip()],
        out_specs=[anywhere(), anywhere(), on_chip(), on_chip()],
        out_shape=[shape_of((tiles, total, width)), shape_of(late.shape), shape_of((2, width), F32),
                   shape_of((memory, width // sections), F32)],
        scratch_shapes=[
            operand, operand, kept, kept, pltpu.VMEM((2, width, width), BF16), kept,
            pltpu.VMEM((tiles, 2, n - 1, piece, width), BF16), sums, sums,
            dma((2,)), dma((2,)), dma((tiles,)), dma((tiles,)),
            dma((tiles, 2, n - 1)), dma((tiles, 2, n - 1)), dma((tiles, 2, n - 1)), dma((tiles, 2, n - 1)),
            dma((len(hops),)), dma((len(hops),)), dma((tiles,)), dma((2,))],
        compiler_params=pltpu.CompilerParams(vmem_limit_bytes=VMEM_BYTES, collective_id=0, has_side_effects=True),
        name="weight_gradients",
    )(*stacks, late, small)


def widen_kernel(in_ref, proj_ref, down_ref, *, ups):
    step = pl.program_id(0)

    @pl.when(step < ups)
    def _():
        proj_ref[...] = in_ref[...].astype(F32)

    @pl.when(step >= ups)
    def _():
        down_ref[...] = in_ref[...].astype(F32)


def widen(data, ups, halves):
    width = data.shape[2]
    return pl.pallas_call(
        functools.partial(widen_kernel, ups=ups), grid=(ups + halves,),
        in_specs=[pl.BlockSpec((None, width, width), lambda b: (b, 0, 0))],
        out_specs=[pl.BlockSpec((width, width), lambda b: (0, jnp.minimum(b, ups - 1))),
                   pl.BlockSpec((width, width), lambda b: (jnp.maximum(b - ups, 0), 0))],
        out_shape=[shape_of((width, ups * width), F32), shape_of((halves * width, width), F32)],
        compiler_params=pltpu.CompilerParams(vmem_limit_bytes=VMEM_BYTES), name="widen",
    )(data)


def body(tokens, doc_ids, reset_flags, memory_init, w_proj, vectors, w_down, cotangent):
    data_count = lax.axis_size("dp")
    sections = lax.axis_size("section")
    width = tokens.shape[3]
    blocks = w_proj.shape[2] // width
    half = w_down.shape[0] // width

    results = run_layers(tokens[0], cotangent[0], w_proj[0], w_down, doc_ids, vectors[0], memory_init, reset_flags)
    block_rows, input_rows, late, small = results[:4]
    x_in, q, k_rows, v, o, n1, y1, n2, h, slope, p, df, db, dq, dk, dv, da = results[4:21]
    summed, late, total_vec, total_memory = weight_gradients(
        [x_in, o, y1, h, dq, dk, dv, db, da, df], late, small, data_count, sections, width, blocks, half,
        memory_init.shape[0])
    first = lax.axis_index("section") < 2
    input_rows = jnp.concatenate([jnp.where(first, input_rows[0], late)[None], input_rows[1:]], axis=0)
    total_proj, total_down = widen(summed, blocks, half)
    return (block_rows[None], input_rows[None], total_proj[None], total_vec[None], total_down, total_memory)


def solution(mesh):
    items = P(("section", "dp"), None, None, None)
    return jax.shard_map(
        body,
        mesh=mesh,
        in_specs=(items, P(), P(), P(), P("section", None, None), P("section", None, None),
                  P("section", None), items),
        out_specs=(items, items, P("section", None, None), P("section", None, None),
                   P("section", None), P(None, "section")),
        check_vma=False,
    )
```

```python
import functools

import jax
import jax.numpy as jnp
from jax import lax
from jax.experimental import pallas as pl
from jax.experimental.pallas import tpu as pltpu
from jax.sharding import PartitionSpec as P

HEADS = 12
DOCS = 4
NORM_EPSILON = 1e-06
NEGATIVE = -1e30
BF16 = jnp.bfloat16
F32 = jnp.float32
VMEM_BYTES = 60 * 2**20
LAYER_BYTES = 62 * 2**20
GROUP = 4
FF_BLOCK = 1536
TILE = 16
MESH = pl.DeviceIdType.MESH


def mm(left, right, ca=1, cb=0):
    return lax.dot_general(
        left, right, (((ca,), (cb,)), ((), ())), preferred_element_type=F32
    )


def shape_of(shape, dtype=BF16):
    return jax.ShapeDtypeStruct(shape, dtype)


def anywhere():
    return pl.BlockSpec(memory_space=pl.ANY)


def on_chip():
    return pl.BlockSpec(memory_space=pltpu.VMEM)


def head_rows(block, group, head):
    lane = lax.broadcasted_iota(jnp.int32, (1, block.shape[1]), 1) // head
    return jnp.concatenate([jnp.where(lane == h, block, jnp.zeros_like(block)) for h in range(group)], axis=0)


def head_fold(stacked, group, head):
    total, width = stacked.shape
    rows = total // group
    lane = lax.broadcasted_iota(jnp.int32, (1, width), 1) // head
    out = stacked[:rows]
    for h in range(1, group):
        out = jnp.where(lane == h, stacked[h * rows:(h + 1) * rows], out)
    return out


def normalise(summed):
    center = summed - jnp.mean(summed, axis=-1, keepdims=True)
    variance = jnp.mean(center * center, axis=-1, keepdims=True)
    inverse = lax.rsqrt(variance + NORM_EPSILON)
    return center * inverse, inverse


def across_lanes(narrow, width):
    return jnp.concatenate([narrow] * (width // narrow.shape[1]), axis=1)


def norm_back(g, n, inverse, gain):
    u = g * gain
    dz = inverse * (u - jnp.mean(u, axis=-1, keepdims=True) - n * jnp.mean(u * n, axis=-1, keepdims=True))
    return dz, jnp.sum(g * n, axis=0, keepdims=True), jnp.sum(g, axis=0, keepdims=True)


def layers_kernel(tokens_ref, cot_ref, proj_ref, down_ref, docs_ref, vec_ref, memory_ref, flags_ref,
                  out_ref, gtok_ref, late_ref, small_ref,
                  xs, qs, ks, vs, os_, n1s, y1s, n2s, hs, ss, ps, dfs, dbs, dqs, dks, dvs, das,
                  wa, w1, w2, vecs, docs, key_ref, query_ref, init_ref, fresh_ref, cot_other, mask_ref, land, dq_ref, q, k, v, o, n1, y1, n2, df, db, acc, y, hb, sb, pb, r1, r2,
                  mem_in, mem_grad,
                  share_local, share_send, share_recv, tok_local, tok_send, tok_recv, cot_send, cot_recv,
                  hop_send, hop_recv, back_send, back_recv, mem_send, mem_recv, mg_send, mg_recv,
                  out_sem, out_send, out_recv, gt_sem, gt_send, gt_recv,
                  gmem_ref, gvec_ref, load_sem, save_sem, keep_sem, h_sem, s_sem, p_sem):
    section = lax.axis_index("section")
    stage = section // 2
    core = lax.rem(section, 2)
    first = stage == 0
    second = stage == 1
    mate = {"section": section + 1 - 2 * core}
    across = {"section": section + 2 - 4 * stage}
    segments, tokens, width = tokens_ref.shape
    rows = land.shape[1]
    memory = memory_ref.shape[0]
    data = lax.axis_index("dp")
    data_count = lax.axis_size("dp")
    owners = (core * data_count + data, (core + 2) * data_count + data)
    hidden = proj_ref.shape[1]
    head = width // HEADS
    cols = GROUP * head
    groups = HEADS // GROUP
    blocks = hidden // FF_BLOCK
    halfd = down_ref.shape[0]
    micros = 2 * segments
    scale = head ** (-0.5)
    body_rows = pl.ds(0, tokens)
    last_rows = pl.ds(tokens, rows - tokens)

    def remote(source, target, send, recv, device):
        return pltpu.make_async_remote_copy(src_ref=source, dst_ref=target, send_sem=send, recv_sem=recv,
                                            device_id=device, device_id_type=MESH)

    local = pltpu.make_async_copy

    barrier = pltpu.get_barrier_semaphore()
    pl.semaphore_signal(barrier, inc=1, device_id=mate, device_id_type=MESH)
    pl.semaphore_signal(barrier, inc=1, device_id=across, device_id_type=MESH)
    pl.semaphore_wait(barrier, 2)

    down_rows = pl.ds(pl.multiple_of(core * halfd, 16), halfd)
    other_rows = pl.ds(pl.multiple_of((1 - core) * halfd, 16), halfd)
    down_away = remote(down_ref, w2.at[down_rows], share_send.at[1], share_recv.at[1], mate)
    vec_away = remote(vec_ref, vecs.at[core], share_send.at[2], share_recv.at[2], mate)
    proj_a = remote(proj_ref, wa, share_send.at[0], share_recv.at[0], mate)
    proj_b = remote(proj_ref, w1, share_send.at[0], share_recv.at[0], mate)
    proj_here_a = local(proj_ref, wa, share_local.at[0])
    proj_here_b = local(proj_ref, w1, share_local.at[0])
    down_here = local(down_ref, w2.at[down_rows], share_local.at[1])
    vec_here = local(vec_ref, vecs.at[core], share_local.at[2])

    @pl.when(core == 0)
    def _():
        proj_a.start()
        proj_here_a.start()

    @pl.when(core == 1)
    def _():
        proj_b.start()
        proj_here_b.start()

    vec_away.start()
    vec_here.start()
    down_away.start()
    down_here.start()

    doc_loads = [local(docs_ref.at[owners[i]], docs.at[i], load_sem.at[i]) for i in (0, 1)]
    for load in doc_loads:
        load.start()

    def tok_here(k_):
        return local(tokens_ref.at[k_], land.at[2 * k_, body_rows], tok_local.at[k_])

    def tok_copy(k_):
        return remote(tokens_ref.at[k_], land.at[2 * k_ + 1, body_rows], tok_send.at[k_], tok_recv.at[k_], across)

    def cot_copy(k_):
        return remote(cot_ref.at[k_], cot_other.at[k_], cot_send.at[k_], cot_recv.at[k_], across)

    @pl.when(second)
    def _():
        tok_copy(0).start()

    @pl.when(first)
    def _():
        for k_ in range(segments):
            tok_here(k_).start()
        cot_copy(segments - 1).start()

    for i in (0, 1):
        lane = lax.broadcasted_iota(jnp.int32, (1, flags_ref.shape[1]), 1)
        flag = jnp.where(lane == owners[i], flags_ref[segments - 1:segments, :].astype(F32), 0.0)
        fresh_ref[i] = jnp.broadcast_to(jnp.sum(flag, axis=1, keepdims=True), fresh_ref.shape[1:])
    init_ref[...] = jnp.concatenate([memory_ref[...], jnp.zeros((rows - tokens - memory, width), BF16)], axis=0)
    for load in doc_loads:
        load.wait()
    every = (1 << DOCS) - 1
    tail = lax.broadcasted_iota(jnp.int32, (rows - tokens, key_ref.shape[2]), 0)
    for m_ in range(micros):
        bits = jnp.left_shift(jnp.int32(1), docs[m_ % 2, m_ // 2:m_ // 2 + 1, :])
        row = jnp.concatenate([bits, jnp.full((1, rows - tokens), every, jnp.int32)], axis=1)
        query_ref[m_] = jnp.concatenate([row] * GROUP, axis=1)
        column = jnp.broadcast_to(bits.astype(F32), (8, tokens)).T[:, 0:1].astype(jnp.int32)
        key_ref[m_, body_rows, :] = jnp.broadcast_to(column, (tokens, key_ref.shape[2]))
        key_ref[m_, last_rows, :] = jnp.where(tail < memory, every, 0)

    def fresh(item):
        return jnp.broadcast_to(fresh_ref[item], (rows - tokens, width)) > 0.5

    vec_here.wait()
    vec_away.wait_recv()

    @pl.when(core == 0)
    def _():
        proj_here_a.wait()

    @pl.when(core == 1)
    def _():
        proj_a.wait_recv()
        remote(down_ref, w2.at[other_rows], share_send.at[1], share_recv.at[1], mate).wait_recv()

    @pl.when(second)
    def _():
        tok_copy(0).wait_send()
        for k_ in range(1, segments):
            tok_copy(k_).start()

    parts = (pl.ds(0, tokens // 2), pl.ds(tokens // 2, rows - tokens // 2))

    def hop_copy(m, i):
        return remote(y.at[lax.rem(m, 2), parts[i]], land.at[m, parts[i]], hop_send.at[m, i], hop_recv.at[m, i],
                      across)

    def mem_copy(m):
        return remote(y.at[lax.rem(m, 2), last_rows], mem_in.at[m], mem_send.at[m], mem_recv.at[m], across)

    def out_here(m, seg):
        return local(y.at[lax.rem(m, 2), body_rows], out_ref.at[seg], out_sem.at[m])

    def out_away(m, seg):
        return remote(y.at[lax.rem(m, 2), body_rows], out_ref.at[seg], out_send.at[seg], out_recv.at[seg], across)

    kept = [(q, qs), (k, ks), (v, vs), (o, os_), (n1, n1s), (y1, y1s), (n2, n2s)]

    def keep(m):
        return local(land.at[m], xs.at[m], keep_sem.at[m])

    def grad_load(t, seg):
        source = cot_ref if t % 2 else cot_other
        return local(source.at[seg], land.at[t, body_rows], load_sem.at[6 + t])

    def saves(m):
        return [local(here, there.at[m], save_sem.at[i]) for i, (here, there) in enumerate(kept)]

    def band(g):
        return pl.ds(g * cols, cols)

    def feed_copy(buffer, stack, sems, m, i, j):
        columns = pl.ds(pl.multiple_of(j * FF_BLOCK, FF_BLOCK), FF_BLOCK)
        return local(buffer.at[j, parts[i]], stack.at[m, parts[i], columns], sems.at[i, j])

    def h_save(m, i, j):
        return feed_copy(hb, hs, h_sem, m, i, j)

    def s_save(m, i, j):
        return feed_copy(sb, ss, s_sem, m, i, j)

    def p_save(m, g):
        return local(pb.at[g % 2], ps.at[m, g], p_sem.at[g % 2])

    def forward(m, carry):
        item = lax.rem(m, 2)
        seg = m // 2

        @pl.when(m > 0)
        def _():
            for save in saves(m - 1):
                save.wait()

        keys = jnp.concatenate([key_ref[m]] * -(-mask_ref.shape[1] // key_ref.shape[2]), axis=1)
        mask_ref[...] = jnp.where((keys[:, :mask_ref.shape[1]] & query_ref[m]) != 0, 0.0, NEGATIVE)
        x = land.at[m]

        @pl.when(first)
        def _():
            @pl.when(item == 0)
            def _():
                tok_here(seg).wait()

            @pl.when(item == 1)
            def _():
                tok_copy(seg).wait_recv()

            @pl.when(seg == 0)
            def _():
                x[last_rows, :] = init_ref[...]

            @pl.when(seg > 0)
            def _():
                mem_copy(m - 2).wait_recv()
                x[last_rows, :] = jnp.where(fresh(item), init_ref[...], mem_in[m - 2])

        @pl.when(second)
        def _():
            for i in (0, 1):
                hop_copy(m, i).wait_recv()

            @pl.when(m == micros - 1)
            def _():
                keep(0).wait()
                keep(1).wait()
                cot_copy(segments - 1).wait_recv()
                for t in (0, 1):
                    grad_load(t, segments - 1).start()

        keep(m).start()
        out = saves(m)

        def project(g):
            here = band(g)
            xv = x[...]
            q[:, here] = mm(xv, wa[:, here]).astype(BF16)
            k[:, here] = mm(xv, wa[:, pl.ds(width + g * cols, cols)]).astype(BF16)
            v[:, here] = mm(xv, wa[:, pl.ds(2 * width + g * cols, cols)]).astype(BF16)
            return mm(k[:, here], head_rows(q[:, here] * scale, GROUP, head), 1, 1) + mask_ref[...]

        score = project(0)
        for g in range(groups):
            following = project(g + 1) if g + 1 < groups else None
            if g >= 2:
                p_save(m, g - 2).wait()
            else:
                @pl.when(m > 0)
                def _():
                    p_save(m - 1, groups - 1 - (groups - 1 - g) % 2).wait()
            e = jnp.exp(score - jnp.max(score, axis=0, keepdims=True))
            p = (e * (1.0 / jnp.sum(e, axis=0, keepdims=True))).astype(BF16)
            pb[g % 2] = p
            p_save(m, g).start()
            o[:, band(g)] = head_fold(mm(p, v[:, band(g)], 0, 0), GROUP, head).astype(BF16)
            score = following
        for i in (0, 1, 2, 3):
            out[i].start()
        normed, inverse = normalise(x[...].astype(F32) + mm(o[...], wa[:, pl.ds(3 * width, width)]))
        n1[...] = normed.astype(BF16)
        r1[m] = jnp.broadcast_to(inverse, r1.shape[1:])
        y1v = (normed * vecs[0, 0:1, :] + vecs[0, 1:2, :]).astype(BF16)
        y1[...] = y1v
        acc[...] = y1v.astype(F32)
        out[4].start()
        out[5].start()

        @pl.when(m == 0)
        def _():
            @pl.when(core == 0)
            def _():
                proj_b.wait_recv()
                remote(down_ref, w2.at[other_rows], share_send.at[1], share_recv.at[1], mate).wait_recv()

            @pl.when(core == 1)
            def _():
                proj_here_b.wait()

            down_here.wait()

        def feed(i, j, carry2):
            here = parts[i]

            @pl.when(m > 0)
            def _():
                h_save(m - 1, i, j).wait()
                s_save(m - 1, i, j).wait()

            half = FF_BLOCK // 2
            yv = y1[here, :]
            pre = [mm(yv, w1[:, pl.ds(pl.multiple_of(j * FF_BLOCK + c * half, half), half)]) for c in range(2)]
            for c in range(2):
                a = pre[c]
                gate = 0.5 * (1.0 + lax.erf(a * 0.7071067811865476))
                hb[j, here, c * half:(c + 1) * half] = (a * gate).astype(BF16)
                sb[j, here, c * half:(c + 1) * half] = (
                    gate + a * jnp.exp(-0.5 * a * a) * 0.3989422804014327).astype(BF16)
            h_save(m, i, j).start()
            s_save(m, i, j).start()
            acc[here, :] += mm(hb[j, here, :], w2[pl.ds(pl.multiple_of(j * FF_BLOCK, FF_BLOCK), FF_BLOCK), :])
            return carry2

        @pl.when(m >= 2)
        def _():
            @pl.when(first)
            def _():
                for i in (0, 1):
                    hop_copy(m - 2, i).wait_send()

            @pl.when(second)
            def _():
                mem_copy(m - 2).wait_send()

                @pl.when(item == 0)
                def _():
                    out_away(m - 2, seg - 1).wait_send()

                @pl.when(item == 1)
                def _():
                    out_here(m - 2, seg - 1).wait()

        @pl.when(first & (m == micros - 1))
        def _():
            for m_ in range(micros):
                keep(m_).wait()

        for i in (0, 1):
            here = parts[i]
            lax.fori_loop(0, blocks, functools.partial(feed, i), 0)
            normed, inverse = normalise(acc[here, :])
            n2[here, :] = normed.astype(BF16)
            r2[m, here, :] = jnp.broadcast_to(inverse, (here.size, r2.shape[2]))
            y[item, here, :] = (normed * vecs[1, 0:1, :] + vecs[1, 1:2, :]).astype(BF16)

            @pl.when(first)
            def _():
                hop_copy(m, i).start()

        out[6].start()

        @pl.when(second)
        def _():
            @pl.when(seg + 1 < segments)
            def _():
                mem_copy(m).start()

            @pl.when(item == 0)
            def _():
                out_away(m, seg).start()

            @pl.when(item == 1)
            def _():
                out_here(m, seg).start()

        return carry

    lax.fori_loop(0, micros, forward, 0)
    for save in saves(micros - 1):
        save.wait()
    for g in (groups - 2, groups - 1):
        p_save(micros - 1, g).wait()
    for i in (0, 1):
        for j in range(blocks):
            h_save(micros - 1, i, j).wait()
            s_save(micros - 1, i, j).wait()

    @pl.when(first)
    def _():
        for m in range(micros - 2, micros):
            for i in (0, 1):
                hop_copy(m, i).wait_send()
        for k_ in reversed(range(segments - 1)):
            cot_copy(k_).start()
        for k_ in range(segments):
            out_away(0, k_).wait_recv()

    @pl.when(second)
    def _():
        out_away(micros - 2, segments - 1).wait_send()
        out_here(micros - 1, segments - 1).wait()
        for m in range(2, micros):
            keep(m).wait()

    gmem_ref[...] = jnp.zeros(gmem_ref.shape, F32)
    gvec_ref[...] = jnp.zeros(gvec_ref.shape, F32)

    def back_copy(t, i):
        return remote(y.at[lax.rem(t, 2), parts[i]], land.at[t, parts[i]], back_send.at[t, i], back_recv.at[t, i],
                      across)

    def mg_copy(t):
        return remote(y.at[lax.rem(t, 2), last_rows], mem_grad.at[t], mg_send.at[t], mg_recv.at[t], across)

    def gt_here(t, seg):
        return local(y.at[lax.rem(t, 2), body_rows], gtok_ref.at[seg], gt_sem.at[t])

    def gt_away(t, seg):
        return remote(y.at[lax.rem(t, 2), body_rows], gtok_ref.at[seg], gt_send.at[seg], gt_recv.at[seg], across)

    def gt_late():
        return local(y.at[1, body_rows], late_ref, gt_sem.at[micros - 1])

    def s_load(m, j):
        columns = pl.ds(j * FF_BLOCK, FF_BLOCK)
        return local(ss.at[m, :, columns], sb.at[j], s_sem.at[0, j])

    def d_save(m, i, j):
        return feed_copy(hb, das, h_sem, m, i, j)

    def p_load(m, g):
        return local(ps.at[m, g], pb.at[g % 2], p_sem.at[g % 2])

    def n2_load(m):
        return local(n2s.at[m], n2, load_sem.at[1])

    n2_load(2 * segments - 2).start()
    for j in range(blocks):
        s_load(2 * segments - 2, j).start()

    def back_saves(m):
        pairs = [(df, dfs), (db, dbs), (dq_ref, dqs), (o, dks), (y1, dvs)]
        return [local(here, there.at[m], save_sem.at[i]) for i, (here, there) in enumerate(pairs)]

    def backward(t, carry):
        item = lax.rem(t, 2)
        seg = segments - 1 - t // 2
        m = 2 * seg + item
        before = 2 * (segments - 1 - (t - 1) // 2) + lax.rem(t - 1 + 2, 2)

        @pl.when(t > 0)
        def _():
            for save in back_saves(before):
                save.wait()

        loads = [local(source.at[m], here, load_sem.at[2 + i])
                 for i, (source, here) in enumerate([(qs, q), (ks, k), (vs, v), (n1s, n1)])]
        grads_in = land.at[t]

        @pl.when(second)
        def _():
            @pl.when(t == 2)
            def _():
                cot_copy(0).wait_recv()
                for t_ in range(2, micros):
                    grad_load(t_, 0).start()

            for t_ in range(micros):
                @pl.when(t == t_)
                def _():
                    grad_load(t_, 0).wait()

            @pl.when(seg + 1 == segments)
            def _():
                grads_in[last_rows, :] = jnp.zeros((rows - tokens, width), BF16)

        n2_load(m).wait()
        out = back_saves(m)
        for load in loads:
            load.start()
        p_load(m, 0).start()
        p_load(m, 1).start()
        following = 2 * (segments - 1 - (t + 1) // 2) + lax.rem(t + 1, 2)

        def feed(i, j, carry2):
            here = parts[i]

            @pl.when(t > 0)
            def _():
                d_save(before, i, j).wait()

            half = FF_BLOCK // 2
            dfv = df[here, :]
            dh = [mm(dfv, w2[pl.ds(pl.multiple_of(j * FF_BLOCK + c * half, half), half), :], 1, 1) for c in range(2)]
            for c in range(2):
                cut = slice(c * half, (c + 1) * half)
                hb[j, here, cut] = (dh[c] * sb[j, here, cut].astype(F32)).astype(BF16)
            d_save(m, i, j).start()
            acc[here, :] += mm(hb[j, here, :], w1[:, pl.ds(pl.multiple_of(j * FF_BLOCK, FF_BLOCK), FF_BLOCK)], 1, 1)
            return carry2

        for i in (0, 1):
            here = parts[i]

            @pl.when(first)
            def _():
                back_copy(t, i).wait_recv()

            if i == 1:
                @pl.when(second & (seg + 1 < segments))
                def _():
                    mg_copy(t - 2).wait_recv()
                    got = mem_grad[t - 2]
                    grads_in[last_rows, :] = jnp.where(fresh(item), jnp.zeros_like(got), got)

            dz, gain_grad, bias_grad = norm_back(grads_in[here, :].astype(F32), n2[here, :].astype(F32),
                                                 across_lanes(r2[m, here, :], width), vecs[1, 0:1, :])
            gvec_ref[2:3, :] += gain_grad
            gvec_ref[3:4, :] += bias_grad
            df[here, :] = dz.astype(BF16)
            acc[here, :] = dz
            if i == 0:
                for j in range(blocks):
                    s_load(m, j).wait()
            lax.fori_loop(0, blocks, functools.partial(feed, i), 0)

        out[0].start()

        @pl.when(t + 1 < micros)
        def _():
            n2_load(following).start()
            for j in range(blocks):
                s_load(following, j).start()

        for load in loads:
            load.wait()
        dz, gain_grad, bias_grad = norm_back(acc[...].astype(BF16).astype(F32), n1[...].astype(F32), across_lanes(r1[m], width),
                                             vecs[0, 0:1, :])
        gvec_ref[0:1, :] += gain_grad
        gvec_ref[1:2, :] += bias_grad
        db[...] = dz.astype(BF16)
        acc[...] = dz
        out[1].start()

        def begin(g):
            gv = mm(db[...], wa[band(g), pl.ds(3 * width, width)], 1, 1).astype(BF16)
            grads = head_rows(gv, GROUP, head)
            return grads, mm(v[:, band(g)], grads, 1, 1)

        ahead = begin(0)
        for g in range(groups):
            here = band(g)
            grads, dp = ahead
            ahead = begin(g + 1) if g + 1 < groups else None
            p_load(m, g).wait()
            p = pb[g % 2]
            dv = mm(p, grads).astype(BF16)
            weight = p.astype(F32)
            ds = (weight * (dp - jnp.sum(weight * dp, axis=0, keepdims=True))).astype(BF16)
            if g + 2 < groups:
                p_load(m, g + 2).start()
            dk = mm(ds, head_rows(q[:, here] * scale, GROUP, head)).astype(BF16)
            dq = (head_fold(mm(ds, k[:, here], 0, 0), GROUP, head) * scale).astype(BF16)
            dq_ref[:, here] = dq
            o[:, here] = dk
            y1[:, here] = dv
        for i in (2, 3, 4):
            out[i].start()

        @pl.when(t >= 2)
        def _():
            @pl.when(second)
            def _():
                for i in (0, 1):
                    back_copy(t - 2, i).wait_send()

            @pl.when(first)
            def _():
                mg_copy(t - 2).wait_send()

                @pl.when(item == 1)
                def _():
                    gt_away(t - 2, seg + 1).wait_send()

                @pl.when(item == 0)
                def _():
                    gt_here(t - 2, seg + 1).wait()

        for i in (0, 1):
            here = parts[i]
            dx = (acc[here, :] + mm(dq_ref[here, :], wa[:, pl.ds(0, width)], 1, 1)
                  + mm(o[here, :], wa[:, pl.ds(width, width)], 1, 1)
                  + mm(y1[here, :], wa[:, pl.ds(2 * width, width)], 1, 1)).astype(BF16)
            y[item, here, :] = dx

            @pl.when(second)
            def _():
                back_copy(t, i).start()

        @pl.when(first)
        def _():
            tail_grad = y[item, last_rows, :].astype(F32)

            @pl.when(seg > 0)
            def _():
                mg_copy(t).start()
                gmem_ref[...] += jnp.where(fresh(item), tail_grad, 0.0)

            @pl.when(seg == 0)
            def _():
                gmem_ref[...] += tail_grad

            @pl.when(item == 0)
            def _():
                gt_here(t, seg).start()

            @pl.when((item == 1) & (seg > 0))
            def _():
                gt_away(t, seg).start()

            @pl.when((item == 1) & (seg == 0))
            def _():
                gt_late().start()

        return carry

    lax.fori_loop(0, micros, backward, 0)
    for save in back_saves(1):
        save.wait()
    for i in (0, 1):
        for j in range(blocks):
            d_save(1, i, j).wait()

    @pl.when(second)
    def _():
        for t in range(micros - 2, micros):
            for i in (0, 1):
                back_copy(t, i).wait_send()
        for k_ in range(1, segments):
            tok_copy(k_).wait_send()
        for k_ in range(1, segments):
            gt_away(1, k_).wait_recv()

    @pl.when(first)
    def _():
        gt_here(micros - 2, 0).wait()
        gt_late().wait()
        for k_ in range(segments):
            cot_copy(k_).wait_send()

    own = gvec_ref[0:4, :]
    none = jnp.zeros_like(own)
    for mine_, parts in ((first, [own, none]), (second, [none, own])):
        @pl.when(mine_)
        def _():
            small_ref[...] = jnp.concatenate(parts + [gmem_ref[...]], axis=0)

    proj_a.wait_send()
    down_away.wait_send()
    vec_away.wait_send()


def run_layers(tokens, cotangent, proj, down, docs, vec, memory, flags):
    segments, seg_tokens, width = tokens.shape
    rows = seg_tokens + TILE
    hidden = proj.shape[1]
    micros = 2 * segments
    groups = HEADS // GROUP
    span = GROUP * rows
    stack = shape_of((micros, rows, width))
    wide = shape_of((micros, rows, hidden))
    low = pltpu.VMEM((rows, width), BF16)
    dma = pltpu.SemaphoreType.DMA
    pair = pltpu.VMEM((hidden // FF_BLOCK, rows, FF_BLOCK), BF16)
    inverse = pltpu.VMEM((micros, rows, 128), F32)
    tails = pltpu.VMEM((2, TILE, width), BF16)
    return pl.pallas_call(
        layers_kernel,
        in_specs=[anywhere()] * 5 + [on_chip()] * 3,
        out_specs=[anywhere()] * 3 + [on_chip()] + [anywhere()] * 17,
        out_shape=[shape_of(tokens.shape), shape_of(tokens.shape), shape_of(tokens.shape[1:]),
                   shape_of((8 + TILE, width), F32)]
        + [stack] * 8 + [wide] * 2 + [shape_of((micros, groups, rows, span))] + [stack] * 5 + [wide],
        scratch_shapes=[
            pltpu.VMEM((width, hidden), BF16), pltpu.VMEM((width, hidden), BF16), pltpu.VMEM((hidden, width), BF16),
            pltpu.VMEM((2, 2, width), F32), pltpu.VMEM((2, segments, seg_tokens), jnp.int32),
            pltpu.VMEM((micros, rows, 128), jnp.int32), pltpu.VMEM((micros, 1, span), jnp.int32),
            pltpu.VMEM((TILE, width), BF16), pltpu.VMEM((2, 1, width), F32),
            pltpu.VMEM(tokens.shape, BF16), pltpu.VMEM((rows, span), F32), pltpu.VMEM((micros, rows, width), BF16)] + [low] * 10 + [
            pltpu.VMEM((rows, width), F32), pltpu.VMEM((2, rows, width), BF16), pair, pair,
            pltpu.VMEM((2, rows, span), BF16), inverse, inverse, tails, tails,
            dma((3,)), dma((3,)), dma((3,)), dma((segments,)), dma((segments,)), dma((segments,)), dma((segments,)),
            dma((segments,)),
            dma((micros, 2)), dma((micros, 2)), dma((micros, 2)), dma((micros, 2)),
            dma((2,)), dma((2,)), dma((2,)), dma((2,)),
            dma((micros,)), dma((segments,)), dma((segments,)), dma((micros,)), dma((segments,)), dma((segments,)),
            pltpu.VMEM((TILE, width), F32), pltpu.VMEM((8, width), F32),
            dma((6 + micros,)), dma((7,)), dma((micros,)),
            dma((2, hidden // FF_BLOCK)), dma((2, hidden // FF_BLOCK)), dma((2,))],
        compiler_params=pltpu.CompilerParams(vmem_limit_bytes=LAYER_BYTES, collective_id=1, has_side_effects=True),
        name="layers",
    )(tokens, cotangent, proj, down, docs, vec, memory, flags)


def flipped(index, bit):
    return index + bit - 2 * bit * lax.rem(index // bit, 2)


def ring_piece(n, width):
    piece = -(-width // (2 * n))
    return piece + -piece % 16


def grads_kernel(xs, os_, y1s, hs, dqs, dks, dvs, dbs, das, dfs, late_ref, small_ref, out_ref, late_out, vec_out, memory_out,
                 lbuf, rbuf, mine, got, away, final, slots, held, arrived,
                 left_sem, right_sem, swap_send, swap_recv, sum_send, sum_recv, full_send, full_recv,
                 small_send, small_recv, store_sem, late_sem, *, n, piece, hops, ups, halves):
    section = lax.axis_index("section")
    data = lax.axis_index("dp")
    core = lax.rem(section, 2)
    mate = {"section": section + 1 - 2 * core}
    width = final.shape[2]
    tiles = ups + halves
    half = n // 2
    micros, rows = lbuf.shape[1:3]

    def place(p):
        p = lax.rem(p + 2 * n, n)
        return jnp.where(p < half, 2 * p, 2 * (n - 1 - p) + 1)

    me = jnp.where(lax.rem(data, 2) == 0, data // 2, n - 1 - data // 2)
    peers = ({"dp": place(me + 1)}, {"dp": place(me - 1)})
    signs = (1, -1)

    def remote(source, target, send, recv, device):
        return pltpu.make_async_remote_copy(src_ref=source, dst_ref=target, send_sem=send, recv_sem=recv,
                                            device_id=device, device_id_type=MESH)

    def part(ref, column):
        return ref.at[:, :, pl.ds(column * width, width)]

    attn = [(xs, dqs), (xs, dks), (xs, dvs), (os_, dbs)] + [(part(hs, i), dfs) for i in range(halves)]
    feed = [(y1s, part(das, i)) for i in range(ups)] + [(part(hs, halves + i), dfs) for i in range(halves)]

    def load(t, which, j):
        b = lax.rem(t, 2)
        left, right = (attn, feed)[which][j]
        return (pltpu.make_async_copy(left, lbuf.at[b], left_sem.at[b]),
                pltpu.make_async_copy(right, rbuf.at[b], right_sem.at[b]))

    def start_load(t):
        turn = jnp.where(lax.rem(t, 2) == 1, core, 1 - core)
        for which in (0, 1):
            for j in range(tiles):
                @pl.when((turn == which) & (t // 2 == j))
                def _():
                    for copy in load(t, which, j):
                        copy.start()

    start_load(jnp.int32(0))
    barrier = pltpu.get_barrier_semaphore()
    friends = [{axis: flipped(section if axis == "section" else data, bit)} for axis, bit in hops]
    greeted = [mate, *peers, *friends]
    for device in greeted:
        pl.semaphore_signal(barrier, inc=1, device_id=device, device_id_type=MESH)
    pl.semaphore_wait(barrier, len(greeted))

    across = {"section": flipped(section, 2)}
    late = remote(late_ref, late_out, late_sem.at[0], late_sem.at[1], across)

    @pl.when(section < 2)
    def _():
        late.start()

    held[0] = small_ref[...]

    def small_copy(i):
        return remote(held.at[i], arrived.at[i], small_send.at[i], small_recv.at[i], friends[i])

    small_copy(0).start()

    def finish_small(i):
        small_copy(i).wait_recv()
        total = held[i] + arrived[i]
        if i + 1 < len(friends):
            held[i + 1] = total
            small_copy(i + 1).start()
        else:
            share, lines = memory_out.shape[1], memory_out.shape[0]
            for which in range(width // share):
                @pl.when(section == which)
                def _():
                    vec_out[...] = total[2 * which:2 * which + 2, :]
                    memory_out[...] = total[8:8 + lines, which * share:(which + 1) * share]

    def swap(j):
        return remote(away.at[lax.rem(j, 2)], got.at[j, pl.ds(0, width)], swap_send.at[j], swap_recv.at[j], mate)

    def piece_rows(index, d):
        return pl.ds(pl.multiple_of((lax.rem(index + 2 * n, n) * 2 + d) * piece, 16), piece)

    def sum_copy(i, d, s):
        where = mine.at[i, piece_rows(me - signs[d] * s, d)]
        return remote(where, slots.at[i, d, s], sum_send.at[i, d, s], sum_recv.at[i, d, s], peers[d])

    def full_copy(i, d, s):
        where = final.at[i, piece_rows(me + signs[d] * (1 - s), d)]
        return remote(where, where, full_send.at[i, d, s], full_recv.at[i, d, s], peers[d])

    def store(i):
        return pltpu.make_async_copy(final.at[i], out_ref.at[i], store_sem.at[i])

    def serve(i, s):
        @pl.when(s == 0)
        def _():
            swap(i).wait_recv()

        @pl.when((s >= 0) & (s < n))
        def _():
            for d in (0, 1):
                here = piece_rows(me - signs[d] * s, d)
                value = mine[i, here, :].astype(F32) + got[i, here, :].astype(F32)

                @pl.when(s == 0)
                def _():
                    mine[i, here, :] = value.astype(BF16)
                    sum_copy(i, d, s).start()

                @pl.when(s > 0)
                def _():
                    sum_copy(i, d, s - 1).wait_recv()
                    total = (value + slots[i, d, s - 1].astype(F32)).astype(BF16)

                    @pl.when(s < n - 1)
                    def _():
                        mine[i, here, :] = total
                        sum_copy(i, d, s).start()

                    @pl.when(s == n - 1)
                    def _():
                        final[i, here, :] = total
                        full_copy(i, d, 0).start()

        @pl.when((s >= n) & (s < 2 * n - 1))
        def _():
            f = s - n + 1
            for d in (0, 1):
                full_copy(i, d, f - 1).wait_recv()

                @pl.when(f < n - 1)
                def _():
                    full_copy(i, d, f).start()

            @pl.when(f == n - 1)
            def _():
                store(i).start()

    def finish_sends(i):
        def sends(s, carry2):
            for d in (0, 1):
                sum_copy(i, d, s).wait_send()
                full_copy(i, d, s).wait_send()
            return carry2

        lax.fori_loop(0, n - 1, sends, 0)

    def advance(t, carry):
        @pl.when(t + 1 < 2 * tiles)
        def _():
            start_load(t + 1)

        @pl.when(t < 2 * tiles)
        def _():
            b, j = lax.rem(t, 2), t // 2
            for copy in load(t, 0, 0):
                copy.wait()
            tile = mm(lbuf[b].reshape(micros * rows, width), rbuf[b].reshape(micros * rows, width), 0, 0).astype(BF16)

            @pl.when(b == 0)
            def _():
                @pl.when(j >= 2)
                def _():
                    swap(j - 2).wait_send()

                away[lax.rem(j, 2)] = tile
                swap(j).start()

            @pl.when(b == 1)
            def _():
                mine[j, 0:width, :] = tile

        for k in range(len(friends)):
            @pl.when(t == 2 * tiles + k)
            def _():
                finish_small(k)

        def one(i, carry2):
            serve(i, t - 2 * i - 1)
            return carry2

        lax.fori_loop(0, tiles, one, 0)
        return carry

    lax.fori_loop(0, 2 * tiles + 2 * n - 2, advance, 0)

    def finish(i, carry):
        finish_sends(i)
        store(i).wait()
        return carry

    lax.fori_loop(0, tiles, finish, 0)
    for j in range(tiles - 2, tiles):
        swap(j).wait_send()
    for i in range(len(friends)):
        small_copy(i).wait_send()

    @pl.when(section < 2)
    def _():
        late.wait_send()

    @pl.when(section >= 2)
    def _():
        late.wait_recv()


def weight_gradients(stacks, late, small, n, sections, width, ups, halves, memory):
    piece = ring_piece(n, width)
    total = 2 * n * piece
    micros, rows = stacks[0].shape[:2]
    tiles = ups + halves
    hops = [("dp", 1 << i) for i in range(n.bit_length() - 1)]
    hops += [("section", 1 << i) for i in range(sections.bit_length() - 1)]
    dma = pltpu.SemaphoreType.DMA
    kept = pltpu.VMEM((tiles, total, width), BF16)
    operand = pltpu.VMEM((2, micros, rows, width), BF16)
    sums = pltpu.VMEM((len(hops),) + small.shape, F32)
    return pl.pallas_call(
        functools.partial(grads_kernel, n=n, piece=piece, hops=hops, ups=ups, halves=halves),
        in_specs=[anywhere()] * (len(stacks) + 1) + [on_chip()],
        out_specs=[anywhere(), anywhere(), on_chip(), on_chip()],
        out_shape=[shape_of((tiles, total, width)), shape_of(late.shape), shape_of((2, width), F32),
                   shape_of((memory, width // sections), F32)],
        scratch_shapes=[
            operand, operand, kept, kept, pltpu.VMEM((2, width, width), BF16), kept,
            pltpu.VMEM((tiles, 2, n - 1, piece, width), BF16), sums, sums,
            dma((2,)), dma((2,)), dma((tiles,)), dma((tiles,)),
            dma((tiles, 2, n - 1)), dma((tiles, 2, n - 1)), dma((tiles, 2, n - 1)), dma((tiles, 2, n - 1)),
            dma((len(hops),)), dma((len(hops),)), dma((tiles,)), dma((2,))],
        compiler_params=pltpu.CompilerParams(vmem_limit_bytes=VMEM_BYTES, collective_id=0, has_side_effects=True),
        name="weight_gradients",
    )(*stacks, late, small)


def widen_kernel(in_ref, proj_ref, down_ref, *, ups):
    step = pl.program_id(0)

    @pl.when(step < ups)
    def _():
        proj_ref[...] = in_ref[...].astype(F32)

    @pl.when(step >= ups)
    def _():
        down_ref[...] = in_ref[...].astype(F32)


def widen(data, ups, halves):
    width = data.shape[2]
    return pl.pallas_call(
        functools.partial(widen_kernel, ups=ups), grid=(ups + halves,),
        in_specs=[pl.BlockSpec((None, width, width), lambda b: (b, 0, 0))],
        out_specs=[pl.BlockSpec((width, width), lambda b: (0, jnp.minimum(b, ups - 1))),
                   pl.BlockSpec((width, width), lambda b: (jnp.maximum(b - ups, 0), 0))],
        out_shape=[shape_of((width, ups * width), F32), shape_of((halves * width, width), F32)],
        compiler_params=pltpu.CompilerParams(vmem_limit_bytes=VMEM_BYTES), name="widen",
    )(data)


def body(tokens, doc_ids, reset_flags, memory_init, w_proj, vectors, w_down, cotangent):
    data_count = lax.axis_size("dp")
    sections = lax.axis_size("section")
    width = tokens.shape[3]
    blocks = w_proj.shape[2] // width
    half = w_down.shape[0] // width

    results = run_layers(tokens[0], cotangent[0], w_proj[0], w_down, doc_ids, vectors[0], memory_init, reset_flags.T)
    block_rows, input_rows, late, small = results[:4]
    x_in, q, k_rows, v, o, n1, y1, n2, h, slope, p, df, db, dq, dk, dv, da = results[4:21]
    summed, late, total_vec, total_memory = weight_gradients(
        [x_in, o, y1, h, dq, dk, dv, db, da, df], late, small, data_count, sections, width, blocks, half,
        memory_init.shape[0])
    first = lax.axis_index("section") < 2
    input_rows = jnp.concatenate([jnp.where(first, input_rows[0], late)[None], input_rows[1:]], axis=0)
    total_proj, total_down = widen(summed, blocks, half)
    return (block_rows[None], input_rows[None], total_proj[None], total_vec[None], total_down, total_memory)


def solution(mesh):
    items = P(("section", "dp"), None, None, None)
    return jax.shard_map(
        body,
        mesh=mesh,
        in_specs=(items, P(), P(), P(), P("section", None, None), P("section", None, None),
                  P("section", None), items),
        out_specs=(items, items, P("section", None, None), P("section", None, None),
                   P("section", None), P(None, "section")),
        check_vma=False,
    )
```
